512 devices in a mesh: ctx: 16 (over y, x_lo), exp: 32 (over z, x_hi, core).
Axes of the slice: x: 4 (x_hi: 2, x_lo: 2; x = x_hi * 2 + x_lo), y: 8, z: 8, core: 2. Of those that a mesh axis runs over, the one named last changes fastest.
Arguments:
- queries: bfloat16 [4096, 64, 576], P('ctx', 'exp'), may hold values from -40 to 40
- latent: bfloat16 [4096, 576], P('ctx'), may hold values from -6.5 to 6.5
- segment_ids: int32 [4096], P('ctx'), may hold values from 0 to 7, never falling along the last dimension, each value on 1 to 2048 neighbouring positions
- value_up: bfloat16 [64, 512, 128], P('exp'), may hold values from -0.25 to 0.25
- out_proj: bfloat16 [8192, 2560], P('exp'), may hold values from -0.125 to 0.125
- residual: bfloat16 [4096, 2560], P(('ctx', 'exp')), may hold values from -4 to 4
- norm_gain: float32 [2560], replicated, may hold values from 0.1 to 1.9
- route_ids: int32 [256, 16, 6], P('exp'), may hold values from 0 to 95, all different within a row; in each aligned block of 128 rows (0 to 127, 128 to 255, ..., all dimensions but the last counted through in order) at most 10 rows name the same one
- route_gates: float32 [256, 16, 6], P('exp'), may hold values from 0.1 to 1
- expert_gate: bfloat16 [96, 2560, 768], P('exp', 'ctx'), may hold values from -0.125 to 0.125
- expert_up: bfloat16 [96, 2560, 768], P('exp', 'ctx'), may hold values from -0.125 to 0.125
- expert_down: bfloat16 [96, 768, 2560], P('exp', None, 'ctx'), may hold values from -0.21875 to 0.21875
Outputs:
- layer_out: bfloat16 [256, 16, 2560], P('exp', None, 'ctx')
The draws below stay inside these ranges and needn't reach their ends.
Inputs may be any that keep to these rules, and one draw needn't show every extreme that they name: `segment_ids`: never falling along the sequence; no document is longer than half of 4096 tokens, and one has exactly that length. `route_ids`: in the rows of one device (aligned blocks of 128 rows over the first two dimensions together, in order) no expert is named more than 10 times, a bound that some block reaches.
All inputs are finite; a program needn't handle non-finite values.
Results may differ from the reference program's by a relative error of at most 0.04.
Values may be sent and summed in bfloat16 or wider, within the bound.
No kernel may reach another device: no remote copies, remote signals or barrier semaphores. Data moves between devices by JAX's collectives and lax.ppermute only.
A program may use at most 64 MiB of HBM per device.

```python
import math
import jax
import jax.numpy as jnp
import numpy as np
from jax import lax

D = 2560
HEADS = 64
LATENT = 512
ROPE = 64
VDIM = 128
QKDIM = 192
FF = 768
EXPERTS = 96
TOPK = 6
CAP = 10
BLK = 256
BLOCKS = 16
LENGTH = 4096
TOK_DEV = 8
N_CTX = 16
N_EXP = 32


def anchor_draw(key):
    base_rows = jnp.clip(jax.random.normal(jax.random.fold_in(key, 13), (LENGTH, LATENT + ROPE), jnp.float32), -5.0, 5.0)
    return base_rows


def draw_latent(key, part):
    base_rows = anchor_draw(key)
    chosen_rows = base_rows
    return chosen_rows.astype(jnp.bfloat16)


def draw_queries(key, part):
    key = jax.random.fold_in(key, 2)
    values_drawn = jnp.clip(jax.random.normal(key, (LENGTH, HEADS, LATENT + ROPE), jnp.float32), -5.0, 5.0)
    return values_drawn.astype(jnp.bfloat16)


def steps_of(rng, extent, cuts, smallest, high):
    gain, own = 1.0, jax.random.fold_in(rng, 6)
    for dim, blocks in cuts:
        steps = jnp.exp(jax.random.uniform(jax.random.fold_in(own, dim), (blocks,), jnp.float32, smallest / len(cuts), high / len(cuts)))
        gain = gain * jnp.repeat(steps, extent[dim] // blocks).reshape([-1 if axis == dim else 1 for axis in range(len(extent))])
    return gain


def profile(count, total, limit, skew):
    weights = [(1 << 20) // math.isqrt(grade ** skew) + 1 for grade in range(2, count + 1)]
    rest, given = total - limit - (count - 1), [1] * (count - 1)
    while rest > 0:
        free = [i for i in range(count - 1) if given[i] < limit]
        pool, budget = sum([weights[i] for i in free]), rest
        for i in free:
            extra = min(limit - given[i], max(1, budget * weights[i] // pool), rest)
            given[i] = given[i] + extra
            rest = rest - extra
    return np.array([limit] + given)


def ragged(rng, number_of, total, bound, lean):
    if number_of == 2:
        one = jax.random.randint(rng, (), max(1, total - bound), min(bound, total - 1) + 1)
        return jnp.stack([one, total - one])
    sizes = jnp.asarray(profile(number_of, total, bound, lean), jnp.int32)
    twos = (number_of - 1) // 2
    source_of, receiver = sizes[1:1 + 2 * twos:2], sizes[2:2 + 2 * twos:2]
    room = jnp.minimum(source_of - 1, bound - receiver)
    moved = jax.random.randint(jax.random.fold_in(rng, 1), (twos,), 0, 1 << 20) % (room + 1)
    sizes = sizes.at[1:1 + 2 * twos:2].set(source_of - moved).at[2:2 + 2 * twos:2].set(receiver + moved)
    return sizes[jax.random.permutation(jax.random.fold_in(rng, 2), number_of)]


def routed_block(rng, own, number, rows, number_of, top, reach, lean):
    sequence = jax.random.permutation(rng, number_of)
    packed, usual = load_shares(number_of, rows * top, reach, lean, True), load_shares(number_of, rows * top, reach, lean, False)
    places = jnp.arange(number_of)

    def named(lengths, turn):
        used = int((lengths > 0).sum())
        fixed = max(1, used // 4)
        passed = fixed + (places - fixed + turn * (used - fixed)) % max(1, number_of - fixed)
        return jnp.zeros((number_of,), jnp.int32).at[sequence[jnp.where(places < fixed, places, passed)]].set(jnp.asarray(lengths, jnp.int32))

    lengths = jnp.where(number % 4 == 0, named(packed, number // 4), named(usual, number - number // 4 - 1))
    mixed = jax.random.permutation(jax.random.fold_in(own, 3), number_of)
    giver, taker = mixed[0:number_of // 2 * 2:2], mixed[1:number_of // 2 * 2:2]
    slack = jnp.minimum(lengths[giver] - 1, reach - lengths[taker]) // 2
    slack = jnp.where((giver == sequence[0]) | (taker == sequence[0]) | (lengths[taker] == 0), 0, jnp.maximum(slack, 0))
    passed = jax.random.randint(jax.random.fold_in(own, 4), (number_of // 2,), 0, 1 << 20) % (slack + 1)
    lengths = lengths.at[giver].add(-passed).at[taker].add(passed)
    items = jnp.searchsorted(jnp.cumsum(lengths), jnp.arange(rows * top), side="right").astype(jnp.int32)
    table = items.reshape(top, rows).T
    table = table[jax.random.permutation(jax.random.fold_in(own, 1), rows)]
    turn = jax.random.randint(jax.random.fold_in(own, 2), (rows, 1), 0, top)
    return jnp.take_along_axis(table, (jnp.arange(top)[None, :] + turn) % top, axis=1)


def load_shares(amount, total, bound, slope, full):
    weights = [(1 << 20) // math.isqrt(grade ** slope) + 1 for grade in range(1, amount + 1)]
    largest = bound if full else min(bound, max(-(-total // amount), total * weights[0] // sum(weights)))
    least = 1 if total - largest >= amount - 1 else 0
    counts, rest = [largest] + [least] * (amount - 1), total - largest - least * (amount - 1)
    while rest > 0:
        candidates = [i for i in range(1, amount) if counts[i] < largest] or [i for i in range(1, amount) if counts[i] < bound]
        mass, budget = sum([weights[i] for i in candidates]), rest
        for i in candidates:
            more = min(bound - counts[i], max(1, budget * weights[i] // mass), rest)
            counts[i] = counts[i] + more
            rest = rest - more
    return np.array(counts)


def noise(rng, extent, spread, most, shards=(), kind=jnp.bfloat16):
    drawn = spread * jax.random.normal(rng, extent, jnp.float32)
    if shards:
        drawn = drawn * steps_of(rng, extent, shards, -0.22, 0.18)
    return jnp.clip(drawn, -most, most).astype(kind)


def setup_inputs(seed: int = 0) -> dict:
    key_list = jax.random.split(jax.random.key(seed), 13)
    queries = draw_queries(jax.random.fold_in(key_list[12], 71), 0)
    latent = draw_latent(jax.random.fold_in(key_list[12], 71), 0)
    segment_ids = jnp.searchsorted(jnp.cumsum(ragged(key_list[2], 8, LENGTH, LENGTH // 2, 2)), jnp.arange(LENGTH), side="right").astype(jnp.int32)
    value_up = noise(key_list[3], (HEADS, LATENT, VDIM), LATENT ** -0.5, 0.25, ((0, 32),))
    out_proj = noise(key_list[4], (HEADS * VDIM, D), (HEADS * VDIM // 4) ** -0.5, 0.125, ((0, 32),))
    residual = noise(key_list[5], (LENGTH, D), 0.3, 4.0, ((0, 512),))
    norm_gain = jnp.clip(1.0 + 0.18 * jax.random.normal(key_list[6], (D,), jnp.float32), 0.1, 1.9)
    route_ids_keys = jax.random.split(jax.random.fold_in(key_list[7], 1), BLK * BLOCKS // (TOK_DEV * BLOCKS))
    route_ids_turns = jax.random.permutation(jax.random.fold_in(key_list[7], 3), BLK * BLOCKS // (TOK_DEV * BLOCKS))
    route_ids = jax.vmap(lambda own, number: routed_block(jax.random.fold_in(key_list[7], 2), own, number, TOK_DEV * BLOCKS, EXPERTS, TOPK, CAP, 2))(route_ids_keys, route_ids_turns).reshape((BLK, BLOCKS, TOPK))
    route_gates = jnp.clip(0.1 + 0.9 * jax.random.uniform(key_list[8], (BLK, BLOCKS, TOPK), jnp.float32) ** steps_of(key_list[8], (BLK, BLOCKS, TOPK), ((0, 32),), -0.2, 0.2), 0.1, 1.0)
    expert_gate = noise(key_list[9], (EXPERTS, D, FF), D ** -0.5, 0.125, ((0, 32), (1, 16)))
    expert_up = noise(key_list[10], (EXPERTS, D, FF), D ** -0.5, 0.125, ((0, 32), (1, 16)))
    expert_down = noise(key_list[11], (EXPERTS, FF, D), FF ** -0.5, 0.21875, ((0, 32), (2, 16)))
    return dict(queries=queries, latent=latent, segment_ids=segment_ids, value_up=value_up, out_proj=out_proj, residual=residual, norm_gain=norm_gain, route_ids=route_ids, route_gates=route_gates, expert_gate=expert_gate, expert_up=expert_up, expert_down=expert_down)


def reference(queries, latent, segment_ids, value_up, out_proj, residual, norm_gain, route_ids, route_gates, expert_gate, expert_up, expert_down):
    scaling = QKDIM ** (-0.5)
    position = jnp.arange(LENGTH, dtype=jnp.int32)
    allowed = (position[None, :] <= position[:, None]) & (segment_ids[None, :] == segment_ids[:, None])
    values_latent = latent[:, :LATENT]

    def head_step(head_index, attended):
        query_head = lax.dynamic_index_in_dim(queries, head_index, 1, keepdims=False)
        scores = jnp.dot(query_head, latent.T, preferred_element_type=jnp.float32) * scaling
        scores = jnp.where(allowed, scores, -jnp.inf)
        peak_row = lax.optimization_barrier(jnp.max(scores, axis=1, keepdims=True))
        exp_terms = jnp.exp(scores - peak_row)
        totals = lax.optimization_barrier(jnp.sum(exp_terms, axis=1, keepdims=True))
        mixed_latent = (jnp.dot(exp_terms.astype(jnp.bfloat16), values_latent, preferred_element_type=jnp.float32) / totals).astype(jnp.bfloat16)
        up_head = lax.dynamic_index_in_dim(value_up, head_index, 0, keepdims=False)
        head_values = jnp.dot(mixed_latent, up_head, preferred_element_type=jnp.float32).astype(jnp.bfloat16)
        proj_rows = lax.dynamic_slice_in_dim(out_proj, head_index * VDIM, VDIM, 0)
        return attended + jnp.dot(head_values, proj_rows, preferred_element_type=jnp.float32)
    attended = lax.fori_loop(0, HEADS, head_step, jnp.zeros((LENGTH, D), jnp.float32))
    stream = (residual.astype(jnp.float32) + attended).astype(jnp.bfloat16)
    stream_wide = stream.astype(jnp.float32)
    mean_sq = lax.optimization_barrier(jnp.mean(stream_wide * stream_wide, axis=1, keepdims=True))
    normed = (stream_wide * lax.rsqrt(mean_sq + 1e-06) * norm_gain.astype(jnp.float32)[None, :]).astype(jnp.bfloat16)
    token_ids = jnp.transpose(route_ids, (1, 0, 2)).reshape(LENGTH * TOPK)
    token_gates = jnp.transpose(route_gates, (1, 0, 2)).reshape(LENGTH * TOPK)
    width_group = D // N_CTX
    most_rows = N_EXP * CAP
    grouped = normed.reshape(LENGTH, N_CTX, width_group)

    def group_product(inputs, matrix):
        partials = jnp.einsum('rcd,cdf->rcf', inputs, matrix.astype(jnp.float32))
        rounded = lax.optimization_barrier(partials.astype(jnp.bfloat16))
        return lax.optimization_barrier(jnp.sum(rounded.astype(jnp.float32), axis=1))

    def expert_step(expert, mixture):
        chosen = token_ids == expert
        route_count = jnp.sum(chosen.astype(jnp.int32))
        route_pos = jnp.nonzero(chosen, size=most_rows, fill_value=0)[0].astype(jnp.int32)
        is_valid = jnp.arange(most_rows, dtype=jnp.int32) < route_count
        token_rows = (route_pos // TOPK).astype(jnp.int32)
        inputs = grouped[token_rows].astype(jnp.float32)
        gate_mat = lax.dynamic_index_in_dim(expert_gate, expert, 0, keepdims=False).reshape(N_CTX, width_group, FF)
        up_mat = lax.dynamic_index_in_dim(expert_up, expert, 0, keepdims=False).reshape(N_CTX, width_group, FF)
        down_mat = lax.dynamic_index_in_dim(expert_down, expert, 0, keepdims=False)
        gate_pre = group_product(inputs, gate_mat)
        up_pre = group_product(inputs, up_mat)
        hidden = (jax.nn.silu(gate_pre) * up_pre).astype(jnp.bfloat16)
        expert_out = jnp.dot(hidden, down_mat, preferred_element_type=jnp.float32).astype(jnp.bfloat16)
        weight = jnp.where(is_valid, token_gates[route_pos], jnp.zeros((), token_gates.dtype))
        return mixture.at[token_rows].add(weight[:, None] * expert_out.astype(jnp.float32))
    mixture = lax.fori_loop(0, EXPERTS, expert_step, jnp.zeros((LENGTH, D), jnp.float32))
    layer_out = (stream_wide + mixture).astype(jnp.bfloat16)
    return layer_out.reshape(N_CTX, BLK, D).transpose(1, 0, 2)
```

```python
import jax
import jax.numpy as jnp
from jax import lax
from jax.sharding import Mesh, PartitionSpec as P

LATENT = 512
VDIM = 128
QKDIM = 192
EXPERTS = 96
TOPK = 6
CAP = 10
SLOTS = 32

CTX = ("y", "xl")
EXP = ("z", "xh", "core")
SWAP = [(0, 1), (1, 0)]


def shift(count, by):
    return [(i, (i + by) % count) for i in range(count)]


def on_device(
    queries,
    latent,
    segment_ids,
    value_up,
    out_proj,
    residual,
    norm_gain,
    route_ids,
    route_gates,
    expert_gate,
    expert_up,
    expert_down,
):
    f32, bf16 = jnp.float32, jnp.bfloat16
    block_len, local_heads, width_key = queries.shape
    width_model = residual.shape[1]
    width_out = width_model // 16
    width_pair = 2 * width_out
    ff = expert_gate.shape[2]
    ff_half = ff // 2
    y, xl, core = (lax.axis_index(a) for a in ("y", "xl", "core"))
    half = block_len // 2

    def keep_send(array, axis):
        parts = jnp.split(array, 2, axis=axis)
        return jnp.where(xl == 0, parts[0], parts[1]), jnp.where(xl == 0, parts[1], parts[0])

    gate_keep, gate_send = keep_send(expert_gate, 2)
    up_keep, up_send = keep_send(expert_up, 2)
    down_keep, down_send = keep_send(expert_down, 1)
    in_keep = jnp.concatenate([gate_keep, up_keep], axis=2)
    in_got = lax.ppermute(jnp.concatenate([gate_send, up_send], axis=2), "xl", SWAP)
    down_got = lax.ppermute(down_send, "xl", SWAP)
    w_in = jnp.concatenate(
        [jnp.where(xl == 0, in_keep, in_got), jnp.where(xl == 0, in_got, in_keep)], axis=1
    ).reshape(3 * width_pair, 2 * ff_half)
    w_down = jnp.concatenate(
        [jnp.where(xl == 0, down_keep, down_got), jnp.where(xl == 0, down_got, down_keep)], axis=2
    ).reshape(3 * ff_half, width_pair)

    pad = 640 - width_key - 1
    keys_own = jnp.concatenate(
        [latent, segment_ids.astype(bf16)[:, None], jnp.zeros((block_len, pad), bf16)], axis=1
    )
    mine = lax.dynamic_slice_in_dim(keys_own, core * half, half, 0)
    back = [lax.ppermute(mine, "y", shift(8, k)) for k in (1, 2, 3, 4)]
    column = jnp.stack(back)
    other_send = jnp.where(xl == 0, jnp.stack([mine] + back[:3]), column)
    other = lax.ppermute(other_send, "xl", SWAP)
    halves = jnp.concatenate([column, other])
    halves_other = lax.ppermute(halves, "core", SWAP)
    keys_all = jnp.concatenate([halves, halves_other]).reshape(16 * half, 640)
    keys_all = jnp.concatenate([keys_own, keys_all])
    block = 2 * y + xl
    step = jnp.arange(1, 5, dtype=jnp.int32)
    first_other = jnp.where(xl == 0, 2 * (y - step) + 1, 2 * (y - step + 1))
    blocks = jnp.concatenate([2 * (y - step) + xl, first_other])
    rows = jnp.arange(half, dtype=jnp.int32)
    start = blocks * block_len
    pos_halves = jnp.concatenate(
        [
            (start[:, None] + core * half + rows[None, :]).reshape(-1),
            (start[:, None] + (1 - core) * half + rows[None, :]).reshape(-1),
        ]
    )
    key_pos = jnp.concatenate(
        [block * block_len + jnp.arange(block_len, dtype=jnp.int32), pos_halves]
    )
    key_seg = keys_all[:, width_key].astype(jnp.int32)
    rows_all = block_len * local_heads
    query_rows = queries.reshape(rows_all, width_key)
    query_pos = block * block_len + jnp.arange(rows_all, dtype=jnp.int32) // local_heads
    query_seg = jnp.repeat(segment_ids, local_heads)
    allowed = (
        (key_pos[None, :] >= 0)
        & (key_pos[None, :] <= query_pos[:, None])
        & (key_seg[None, :] == query_seg[:, None])
    )
    scores = lax.dot_general(
        query_rows, keys_all[:, :width_key], (((1,), (1,)), ((), ())), preferred_element_type=f32
    ) * (QKDIM ** (-0.5))
    scores = jnp.where(allowed, scores, -jnp.inf)
    peak = jnp.max(scores, axis=1, keepdims=True)
    terms = jnp.exp(scores - peak)
    totals = jnp.sum(terms, axis=1, keepdims=True)
    mixed = jnp.dot(terms.astype(bf16), keys_all[:, :LATENT], preferred_element_type=f32) / totals
    mixed = mixed.astype(bf16).reshape(block_len, local_heads, LATENT)
    head_values = jnp.einsum("thl,hlv->thv", mixed, value_up, preferred_element_type=f32)
    head_values = head_values.astype(bf16).reshape(16, 2, 8, local_heads * VDIM)

    def project(which):
        picked = lax.dynamic_index_in_dim(head_values, which, 1, keepdims=False)
        return jnp.dot(
            picked.reshape(half, local_heads * VDIM), out_proj, preferred_element_type=f32
        )

    got = lax.ppermute(project(1 - core).astype(bf16), "core", SWAP)
    pair_sum = (project(core) + got.astype(f32)).astype(bf16).reshape(16, 8, width_model)
    spread = lax.all_to_all(pair_sum, ("z", "xh"), split_axis=0, concat_axis=0, tiled=True)
    attended = jnp.sum(spread.astype(f32), axis=0)
    stream = (residual.astype(f32) + attended).astype(bf16)
    stream_wide = stream.astype(f32)
    mean_sq = jnp.mean(stream_wide * stream_wide, axis=1, keepdims=True)
    normed = (stream_wide * lax.rsqrt(mean_sq + 1e-06) * norm_gain[None, :]).astype(bf16)

    packed = jnp.stack(
        [
            jnp.concatenate(
                [
                    normed[:, (c // 2) * width_pair : (c // 2 + 1) * width_pair],
                    stream[:, c * width_out : (c + 1) * width_out],
                ],
                axis=1,
            )
            for c in range(16)
        ]
    )
    split = lax.all_to_all(packed, CTX, split_axis=0, concat_axis=0, tiled=True)
    split = split.reshape(128, width_pair + width_out)

    routes = jnp.transpose(route_ids, (1, 0, 2)).reshape(128, TOPK)
    expert_axis = jnp.arange(EXPERTS, dtype=jnp.int32)
    named = jnp.any(routes[:, :, None] == expert_axis[None, None, :], axis=1)
    earlier_tokens = jnp.tril(jnp.ones((128, 128), bf16), -1)
    slot_all = jnp.dot(earlier_tokens, named.astype(bf16), preferred_element_type=f32).astype(jnp.int32)
    slot_of = jnp.sum(
        jnp.where(routes[:, :, None] == expert_axis[None, None, :], slot_all[:, None, :], 0), axis=2
    )
    target = (routes // 3) * SLOTS + (routes % 3) * CAP + slot_of
    slot_axis = jnp.arange(32 * SLOTS, dtype=jnp.int32)
    matches = target[:, :, None] == slot_axis[None, None, :]
    picker = jnp.any(matches, axis=1).astype(bf16)
    order = jnp.arange(128, dtype=jnp.int32)
    back_order = ((order % 16) * 8 + order // 16)[:, None] == order[None, :]
    target_rb = jnp.transpose(target.reshape(16, 8, TOPK), (1, 0, 2)).reshape(128, TOPK)
    gates_rb = route_gates.reshape(128, TOPK)
    weighting = jnp.sum(
        jnp.where(target_rb[:, :, None] == slot_axis[None, None, :], gates_rb[:, :, None], 0.0),
        axis=1,
    )

    outgoing = lax.dot_general(
        picker, split[:, :width_pair], (((0,), (0,)), ((), ())), preferred_element_type=f32
    ).astype(bf16)
    received = lax.all_to_all(
        outgoing.reshape(32, SLOTS, width_pair), EXP, split_axis=0, concat_axis=0, tiled=True
    ).reshape(32 * SLOTS, width_pair)
    row_expert = (slot_axis % SLOTS) // CAP

    def widen(array):
        return jnp.concatenate(
            [jnp.where((row_expert == j)[:, None], array, jnp.zeros_like(array)) for j in range(3)],
            axis=1,
        )

    pre = jnp.dot(widen(received), w_in, preferred_element_type=f32).astype(bf16)
    pre_parts = lax.all_to_all(
        pre.reshape(8, 128, 2 * ff_half), "y", split_axis=0, concat_axis=0, tiled=True
    )
    pre_sum = jnp.sum(pre_parts.astype(f32), axis=0)
    hidden = (jax.nn.silu(pre_sum[:, :ff_half]) * pre_sum[:, ff_half:]).astype(bf16)
    hidden_all = lax.all_to_all(
        jnp.broadcast_to(hidden[None], (8, 128, ff_half)), "y", split_axis=0, concat_axis=0, tiled=True
    ).reshape(32 * SLOTS, ff_half)
    expert_out = jnp.dot(widen(hidden_all), w_down, preferred_element_type=f32).astype(bf16)
    returned = lax.all_to_all(
        expert_out.reshape(32, SLOTS, width_pair), EXP, split_axis=0, concat_axis=0, tiled=True
    ).reshape(32 * SLOTS, width_pair)
    mixture = jnp.dot(weighting, returned.astype(f32), precision=lax.Precision.HIGHEST)
    low, high = mixture[:, :width_out], mixture[:, width_out:]
    mix_got = lax.ppermute(jnp.where(xl == 0, high, low).astype(bf16), "xl", SWAP)
    stream_rb = jnp.dot(back_order.astype(bf16), split[:, width_pair:], preferred_element_type=f32)
    result = (stream_rb + jnp.where(xl == 0, low, high) + mix_got.astype(f32)).astype(bf16)
    return result.reshape(8, 16, width_out)


def solution(mesh):
    grid = Mesh(mesh.devices.reshape(8, 2, 8, 2, 2), ("y", "xl", "z", "xh", "core"))
    return jax.shard_map(
        on_device,
        mesh=grid,
        in_specs=(
            P(CTX, EXP, None),
            P(CTX, None),
            P(CTX),
            P(EXP, None, None),
            P(EXP, None),
            P(CTX + EXP, None),
            P(),
            P(EXP, None, None),
            P(EXP, None, None),
            P(EXP, CTX, None),
            P(EXP, CTX, None),
            P(EXP, None, CTX),
        ),
        out_specs=P(EXP, None, CTX),
        check_vma=False,
    )
```

```python
import jax
import jax.numpy as jnp
from jax import lax
from jax.experimental import pallas as pl
from jax.experimental.pallas import tpu as pltpu
from jax.sharding import Mesh, PartitionSpec as P

LATENT = 512
VDIM = 128
QKDIM = 192
EXPERTS = 96
TOPK = 6
CAP = 10
SLOTS = 32
SEGMENTS = 8
KEYW = 640
FAR = float(2**20)

CTX = ("y", "xl")
EXP = ("z", "xh", "core")
SWAP = [(0, 1), (1, 0)]
BIG_VMEM = pltpu.CompilerParams(vmem_limit_bytes=44 * 2**20)
f32, bf16, i32 = jnp.float32, jnp.bfloat16, jnp.int32


def nt_dot(a, b):
    return lax.dot_general(a, b, (((1,), (1,)), ((), ())), preferred_element_type=f32)


def attention_kernel(
    info, query, own, p0, p1, p2, p3, o0, o1, o2, o3, value_up, out_proj, send, keep, scores, values
):
    scale = QKDIM ** (-0.5)
    core = info[8]
    chunks = [own] + [p0, p1, p2, p3] + [o0, o1, o2, o3]
    lane = lax.broadcasted_iota(i32, (256, 256), 1)
    row = lax.broadcasted_iota(i32, (256, 256), 0)
    token = (row % 128) // 8 * 16 + row // 128 * 8 + row % 8

    @pl.loop(0, 2)
    def _(head):
        rows = query[head]
        peak = jnp.full((256, 128), -jnp.inf, f32)
        for n, chunk in enumerate(chunks):
            keys = chunk[...].reshape(256, KEYW)
            part = nt_dot(rows, keys) * scale
            if n == 0:
                part = jnp.where(lane <= token, part, -FAR)
            else:
                piece = (n - 1) % 4
                first = jnp.where(info[2 * piece] >= 0, 0.0, -FAR)
                second = jnp.where(info[2 * piece + 1] >= 0, 0.0, -FAR)
                part = part + jnp.where(lane < 128, first, second)
            scores[:, n * 256 : (n + 1) * 256] = part
            peak = jnp.maximum(peak, jnp.maximum(part[:, :128], part[:, 128:]))
        peak = jnp.max(peak, axis=1, keepdims=True)
        sums = jnp.zeros((256, 128), f32)
        mixed = jnp.zeros((256, LATENT), f32)
        for n, chunk in enumerate(chunks):
            keys = chunk[...].reshape(256, KEYW)
            terms = jnp.exp(scores[:, n * 256 : (n + 1) * 256] - peak)
            sums = sums + terms[:, :128] + terms[:, 128:]
            mixed = mixed + jnp.dot(terms.astype(bf16), keys[:, :LATENT], preferred_element_type=f32)
        mixed = (mixed / jnp.sum(sums, axis=1, keepdims=True)).astype(bf16)
        values[head] = jnp.dot(mixed, value_up[head], preferred_element_type=f32).astype(bf16)

    def project(which, out):
        start = pl.multiple_of(which * 128, 128)
        left = values[0, pl.ds(start, 128), :]
        right = values[1, pl.ds(start, 128), :]
        both = jnp.concatenate([left, right], axis=1)
        for c in range(0, out.shape[1], 640):
            out[:, c : c + 640] = jnp.dot(
                both, out_proj[:, c : c + 640], preferred_element_type=f32
            ).astype(out.dtype)

    project(1 - core, send)
    project(core, keep)


def norm_kernel(spread, residual, gain, packed):
    attended = jnp.sum(spread[...].astype(f32), axis=0)
    stream = (residual[...].astype(f32) + attended).astype(bf16).astype(f32)
    mean_sq = jnp.mean(stream * stream, axis=1, keepdims=True)
    normed = (stream * lax.rsqrt(mean_sq + 1e-06) * gain[...]).astype(bf16).astype(f32)
    width = stream.shape[1] // 16
    fill = jnp.zeros((stream.shape[0], packed.shape[2] - 3 * width), f32)
    for c in range(16):
        mine, other = c * width, (c ^ 1) * width
        packed[c] = jnp.concatenate(
            [
                normed[:, mine : mine + width],
                normed[:, other : other + width],
                stream[:, mine : mine + width],
                fill,
            ],
            axis=1,
        ).astype(bf16)


def row_masks(count):
    slot = lax.broadcasted_iota(i32, (count, 1), 0) % SLOTS
    return [(slot >= j * CAP) & (slot < (j + 1) * CAP) for j in range(3)]


def masked(rows, mask):
    return jnp.where(mask, rows.astype(f32), 0.0).astype(bf16)


def gate_up_kernel(received, weights, pre):
    width = pre.shape[1]

    @pl.loop(0, received.shape[0] // 256)
    def _(n):
        start = pl.multiple_of(n * 256, 256)
        rows = received[pl.ds(start, 256), :]
        masks = row_masks(256)
        total = jnp.zeros((256, width), f32)
        for j in range(3):
            total = total + jnp.dot(
                masked(rows, masks[j]), weights[j, :, :width], preferred_element_type=f32
            )
        pre[pl.ds(start, 256), :] = total.astype(bf16)


def hidden_kernel(parts, out):
    total = jnp.sum(parts[...].astype(f32), axis=0)
    half = total.shape[1] // 2
    gate, up = total[:, :half], total[:, half:]
    hidden = (gate / (1.0 + jnp.exp(-gate)) * up).astype(bf16)
    for n in range(out.shape[0]):
        out[n] = hidden


def down_kernel(hidden, weights, out):
    width = hidden.shape[1]

    @pl.loop(0, hidden.shape[0] // 256)
    def _(n):
        start = pl.multiple_of(n * 256, 256)
        rows = hidden[pl.ds(start, 256), :]
        masks = row_masks(256)
        total = jnp.zeros((256, out.shape[1]), f32)
        for j in range(3):
            total = total + nt_dot(masked(rows, masks[j]), weights[j, :, -width:])
        out[pl.ds(start, 256), :] = total.astype(bf16)


def combine_kernel(weighting, returned, keep, send):
    width = keep.shape[1]
    top = weighting[...].astype(bf16)
    rest = (weighting[...] - top.astype(f32)).astype(bf16)
    mixture = jnp.dot(top, returned[...], preferred_element_type=f32) + jnp.dot(
        rest, returned[...], preferred_element_type=f32
    )
    keep[...] = mixture[:, :width]
    send[...] = mixture[:, width:].astype(bf16)


def call(kernel, outs, scratch=(), smem_first=False, count=0):
    specs = [pl.BlockSpec(memory_space=pltpu.VMEM)] * count
    if smem_first:
        specs[0] = pl.BlockSpec(memory_space=pltpu.SMEM)
    out_specs = [pl.BlockSpec(memory_space=pltpu.VMEM)] * len(outs)
    single = len(outs) == 1
    return pl.pallas_call(
        kernel,
        in_specs=specs,
        out_specs=out_specs[0] if single else out_specs,
        out_shape=outs[0] if single else outs,
        scratch_shapes=list(scratch),
        compiler_params=BIG_VMEM,
    )


def sds(shape, dtype):
    return jax.ShapeDtypeStruct(shape, dtype)


def on_device(
    queries,
    latent,
    segment_ids,
    value_up,
    out_proj,
    residual,
    norm_gain,
    route_ids,
    route_gates,
    expert_gate,
    expert_up,
    expert_down,
):
    block_len, local_heads, width_key = queries.shape
    width_model = residual.shape[1]
    width_out = width_model // 16
    width_pair = 2 * width_out
    ff = expert_gate.shape[2]
    ff_half = ff // 2
    y, xl, xh, core = (lax.axis_index(a) for a in ("y", "xl", "xh", "core"))
    half = block_len // 2

    segment_axis = jnp.arange(SEGMENTS, dtype=i32)
    own_segment = segment_ids[:, None] == segment_axis[None, :]
    pad = KEYW - width_key - SEGMENTS
    keys_own = jnp.concatenate(
        [latent, own_segment.astype(bf16), jnp.zeros((block_len, pad), bf16)], axis=1
    )
    mine = lax.dynamic_slice_in_dim(keys_own, core * half, half, 0)

    def along_y(near, far):
        pairs = [
            (2 * i + h, 2 * ((i + (near, far)[h]) % 8) + h) for i in range(8) for h in range(2)
        ]
        return lax.ppermute(mine, ("y", "xh"), pairs)

    column = jnp.stack([along_y(1, 3), along_y(2, 4)])
    to_other = jnp.where(
        (xl == 0) & (xh == 1), jnp.stack([mine, column[0]]), column
    )
    diagonal = [(0, 3), (1, 2), (2, 1), (3, 0)]
    pieces = [
        column,
        lax.ppermute(column, "xh", SWAP),
        lax.ppermute(to_other, "xl", SWAP),
        lax.ppermute(to_other, ("xl", "xh"), diagonal),
    ]
    others = [lax.ppermute(piece, "core", SWAP) for piece in pieces]

    def blocks_of(x, h):
        return [2 * (y - 1 - 2 * h) + x, 2 * (y - 2 - 2 * h) + x]

    def blocks_sent(x, h):
        near, far = blocks_of(x, h)
        odd = (x == 0) & (h == 1)
        return [jnp.where(odd, 2 * y, near), jnp.where(odd, near, far)]

    info = jnp.stack(
        blocks_of(xl, xh)
        + blocks_of(xl, 1 - xh)
        + blocks_sent(1 - xl, xh)
        + blocks_sent(1 - xl, 1 - xh)
        + [core]
    ).astype(i32)

    masks = jnp.where(own_segment, 0.0, -FAR).astype(bf16)
    query_rows = jnp.concatenate(
        [
            queries,
            jnp.broadcast_to(masks[:, None, :], (block_len, local_heads, SEGMENTS)),
            jnp.zeros((block_len, local_heads, pad), bf16),
        ],
        axis=2,
    )
    query_rows = query_rows.reshape(16, 2, 8, local_heads, KEYW).transpose(3, 1, 0, 2, 4)
    query_rows = query_rows.reshape(local_heads, block_len, KEYW)
    send, keep = call(
        attention_kernel,
        [sds((half, width_model), bf16), sds((half, width_model), f32)],
        [pltpu.VMEM((256, 9 * 256), f32), pltpu.VMEM((2, 256, VDIM), bf16)],
        smem_first=True,
        count=13,
    )(info, query_rows, keys_own, *pieces, *others, value_up, out_proj)
    got = lax.ppermute(send, "core", SWAP)
    pair_sum = (keep + got.astype(f32)).astype(bf16).reshape(16, 8, width_model)

    weights = [expert_gate, expert_up, jnp.transpose(expert_down, (0, 2, 1))]
    low = jnp.concatenate([w[:, :, :ff_half] for w in weights], axis=2)
    high = jnp.concatenate([w[:, :, ff_half:] for w in weights], axis=2)
    w_send = jnp.where(xl == 0, high, low)
    w_keep = jnp.where(xl == 0, low, high)
    pair_sum, w_send = lax.optimization_barrier((pair_sum, w_send))
    w_got = lax.ppermute(w_send, "xl", SWAP)

    spread = lax.all_to_all(pair_sum, ("z", "xh"), split_axis=0, concat_axis=0, tiled=True)
    spread, w_got = lax.optimization_barrier((spread, w_got))
    w_all = jnp.concatenate([w_keep, w_got], axis=1)
    packed = call(norm_kernel, [sds((16, 8, 512), bf16)], count=3)(
        spread, residual, norm_gain[None, :]
    )
    split = lax.all_to_all(packed, CTX, split_axis=0, concat_axis=0, tiled=True)
    split = split.reshape(128, 512)

    routes = jnp.transpose(route_ids, (1, 0, 2)).reshape(128, TOPK)
    expert_axis = jnp.arange(EXPERTS, dtype=i32)
    named = jnp.any(routes[:, :, None] == expert_axis[None, None, :], axis=1)
    earlier_tokens = jnp.tril(jnp.ones((128, 128), bf16), -1)
    slot_all = jnp.dot(earlier_tokens, named.astype(bf16), preferred_element_type=f32).astype(i32)
    slot_of = jnp.sum(
        jnp.where(routes[:, :, None] == expert_axis[None, None, :], slot_all[:, None, :], 0), axis=2
    )
    target = (routes // 3) * SLOTS + (routes % 3) * CAP + slot_of
    slot_axis = jnp.arange(32 * SLOTS, dtype=i32)
    picker = jnp.any(target.T[None, :, :] == slot_axis[:, None, None], axis=1).astype(bf16)
    order = jnp.arange(128, dtype=i32)
    back_order = ((order % 16) * 8 + order // 16)[:, None] == order[None, :]
    target_rb = jnp.transpose(target.reshape(16, 8, TOPK), (1, 0, 2)).reshape(128, TOPK)
    gates_rb = route_gates.reshape(128, TOPK)
    weighting = jnp.sum(
        jnp.where(target_rb[:, :, None] == slot_axis[None, None, :], gates_rb[:, :, None], 0.0),
        axis=1,
    )

    outgoing = jnp.dot(picker, split[:, :width_pair], preferred_element_type=f32).astype(bf16)
    received = lax.all_to_all(
        outgoing.reshape(32, SLOTS, width_pair), EXP, split_axis=0, concat_axis=0, tiled=True
    ).reshape(32 * SLOTS, width_pair)
    pre = call(gate_up_kernel, [sds((32 * SLOTS, 2 * ff_half), bf16)], count=2)(received, w_all)
    pre_parts = lax.all_to_all(
        pre.reshape(8, 128, 2 * ff_half), "y", split_axis=0, concat_axis=0, tiled=True
    )
    hidden = call(hidden_kernel, [sds((8, 128, ff_half), bf16)], count=1)(pre_parts)
    hidden_all = lax.all_to_all(hidden, "y", split_axis=0, concat_axis=0, tiled=True)
    expert_out = call(down_kernel, [sds((32 * SLOTS, width_pair), bf16)], count=2)(
        hidden_all.reshape(32 * SLOTS, ff_half), w_all
    )
    returned = lax.all_to_all(
        expert_out.reshape(32, SLOTS, width_pair), EXP, split_axis=0, concat_axis=0, tiled=True
    ).reshape(32 * SLOTS, width_pair)
    mix_keep, mix_send = call(
        combine_kernel, [sds((128, width_out), f32), sds((128, width_out), bf16)], count=2
    )(weighting, returned)
    mix_got = lax.ppermute(mix_send, "xl", SWAP)
    stream_rb = jnp.dot(
        back_order.astype(bf16),
        split[:, width_pair : width_pair + width_out],
        preferred_element_type=f32,
    )
    result = (stream_rb + mix_keep + mix_got.astype(f32)).astype(bf16)
    return result.reshape(8, 16, width_out)


def solution(mesh):
    grid = Mesh(mesh.devices.reshape(8, 2, 8, 2, 2), ("y", "xl", "z", "xh", "core"))
    return jax.shard_map(
        on_device,
        mesh=grid,
        in_specs=(
            P(CTX, EXP, None),
            P(CTX, None),
            P(CTX),
            P(EXP, None, None),
            P(EXP, None),
            P(CTX + EXP, None),
            P(),
            P(EXP, None, None),
            P(EXP, None, None),
            P(EXP, CTX, None),
            P(EXP, CTX, None),
            P(EXP, None, CTX),
        ),
        out_specs=P(EXP, None, CTX),
        check_vma=False,
    )
```

```python
import jax
import jax.numpy as jnp
from jax import lax
from jax.experimental import pallas as pl
from jax.experimental.pallas import tpu as pltpu
from jax.sharding import Mesh, PartitionSpec as P

LATENT = 512
VDIM = 128
QKDIM = 192
EXPERTS = 96
TOPK = 6
CAP = 10
SLOTS = 32
SEGMENTS = 8
KEYW = 640
FAR = float(2**20)

CTX = ("y", "xl")
EXP = ("z", "xh", "core")
SWAP = [(0, 1), (1, 0)]
BIG_VMEM = pltpu.CompilerParams(vmem_limit_bytes=44 * 2**20)
f32, bf16, i32 = jnp.float32, jnp.bfloat16, jnp.int32


def nt_dot(a, b):
    return lax.dot_general(a, b, (((1,), (1,)), ((), ())), preferred_element_type=f32)


def attend_chunks(rows, chunks, biases, scores, old):
    scale = QKDIM ** (-0.5)
    peak = jnp.full((256, 128), -FAR, f32) if old is None else old[0]
    for n, (chunk, bias) in enumerate(zip(chunks, biases)):
        part = bias(nt_dot(rows, chunk[...].reshape(256, KEYW)) * scale)
        scores[:, n * 256 : (n + 1) * 256] = part
        peak = jnp.maximum(peak, jnp.maximum(part[:, :128], part[:, 128:]))
    peak = jnp.max(peak, axis=1, keepdims=True)
    if old is None:
        sums, mixed = jnp.zeros((256, 128), f32), jnp.zeros((256, LATENT), f32)
    else:
        factor = jnp.exp(old[0][:, :1] - peak)
        sums, mixed = old[1] * factor, old[2] * factor
    for n, chunk in enumerate(chunks):
        terms = jnp.exp(scores[:, n * 256 : (n + 1) * 256] - peak)
        sums = sums + terms[:, :128] + terms[:, 128:]
        keys = chunk[...].reshape(256, KEYW)
        mixed = mixed + jnp.dot(terms.astype(bf16), keys[:, :LATENT], preferred_element_type=f32)
    return jnp.broadcast_to(peak, (256, 128)), sums, mixed


def valid_bias(info, piece):
    def bias(part):
        lane = lax.broadcasted_iota(i32, (256, 256), 1)
        first = jnp.where(info[2 * piece] >= 0, 0.0, -FAR)
        second = jnp.where(info[2 * piece + 1] >= 0, 0.0, -FAR)
        return part + jnp.where(lane < 128, first, second)

    return bias


def causal_bias(part):
    lane = lax.broadcasted_iota(i32, (256, 256), 1)
    row = lax.broadcasted_iota(i32, (256, 256), 0)
    token = (row % 128) // 8 * 16 + row // 128 * 8 + row % 8
    return jnp.where(lane <= token, part, -FAR)


def first_attention_kernel(info, query, own, p0, peak, sums, mixed, scores):
    @pl.loop(0, 2)
    def _(head):
        state = attend_chunks(
            query[head], [own, p0], [causal_bias, valid_bias(info, 0)], scores, None
        )
        peak[head], sums[head], mixed[head] = state


def second_attention_kernel(
    info, query, p1, p2, p3, o0, old_peak, old_sums, old_mixed, peak, sums, mixed, scores
):
    @pl.loop(0, 2)
    def _(head):
        old = old_peak[head], old_sums[head], old_mixed[head]
        biases = [valid_bias(info, n) for n in (1, 2, 3, 0)]
        state = attend_chunks(query[head], [p1, p2, p3, o0], biases, scores, old)
        peak[head], sums[head], mixed[head] = state


def last_attention_kernel(
    info,
    query,
    o1,
    o2,
    o3,
    old_peak,
    old_sums,
    old_mixed,
    value_up,
    out_proj,
    send,
    keep,
    scores,
    values,
):
    core = info[8]

    @pl.loop(0, 2)
    def _(head):
        old = old_peak[head], old_sums[head], old_mixed[head]
        biases = [valid_bias(info, n) for n in (1, 2, 3)]
        _, sums, mixed = attend_chunks(query[head], [o1, o2, o3], biases, scores, old)
        mixed = (mixed / jnp.sum(sums, axis=1, keepdims=True)).astype(bf16)
        values[head] = jnp.dot(mixed, value_up[head], preferred_element_type=f32).astype(bf16)

    def project(which, out):
        start = pl.multiple_of(which * 128, 128)
        left = values[0, pl.ds(start, 128), :]
        right = values[1, pl.ds(start, 128), :]
        both = jnp.concatenate([left, right], axis=1)
        for c in range(0, out.shape[1], 640):
            out[:, c : c + 640] = jnp.dot(
                both, out_proj[:, c : c + 640], preferred_element_type=f32
            ).astype(out.dtype)

    project(1 - core, send)
    project(core, keep)


def norm_kernel(spread, residual, gain, packed):
    attended = jnp.sum(spread[...].astype(f32), axis=0)
    stream = (residual[...].astype(f32) + attended).astype(bf16).astype(f32)
    mean_sq = jnp.mean(stream * stream, axis=1, keepdims=True)
    normed = (stream * lax.rsqrt(mean_sq + 1e-06) * gain[...]).astype(bf16).astype(f32)
    width = stream.shape[1] // 16
    fill = jnp.zeros((stream.shape[0], packed.shape[2] - 3 * width), f32)
    for c in range(16):
        mine, other = c * width, (c ^ 1) * width
        packed[c] = jnp.concatenate(
            [
                normed[:, mine : mine + width],
                normed[:, other : other + width],
                stream[:, mine : mine + width],
                fill,
            ],
            axis=1,
        ).astype(bf16)


def pick_kernel(picker, split, out):
    out[...] = jnp.dot(picker[...], split[:, : out.shape[1]], preferred_element_type=f32).astype(bf16)


def row_mask(count, j):
    slot = lax.broadcasted_iota(i32, (count, 1), 0) % SLOTS
    return jnp.where((slot >= j * CAP) & (slot < (j + 1) * CAP), 1.0, 0.0).astype(bf16)


def slot_places(full, packed, expert=None):
    wide = lax.broadcasted_iota(i32, (full, packed), 0)
    tight = lax.broadcasted_iota(i32, (full, packed), 1)
    slot = wide % SLOTS
    low, high = (0, 3 * CAP) if expert is None else (expert * CAP, (expert + 1) * CAP)
    found = (wide // SLOTS * 3 * CAP + slot == tight) & (slot >= low) & (slot < high)
    return jnp.where(found, 1.0, 0.0).astype(bf16)


def gate_up_kernel(received, weights, pre):
    chunks, packed, width = pre.shape
    full = received.shape[0] // chunks
    places = slot_places(full, packed)
    step = 4 * full
    for r in range(0, received.shape[0], step):
        rows = received[r : r + step, :]
        for c in range(0, width, 256):
            total = jnp.zeros((step, 256), f32)
            for j in range(3):
                total = total + jnp.dot(
                    rows * row_mask(step, j),
                    weights[j, :, c : c + 256],
                    preferred_element_type=f32,
                )
            total = total.astype(bf16)
            for n in range(4):
                pre[r // full + n, :, c : c + 256] = lax.dot_general(
                    places,
                    total[n * full : (n + 1) * full],
                    (((0,), (0,)), ((), ())),
                    preferred_element_type=f32,
                ).astype(bf16)


def hidden_kernel(parts, out):
    total = jnp.sum(parts[...].astype(f32), axis=0)
    half = total.shape[1] // 2
    gate, up = total[:, :half], total[:, half:]
    hidden = (gate / (1.0 + jnp.exp(-gate)) * up).astype(bf16)
    for n in range(out.shape[0]):
        out[n] = hidden


def down_kernel(hidden, weights, out):
    chunks, packed, width = hidden.shape
    full = out.shape[0] // chunks
    places = [slot_places(full, packed, j) for j in range(3)]
    for r in range(0, chunks, 4):
        total = jnp.zeros((4 * full, out.shape[1]), f32)
        for j in range(3):
            rows = [
                jnp.dot(places[j], hidden[r + n], preferred_element_type=f32).astype(bf16)
                for n in range(4)
            ]
            total = total + nt_dot(jnp.concatenate(rows, axis=0), weights[j])
        out[r * full : (r + 4) * full, :] = total.astype(bf16)


def combine_kernel(weighting, returned, keep, send):
    width = keep.shape[1]
    top = weighting[...].astype(bf16)
    rest = (weighting[...] - top.astype(f32)).astype(bf16)
    mixture = jnp.dot(top, returned[...], preferred_element_type=f32) + jnp.dot(
        rest, returned[...], preferred_element_type=f32
    )
    keep[...] = mixture[:, :width]
    send[...] = mixture[:, width:].astype(bf16)


def call(kernel, outs, scratch=(), smem_first=False, count=0):
    specs = [pl.BlockSpec(memory_space=pltpu.VMEM)] * count
    if smem_first:
        specs[0] = pl.BlockSpec(memory_space=pltpu.SMEM)
    out_specs = [pl.BlockSpec(memory_space=pltpu.VMEM)] * len(outs)
    single = len(outs) == 1
    return pl.pallas_call(
        kernel,
        in_specs=specs,
        out_specs=out_specs[0] if single else out_specs,
        out_shape=outs[0] if single else outs,
        scratch_shapes=list(scratch),
        compiler_params=BIG_VMEM,
    )


def sds(shape, dtype):
    return jax.ShapeDtypeStruct(shape, dtype)


def on_device(
    queries,
    latent,
    segment_ids,
    value_up,
    out_proj,
    residual,
    norm_gain,
    route_ids,
    route_gates,
    expert_gate,
    expert_up,
    expert_down,
):
    block_len, local_heads, width_key = queries.shape
    width_model = residual.shape[1]
    width_out = width_model // 16
    width_pair = 2 * width_out
    ff = expert_gate.shape[2]
    ff_half = ff // 2
    y, xl, xh, core = (lax.axis_index(a) for a in ("y", "xl", "xh", "core"))
    half = block_len // 2

    segment_axis = jnp.arange(SEGMENTS, dtype=i32)
    own_segment = segment_ids[:, None] == segment_axis[None, :]
    pad = KEYW - width_key - SEGMENTS
    keys_own = jnp.concatenate(
        [latent, own_segment.astype(bf16), jnp.zeros((block_len, pad), bf16)], axis=1
    )
    mine = lax.dynamic_slice_in_dim(keys_own, core * half, half, 0)

    def along_y(near, far):
        pairs = [
            (2 * i + h, 2 * ((i + (near, far)[h]) % 8) + h) for i in range(8) for h in range(2)
        ]
        return lax.ppermute(mine, ("y", "xh"), pairs)

    column = jnp.stack([along_y(1, 3), along_y(2, 4)])
    to_other = jnp.where(
        (xl == 0) & (xh == 1), jnp.stack([mine, column[0]]), column
    )
    diagonal = [(0, 3), (1, 2), (2, 1), (3, 0)]
    pieces = [
        column,
        lax.ppermute(column, "xh", SWAP),
        lax.ppermute(to_other, "xl", SWAP),
        lax.ppermute(to_other, ("xl", "xh"), diagonal),
    ]

    def blocks_of(x, h):
        return [2 * (y - 1 - 2 * h) + x, 2 * (y - 2 - 2 * h) + x]

    def blocks_sent(x, h):
        near, far = blocks_of(x, h)
        odd = (x == 0) & (h == 1)
        return [jnp.where(odd, 2 * y, near), jnp.where(odd, near, far)]

    info = jnp.stack(
        blocks_of(xl, xh)
        + blocks_of(xl, 1 - xh)
        + blocks_sent(1 - xl, xh)
        + blocks_sent(1 - xl, 1 - xh)
        + [core]
    ).astype(i32)

    masks = jnp.where(own_segment, 0.0, -FAR).astype(bf16)
    query_rows = jnp.concatenate(
        [
            queries,
            jnp.broadcast_to(masks[:, None, :], (block_len, local_heads, SEGMENTS)),
            jnp.zeros((block_len, local_heads, pad), bf16),
        ],
        axis=2,
    )
    query_rows = query_rows.reshape(16, 2, 8, local_heads, KEYW).transpose(3, 1, 0, 2, 4)
    query_rows = query_rows.reshape(local_heads, block_len, KEYW)
    state_out = [
        sds((2, 256, 128), f32),
        sds((2, 256, 128), f32),
        sds((2, 256, LATENT), f32),
    ]
    state = call(
        first_attention_kernel, state_out, [pltpu.VMEM((256, 2 * 256), f32)], True, 4
    )(info, query_rows, keys_own, column)
    piece_x, peak = lax.optimization_barrier((pieces[1], state[0]))
    pieces[1], state = piece_x, [peak] + list(state[1:])
    others = [lax.ppermute(piece, "core", SWAP) for piece in pieces]
    state = call(
        second_attention_kernel, state_out, [pltpu.VMEM((256, 4 * 256), f32)], True, 9
    )(info, query_rows, pieces[1], pieces[2], pieces[3], others[0], *state)
    send, keep = call(
        last_attention_kernel,
        [sds((half, width_model), bf16), sds((half, width_model), f32)],
        [pltpu.VMEM((256, 3 * 256), f32), pltpu.VMEM((2, 256, VDIM), bf16)],
        True,
        10,
    )(info, query_rows, others[1], others[2], others[3], *state, value_up, out_proj)
    got = lax.ppermute(send, "core", SWAP)
    pair_sum = (keep + got.astype(f32)).astype(bf16).reshape(16, 8, width_model)

    weights = [expert_gate, expert_up, jnp.transpose(expert_down, (0, 2, 1))]
    low = jnp.concatenate([w[:, :, :ff_half] for w in weights], axis=2)
    high = jnp.concatenate([w[:, :, ff_half:] for w in weights], axis=2)
    w_send = jnp.where(xl == 0, high, low)
    w_keep = jnp.where(xl == 0, low, high)
    pair_sum, w_send = lax.optimization_barrier((pair_sum, w_send))
    w_got = lax.ppermute(w_send, "xl", SWAP)

    spread = lax.all_to_all(pair_sum, ("z", "xh"), split_axis=0, concat_axis=0, tiled=True)
    packed = call(norm_kernel, [sds((16, 8, 512), bf16)], count=3)(
        spread, residual, norm_gain[None, :]
    )
    split = lax.all_to_all(packed, CTX, split_axis=0, concat_axis=0, tiled=True)
    split, w_got = lax.optimization_barrier((split, w_got))
    split = split.reshape(128, 512)
    w_both = jnp.concatenate([w_keep, w_got], axis=1)
    rows_in = 384
    w_in = jnp.pad(w_both[:, :, : 2 * ff_half], ((0, 0), (0, rows_in - width_pair), (0, 0)))
    w_down = w_both[:, :, 2 * ff_half :]

    routes = jnp.transpose(route_ids, (1, 0, 2)).reshape(128, TOPK)
    expert_axis = jnp.arange(EXPERTS, dtype=i32)
    named = jnp.any(routes[:, :, None] == expert_axis[None, None, :], axis=1)
    earlier_tokens = jnp.tril(jnp.ones((128, 128), bf16), -1)
    slot_all = jnp.dot(earlier_tokens, named.astype(bf16), preferred_element_type=f32).astype(i32)
    slot_of = jnp.sum(
        jnp.where(routes[:, :, None] == expert_axis[None, None, :], slot_all[:, None, :], 0), axis=2
    )
    target = (routes // 3) * SLOTS + (routes % 3) * CAP + slot_of
    slot_axis = jnp.arange(32 * SLOTS, dtype=i32)
    picker = jnp.any(target.T[None, :, :] == slot_axis[:, None, None], axis=1).astype(bf16)
    order = jnp.arange(128, dtype=i32)
    back_order = ((order % 16) * 8 + order // 16)[:, None] == order[None, :]
    target_rb = jnp.transpose(target.reshape(16, 8, TOPK), (1, 0, 2)).reshape(128, TOPK)
    gates_rb = route_gates.reshape(128, TOPK)
    weighting = jnp.sum(
        jnp.where(target_rb[:, :, None] == slot_axis[None, None, :], gates_rb[:, :, None], 0.0),
        axis=1,
    )

    outgoing = call(pick_kernel, [sds((32 * SLOTS, rows_in), bf16)], count=2)(picker, split)
    received = lax.all_to_all(
        outgoing.reshape(32, SLOTS, rows_in), EXP, split_axis=0, concat_axis=0, tiled=True
    ).reshape(32 * SLOTS, rows_in)
    packed_rows = 4 * 3 * CAP
    pre = call(gate_up_kernel, [sds((8, packed_rows, 2 * ff_half), bf16)], count=2)(received, w_in)
    pre_parts = lax.all_to_all(pre, "y", split_axis=0, concat_axis=0, tiled=True)
    hidden = call(hidden_kernel, [sds((8, packed_rows, ff_half), bf16)], count=1)(pre_parts)
    hidden_all = lax.all_to_all(hidden, "y", split_axis=0, concat_axis=0, tiled=True)
    expert_out = call(down_kernel, [sds((32 * SLOTS, width_pair), bf16)], count=2)(
        hidden_all, w_down
    )
    returned = lax.all_to_all(
        expert_out.reshape(32, SLOTS, width_pair), EXP, split_axis=0, concat_axis=0, tiled=True
    ).reshape(32 * SLOTS, width_pair)
    mix_keep, mix_send = call(
        combine_kernel, [sds((128, width_out), f32), sds((128, width_out), bf16)], count=2
    )(weighting, returned)
    mix_got = lax.ppermute(mix_send, "xl", SWAP)
    stream_rb = jnp.dot(
        back_order.astype(bf16),
        split[:, width_pair : width_pair + width_out],
        preferred_element_type=f32,
    )
    result = (stream_rb + mix_keep + mix_got.astype(f32)).astype(bf16)
    return result.reshape(8, 16, width_out)


def solution(mesh):
    grid = Mesh(mesh.devices.reshape(8, 2, 8, 2, 2), ("y", "xl", "z", "xh", "core"))
    return jax.shard_map(
        on_device,
        mesh=grid,
        in_specs=(
            P(CTX, EXP, None),
            P(CTX, None),
            P(CTX),
            P(EXP, None, None),
            P(EXP, None),
            P(CTX + EXP, None),
            P(),
            P(EXP, None, None),
            P(EXP, None, None),
            P(EXP, CTX, None),
            P(EXP, CTX, None),
            P(EXP, None, CTX),
        ),
        out_specs=P(EXP, None, CTX),
        check_vma=False,
    )
```

```python
import jax
import jax.numpy as jnp
from jax import lax
from jax.experimental import pallas as pl
from jax.experimental.pallas import tpu as pltpu
from jax.sharding import Mesh, PartitionSpec as P

LATENT = 512
VDIM = 128
QKDIM = 192
EXPERTS = 96
TOPK = 6
CAP = 10
SLOTS = 32
SEGMENTS = 8
KEYW = 640
FAR = float(2**20)

CTX = ("y", "xl")
EXP = ("z", "xh", "core")
SWAP = [(0, 1), (1, 0)]
BIG_VMEM = pltpu.CompilerParams(vmem_limit_bytes=44 * 2**20)
f32, bf16, i32 = jnp.float32, jnp.bfloat16, jnp.int32


def nt_dot(a, b):
    return lax.dot_general(a, b, (((1,), (1,)), ((), ())), preferred_element_type=f32)


def attend_chunks(rows, chunks, biases, scores, old):
    scale = QKDIM ** (-0.5)
    peak = jnp.full((256, 128), -FAR, f32) if old is None else old[0]
    for n, (chunk, bias) in enumerate(zip(chunks, biases)):
        part = bias(nt_dot(rows, chunk[...].reshape(256, KEYW)) * scale)
        scores[:, n * 256 : (n + 1) * 256] = part
        peak = jnp.maximum(peak, jnp.maximum(part[:, :128], part[:, 128:]))
    peak = jnp.max(peak, axis=1, keepdims=True)
    if old is None:
        sums, mixed = jnp.zeros((256, 128), f32), jnp.zeros((256, LATENT), f32)
    else:
        factor = jnp.exp(old[0][:, :1] - peak)
        sums, mixed = old[1] * factor, old[2] * factor
    for n, chunk in enumerate(chunks):
        terms = jnp.exp(scores[:, n * 256 : (n + 1) * 256] - peak)
        sums = sums + terms[:, :128] + terms[:, 128:]
        keys = chunk[...].reshape(256, KEYW)
        mixed = mixed + jnp.dot(terms.astype(bf16), keys[:, :LATENT], preferred_element_type=f32)
    return jnp.broadcast_to(peak, (256, 128)), sums, mixed


def valid_bias(info, piece):
    def bias(part):
        lane = lax.broadcasted_iota(i32, (256, 256), 1)
        first = jnp.where(info[2 * piece] >= 0, 0.0, -FAR)
        second = jnp.where(info[2 * piece + 1] >= 0, 0.0, -FAR)
        return part + jnp.where(lane < 128, first, second)

    return bias


def causal_bias(part):
    lane = lax.broadcasted_iota(i32, (256, 256), 1)
    row = lax.broadcasted_iota(i32, (256, 256), 0)
    token = (row % 128) // 8 * 16 + row // 128 * 8 + row % 8
    return jnp.where(lane <= token, part, -FAR)


def first_attention_kernel(info, query, own, p0, peak, sums, mixed, scores):
    @pl.loop(0, 2)
    def _(head):
        state = attend_chunks(
            query[head], [own, p0], [causal_bias, valid_bias(info, 0)], scores, None
        )
        peak[head], sums[head], mixed[head] = state


def second_attention_kernel(
    info, query, p1, p2, p3, o0, old_peak, old_sums, old_mixed, peak, sums, mixed, scores
):
    @pl.loop(0, 2)
    def _(head):
        old = old_peak[head], old_sums[head], old_mixed[head]
        biases = [valid_bias(info, n) for n in (1, 2, 3, 0)]
        state = attend_chunks(query[head], [p1, p2, p3, o0], biases, scores, old)
        peak[head], sums[head], mixed[head] = state


def last_attention_kernel(
    info, query, others, old_peak, old_sums, old_mixed, value_up, send, keep, scores, values
):
    core = info[8]

    @pl.loop(0, 2)
    def _(head):
        old = old_peak[head], old_sums[head], old_mixed[head]
        chunks = [others.at[2 * n : 2 * n + 2] for n in range(3)]
        biases = [valid_bias(info, n) for n in (1, 2, 3)]
        _, sums, mixed = attend_chunks(query[head], chunks, biases, scores, old)
        mixed = (mixed / jnp.sum(sums, axis=1, keepdims=True)).astype(bf16)
        values[head] = jnp.dot(mixed, value_up[head], preferred_element_type=f32).astype(bf16)

    for which, out in ((1 - core, send), (core, keep)):
        start = pl.multiple_of(which * 128, 128)
        for head in range(2):
            out[:, head * VDIM : (head + 1) * VDIM] = values[head, pl.ds(start, 128), :]


def project_kernel(own, got, proj_own, proj_got, out):
    chips, rows, width = out.shape
    for c in range(0, width, 640):
        total = jnp.dot(own[...], proj_own[:, c : c + 640], preferred_element_type=f32)
        total = total + jnp.dot(got[...], proj_got[:, c : c + 640], preferred_element_type=f32)
        out[:, :, c : c + 640] = total.reshape(chips, rows, 640).astype(bf16)


def gather_kernel(p1, p2, p3, out):
    for n, piece in enumerate((p1, p2, p3)):
        out[2 * n : 2 * n + 2] = piece[...]


def norm_kernel(spread, residual, gain, packed):
    attended = jnp.sum(spread[...].astype(f32), axis=0)
    stream = (residual[...].astype(f32) + attended).astype(bf16).astype(f32)
    mean_sq = jnp.mean(stream * stream, axis=1, keepdims=True)
    normed = (stream * lax.rsqrt(mean_sq + 1e-06) * gain[...]).astype(bf16).astype(f32)
    width = stream.shape[1] // 16
    fill = jnp.zeros((stream.shape[0], packed.shape[2] - 3 * width), f32)
    for c in range(16):
        mine, other = c * width, (c ^ 1) * width
        packed[c] = jnp.concatenate(
            [
                normed[:, mine : mine + width],
                normed[:, other : other + width],
                stream[:, mine : mine + width],
                fill,
            ],
            axis=1,
        ).astype(bf16)


def store_packed(out, n, rows):
    left = lax.broadcasted_iota(i32, (SLOTS // 2, 128), 1) < 64
    out[n, 0:32] = rows[:, :128].astype(bf16)
    out[n, 32:64] = rows[:, 128:256].astype(bf16)
    out[n, 64:80] = jnp.where(left, rows[:16, 256:], rows[16:, 256:]).astype(bf16)


def load_packed(ref, n):
    last = ref[n, 64:80]
    left = jnp.where(lax.broadcasted_iota(i32, (1, 128), 1) < 64, 1.0, 0.0).astype(bf16)
    last = jnp.concatenate([last * left, last * (1 - left)], axis=0)
    return jnp.concatenate([ref[n, 0:32], ref[n, 32:64], last], axis=1)


def pick_kernel(picker, split, out):
    values = split[:, :384]
    doubled = jnp.concatenate([values[:, :320], values[:, 256:320]], axis=1)
    for r in range(0, picker.shape[0], 256):
        rows = jnp.dot(picker[r : r + 256, :], doubled, preferred_element_type=f32)
        for n in range(256 // SLOTS):
            store_packed(out, r // SLOTS + n, rows[n * SLOTS : (n + 1) * SLOTS])


def row_mask(count, j):
    slot = lax.broadcasted_iota(i32, (count, 1), 0) % SLOTS
    return jnp.where((slot >= j * CAP) & (slot < (j + 1) * CAP), 1.0, 0.0).astype(bf16)


def spread_experts(rows, masks):
    return jnp.concatenate([rows * mask for mask in masks], axis=1)


def gate_up_kernel(received, weights, pre):
    masks = [row_mask(256, j) for j in range(3)]
    for r in range(0, received.shape[0], 8):
        rows = jnp.concatenate([load_packed(received, r + n) for n in range(8)], axis=0)
        total = jnp.dot(spread_experts(rows, masks), weights[...], preferred_element_type=f32)
        pre[r * SLOTS : (r + 8) * SLOTS, :] = total.astype(bf16)


def hidden_kernel(parts, out):
    total = jnp.sum(parts[...].astype(f32), axis=0)
    half = total.shape[1] // 2
    gate, up = total[:, :half], total[:, half:]
    hidden = (gate / (1.0 + jnp.exp(-gate)) * up).astype(bf16)
    for n in range(out.shape[0]):
        out[n] = hidden


def down_kernel(hidden, weights, out):
    masks = [row_mask(256, j) for j in range(3)]
    for r in range(0, hidden.shape[0], 256):
        rows = spread_experts(hidden[r : r + 256, :], masks)
        total = nt_dot(rows, weights[...])
        for n in range(256 // SLOTS):
            store_packed(out, r // SLOTS + n, total[n * SLOTS : (n + 1) * SLOTS])


def combine_kernel(weighting, returned, keep, send):
    width = keep.shape[1]
    rows = jnp.concatenate([load_packed(returned, n) for n in range(returned.shape[0])], axis=0)
    top = weighting[...].astype(bf16)
    rest = (weighting[...] - top.astype(f32)).astype(bf16)
    mixture = jnp.dot(top, rows, preferred_element_type=f32) + jnp.dot(
        rest, rows, preferred_element_type=f32
    )
    tail = mixture[:, 256:320] + mixture[:, 320:384]
    keep[...] = mixture[:, :width]
    send[...] = jnp.concatenate([mixture[:, width:256], tail], axis=1).astype(bf16)


def call(kernel, outs, scratch=(), smem_first=False, count=0):
    specs = [pl.BlockSpec(memory_space=pltpu.VMEM)] * count
    if smem_first:
        specs[0] = pl.BlockSpec(memory_space=pltpu.SMEM)
    out_specs = [pl.BlockSpec(memory_space=pltpu.VMEM)] * len(outs)
    single = len(outs) == 1
    return pl.pallas_call(
        kernel,
        in_specs=specs,
        out_specs=out_specs[0] if single else out_specs,
        out_shape=outs[0] if single else outs,
        scratch_shapes=list(scratch),
        compiler_params=BIG_VMEM,
    )


def sds(shape, dtype):
    return jax.ShapeDtypeStruct(shape, dtype)


def on_device(
    queries,
    latent,
    segment_ids,
    value_up,
    out_proj,
    residual,
    norm_gain,
    route_ids,
    route_gates,
    expert_gate,
    expert_up,
    expert_down,
):
    block_len, local_heads, width_key = queries.shape
    width_model = residual.shape[1]
    width_out = width_model // 16
    width_pair = 2 * width_out
    ff = expert_gate.shape[2]
    ff_half = ff // 2
    y, xl, xh, core = (lax.axis_index(a) for a in ("y", "xl", "xh", "core"))
    half = block_len // 2

    segment_axis = jnp.arange(SEGMENTS, dtype=i32)
    own_segment = segment_ids[:, None] == segment_axis[None, :]
    pad = KEYW - width_key - SEGMENTS
    keys_own = jnp.concatenate(
        [latent, own_segment.astype(bf16), jnp.zeros((block_len, pad), bf16)], axis=1
    )
    mine = lax.dynamic_slice_in_dim(keys_own, core * half, half, 0)

    def along_y(near, far):
        pairs = [
            (2 * i + h, 2 * ((i + (near, far)[h]) % 8) + h) for i in range(8) for h in range(2)
        ]
        return lax.ppermute(mine, ("y", "xh"), pairs)

    column = jnp.stack([along_y(1, 2), along_y(3, 4)])
    to_other = jnp.where(
        (xl == 0) & (xh == 1), jnp.stack([mine, column[0]]), column
    )
    diagonal = [(0, 3), (1, 2), (2, 1), (3, 0)]
    pieces = [
        column,
        lax.ppermute(column, "xh", SWAP),
        lax.ppermute(to_other, "xl", SWAP),
        lax.ppermute(to_other, ("xl", "xh"), diagonal),
    ]

    def blocks_of(x, h):
        return [2 * (y - 1 - h) + x, 2 * (y - 3 - h) + x]

    def blocks_sent(x, h):
        near, far = blocks_of(x, h)
        odd = (x == 0) & (h == 1)
        return [jnp.where(odd, 2 * y, near), jnp.where(odd, near, far)]

    info = jnp.stack(
        blocks_of(xl, xh)
        + blocks_of(xl, 1 - xh)
        + blocks_sent(1 - xl, xh)
        + blocks_sent(1 - xl, 1 - xh)
        + [core]
    ).astype(i32)

    masks = jnp.where(own_segment, 0.0, -FAR).astype(bf16)
    query_rows = jnp.concatenate(
        [
            queries,
            jnp.broadcast_to(masks[:, None, :], (block_len, local_heads, SEGMENTS)),
            jnp.zeros((block_len, local_heads, pad), bf16),
        ],
        axis=2,
    )
    query_rows = query_rows.reshape(16, 2, 8, local_heads, KEYW).transpose(3, 1, 0, 2, 4)
    query_rows = query_rows.reshape(local_heads, block_len, KEYW)
    state_out = [
        sds((2, 256, 128), f32),
        sds((2, 256, 128), f32),
        sds((2, 256, LATENT), f32),
    ]
    state = call(
        first_attention_kernel, state_out, [pltpu.VMEM((256, 2 * 256), f32)], True, 4
    )(info, query_rows, keys_own, column)
    proj_got = lax.ppermute(out_proj, "core", SWAP)
    piece_x, peak, proj_got = lax.optimization_barrier((pieces[1], state[0], proj_got))
    pieces[1], state = piece_x, [peak] + list(state[1:])
    first_other = lax.ppermute(column, "core", SWAP)
    three = call(gather_kernel, [sds((6, half, KEYW), bf16)], count=3)(*pieces[1:])
    others = lax.ppermute(three, "core", SWAP)
    state = call(
        second_attention_kernel, state_out, [pltpu.VMEM((256, 4 * 256), f32)], True, 9
    )(info, query_rows, pieces[1], pieces[2], pieces[3], first_other, *state)
    values_out = sds((half, local_heads * VDIM), bf16)
    send, keep = call(
        last_attention_kernel,
        [values_out, values_out],
        [pltpu.VMEM((256, 3 * 256), f32), pltpu.VMEM((2, 256, VDIM), bf16)],
        True,
        7,
    )(info, query_rows, others, *state, value_up)
    got = lax.ppermute(send, "core", SWAP)
    pair_sum = call(project_kernel, [sds((16, 8, width_model), bf16)], count=4)(
        keep, got, out_proj, proj_got
    )

    weights = [expert_gate, expert_up, jnp.transpose(expert_down, (0, 2, 1))]
    low = jnp.concatenate([w[:, :, :ff_half] for w in weights], axis=2)
    high = jnp.concatenate([w[:, :, ff_half:] for w in weights], axis=2)
    w_send = jnp.where(xl == 0, high, low)
    w_keep = jnp.where(xl == 0, low, high)
    pair_sum, w_send = lax.optimization_barrier((pair_sum, w_send))
    w_got = lax.ppermute(w_send, "xl", SWAP)

    spread = lax.all_to_all(pair_sum, ("z", "xh"), split_axis=0, concat_axis=0, tiled=True)
    packed = call(norm_kernel, [sds((16, 8, 512), bf16)], count=3)(
        spread, residual, norm_gain[None, :]
    )
    split = lax.all_to_all(packed, CTX, split_axis=0, concat_axis=0, tiled=True)
    split, w_got = lax.optimization_barrier((split, w_got))
    split = split.reshape(128, 512)
    w_both = jnp.concatenate([w_keep, w_got], axis=1)
    w_both = jnp.concatenate([w_both, w_both[:, 256:width_pair]], axis=1)
    w_in = w_both[:, :, : 2 * ff_half].reshape(3 * 384, 2 * ff_half)
    w_down = jnp.transpose(w_both[:, :, 2 * ff_half :], (1, 0, 2)).reshape(384, 3 * ff_half)

    routes = jnp.transpose(route_ids, (1, 0, 2)).reshape(128, TOPK)
    expert_axis = jnp.arange(EXPERTS, dtype=i32)
    named = jnp.any(routes[:, :, None] == expert_axis[None, None, :], axis=1)
    earlier_tokens = jnp.tril(jnp.ones((128, 128), bf16), -1)
    slot_all = jnp.dot(earlier_tokens, named.astype(bf16), preferred_element_type=f32).astype(i32)
    slot_of = jnp.sum(
        jnp.where(routes[:, :, None] == expert_axis[None, None, :], slot_all[:, None, :], 0), axis=2
    )
    target = (routes // 3) * SLOTS + (routes % 3) * CAP + slot_of
    slot_axis = jnp.arange(32 * SLOTS, dtype=i32)
    picker = jnp.any(target.T[None, :, :] == slot_axis[:, None, None], axis=1).astype(bf16)
    order = jnp.arange(128, dtype=i32)
    back_order = ((order % 16) * 8 + order // 16)[:, None] == order[None, :]
    target_rb = jnp.transpose(target.reshape(16, 8, TOPK), (1, 0, 2)).reshape(128, TOPK)
    gates_rb = route_gates.reshape(128, TOPK)
    weighting = jnp.sum(
        jnp.where(target_rb[:, :, None] == slot_axis[None, None, :], gates_rb[:, :, None], 0.0),
        axis=1,
    )

    travel = sds((32, 80, 128), bf16)
    outgoing = call(pick_kernel, [travel], count=2)(picker, split)
    received = lax.all_to_all(outgoing, EXP, split_axis=0, concat_axis=0, tiled=True)
    pre = call(gate_up_kernel, [sds((32 * SLOTS, 2 * ff_half), bf16)], count=2)(received, w_in)
    pre_parts = lax.all_to_all(
        pre.reshape(8, 128, 2 * ff_half), "y", split_axis=0, concat_axis=0, tiled=True
    )
    hidden = call(hidden_kernel, [sds((8, 128, ff_half), bf16)], count=1)(pre_parts)
    hidden_all = lax.all_to_all(hidden, "y", split_axis=0, concat_axis=0, tiled=True)
    expert_out = call(down_kernel, [travel], count=2)(
        hidden_all.reshape(32 * SLOTS, ff_half), w_down
    )
    returned = lax.all_to_all(expert_out, EXP, split_axis=0, concat_axis=0, tiled=True)
    mix_keep, mix_send = call(
        combine_kernel, [sds((128, width_out), f32), sds((128, width_out), bf16)], count=2
    )(weighting, returned)
    mix_got = lax.ppermute(mix_send, "xl", SWAP)
    stream_rb = jnp.dot(
        back_order.astype(bf16),
        split[:, width_pair : width_pair + width_out],
        preferred_element_type=f32,
    )
    result = (stream_rb + mix_keep + mix_got.astype(f32)).astype(bf16)
    return result.reshape(8, 16, width_out)


def solution(mesh):
    grid = Mesh(mesh.devices.reshape(8, 2, 8, 2, 2), ("y", "xl", "z", "xh", "core"))
    return jax.shard_map(
        on_device,
        mesh=grid,
        in_specs=(
            P(CTX, EXP, None),
            P(CTX, None),
            P(CTX),
            P(EXP, None, None),
            P(EXP, None),
            P(CTX + EXP, None),
            P(),
            P(EXP, None, None),
            P(EXP, None, None),
            P(EXP, CTX, None),
            P(EXP, CTX, None),
            P(EXP, None, CTX),
        ),
        out_specs=P(EXP, None, CTX),
        check_vma=False,
    )
```

```python
import jax
import jax.numpy as jnp
from jax import lax
from jax.experimental import pallas as pl
from jax.experimental.pallas import tpu as pltpu
from jax.sharding import Mesh, PartitionSpec as P

LATENT = 512
VDIM = 128
QKDIM = 192
EXPERTS = 96
TOPK = 6
CAP = 10
SLOTS = 32
SEGMENTS = 8
KEYW = 640
FAR = float(2**20)

CTX = ("y", "xl")
EXP = ("z", "xh", "core")
SWAP = [(0, 1), (1, 0)]
BIG_VMEM = pltpu.CompilerParams(vmem_limit_bytes=20 * 2**20)
f32, bf16, i32 = jnp.float32, jnp.bfloat16, jnp.int32


def nt_dot(a, b):
    return lax.dot_general(a, b, (((1,), (1,)), ((), ())), preferred_element_type=f32)


def attend_chunks(rows, chunks, biases, scores, old):
    scale = QKDIM ** (-0.5)
    peak = jnp.full((256, 128), -FAR, f32) if old is None else old[0]
    for n, (chunk, bias) in enumerate(zip(chunks, biases)):
        part = bias(nt_dot(rows, chunk[...].reshape(256, KEYW)) * scale)
        scores[:, n * 256 : (n + 1) * 256] = part
        peak = jnp.maximum(peak, jnp.maximum(part[:, :128], part[:, 128:]))
    peak = jnp.max(peak, axis=1, keepdims=True)
    if old is None:
        sums, mixed = jnp.zeros((256, 128), f32), jnp.zeros((256, LATENT), f32)
    else:
        factor = jnp.exp(old[0][:, :1] - peak)
        sums, mixed = old[1] * factor, old[2] * factor
    for n, chunk in enumerate(chunks):
        terms = jnp.exp(scores[:, n * 256 : (n + 1) * 256] - peak)
        sums = sums + terms[:, :128] + terms[:, 128:]
        keys = chunk[...].reshape(256, KEYW)
        mixed = mixed + jnp.dot(terms.astype(bf16), keys[:, :LATENT], preferred_element_type=f32)
    return jnp.broadcast_to(peak, (256, 128)), sums, mixed


def valid_bias(info, piece):
    def bias(part):
        lane = lax.broadcasted_iota(i32, (256, 256), 1)
        first = jnp.where(info[2 * piece] >= 0, 0.0, -FAR)
        second = jnp.where(info[2 * piece + 1] >= 0, 0.0, -FAR)
        return part + jnp.where(lane < 128, first, second)

    return bias


def causal_bias(part):
    lane = lax.broadcasted_iota(i32, (256, 256), 1)
    row = lax.broadcasted_iota(i32, (256, 256), 0)
    token = (row % 128) // 8 * 16 + row // 128 * 8 + row % 8
    return jnp.where(lane <= token, part, -FAR)


def first_attention_kernel(info, query, own, p0, peak, sums, mixed, scores):
    @pl.loop(0, 2)
    def _(head):
        state = attend_chunks(
            query[head], [own, p0], [causal_bias, valid_bias(info, 0)], scores, None
        )
        peak[head], sums[head], mixed[head] = state


def second_attention_kernel(
    info, query, p1, p2, p3, o0, old_peak, old_sums, old_mixed, peak, sums, mixed, scores
):
    @pl.loop(0, 2)
    def _(head):
        old = old_peak[head], old_sums[head], old_mixed[head]
        biases = [valid_bias(info, n) for n in (1, 2, 3, 0)]
        state = attend_chunks(query[head], [p1, p2, p3, o0], biases, scores, old)
        peak[head], sums[head], mixed[head] = state


def last_attention_kernel(
    info, query, others, old_peak, old_sums, old_mixed, value_up, send, keep, scores, values
):
    core = info[8]

    @pl.loop(0, 2)
    def _(head):
        old = old_peak[head], old_sums[head], old_mixed[head]
        chunks = [others.at[2 * n : 2 * n + 2] for n in range(3)]
        biases = [valid_bias(info, n) for n in (1, 2, 3)]
        _, sums, mixed = attend_chunks(query[head], chunks, biases, scores, old)
        mixed = (mixed / jnp.sum(sums, axis=1, keepdims=True)).astype(bf16)
        values[head] = jnp.dot(mixed, value_up[head], preferred_element_type=f32).astype(bf16)

    for which, out in ((1 - core, send), (core, keep)):
        start = pl.multiple_of(which * 128, 128)
        for head in range(2):
            out[:, head * VDIM : (head + 1) * VDIM] = values[head, pl.ds(start, 128), :]


def project_kernel(own, got, proj_own, proj_got, out):
    chips, rows, width = out.shape
    for c in range(0, width, 640):
        total = jnp.dot(own[...], proj_own[:, c : c + 640], preferred_element_type=f32)
        total = total + jnp.dot(got[...], proj_got[:, c : c + 640], preferred_element_type=f32)
        out[:, :, c : c + 640] = total.reshape(chips, rows, 640).astype(bf16)


def gather_kernel(p1, p2, p3, out):
    for n, piece in enumerate((p1, p2, p3)):
        out[2 * n : 2 * n + 2] = piece[...]


def norm_kernel(spread, residual, gain, packed):
    attended = jnp.sum(spread[...].astype(f32), axis=0)
    stream = (residual[...].astype(f32) + attended).astype(bf16).astype(f32)
    mean_sq = jnp.mean(stream * stream, axis=1, keepdims=True)
    normed = (stream * lax.rsqrt(mean_sq + 1e-06) * gain[...]).astype(bf16).astype(f32)
    width = stream.shape[1] // 16
    fill = jnp.zeros((stream.shape[0], packed.shape[2] - 3 * width), f32)
    for c in range(16):
        mine, other = c * width, (c ^ 1) * width
        packed[c] = jnp.concatenate(
            [
                normed[:, mine : mine + width],
                normed[:, other : other + width],
                stream[:, mine : mine + width],
                fill,
            ],
            axis=1,
        ).astype(bf16)


def store_packed(out, n, rows):
    left = lax.broadcasted_iota(i32, (SLOTS // 2, 128), 1) < 64
    out[n, 0:32] = rows[:, :128].astype(bf16)
    out[n, 32:64] = rows[:, 128:256].astype(bf16)
    out[n, 64:80] = jnp.where(left, rows[:16, 256:], rows[16:, 256:]).astype(bf16)


def load_packed(ref, n):
    last = ref[n, 64:80]
    left = jnp.where(lax.broadcasted_iota(i32, (1, 128), 1) < 64, 1.0, 0.0).astype(bf16)
    last = jnp.concatenate([last * left, last * (1 - left)], axis=0)
    return jnp.concatenate([ref[n, 0:32], ref[n, 32:64], last], axis=1)


def pick_kernel(picker, split, out):
    values = split[:, :384]
    doubled = jnp.concatenate([values[:, :320], values[:, 256:320]], axis=1)
    for r in range(0, picker.shape[0], 256):
        rows = jnp.dot(picker[r : r + 256, :], doubled, preferred_element_type=f32)
        for n in range(256 // SLOTS):
            store_packed(out, r // SLOTS + n, rows[n * SLOTS : (n + 1) * SLOTS])


def row_mask(count, j):
    slot = lax.broadcasted_iota(i32, (count, 1), 0) % SLOTS
    return jnp.where((slot >= j * CAP) & (slot < (j + 1) * CAP), 1.0, 0.0).astype(bf16)


def spread_experts(rows, masks):
    return jnp.concatenate([rows * mask for mask in masks], axis=1)


def split_weights_kernel(info, gate, up, down, send, keep):
    half = gate.shape[2] // 2

    def move(out, start):
        for n, weights in enumerate((gate, up, down)):
            out[:, :, n * half : (n + 1) * half] = weights[:, :, start : start + half]

    @pl.when(info[9] == 0)
    def _():
        move(keep, 0)
        move(send, half)

    @pl.when(info[9] != 0)
    def _():
        move(keep, half)
        move(send, 0)


def join_weights_kernel(keep, got, into, down):
    rows = keep.shape[1]
    wide = into.shape[1]
    narrow = keep.shape[2] - wide
    for j in range(3):
        base = j * 384
        into[base : base + rows, :] = keep[j, :, :wide]
        into[base + rows : base + 2 * rows, :] = got[j, :, :wide]
        into[base + 2 * rows : base + 384, :] = got[j, 256 - rows :, :wide]
        lanes = slice(j * narrow, (j + 1) * narrow)
        down[:rows, lanes] = keep[j, :, wide:]
        down[rows : 2 * rows, lanes] = got[j, :, wide:]
        down[2 * rows :, lanes] = got[j, 256 - rows :, wide:]


def gate_up_kernel(received, weights, pre):
    masks = [row_mask(256, j) for j in range(3)]
    for r in range(0, received.shape[0], 8):
        rows = jnp.concatenate([load_packed(received, r + n) for n in range(8)], axis=0)
        total = jnp.dot(spread_experts(rows, masks), weights[...], preferred_element_type=f32)
        pre[r * SLOTS : (r + 8) * SLOTS, :] = total.astype(bf16)


def hidden_kernel(parts, out):
    total = jnp.sum(parts[...].astype(f32), axis=0)
    half = total.shape[1] // 2
    gate, up = total[:, :half], total[:, half:]
    hidden = (gate / (1.0 + jnp.exp(-gate)) * up).astype(bf16)
    for n in range(out.shape[0]):
        out[n] = hidden


def down_kernel(hidden, weights, out):
    masks = [row_mask(256, j) for j in range(3)]
    for r in range(0, hidden.shape[0], 256):
        rows = spread_experts(hidden[r : r + 256, :], masks)
        total = nt_dot(rows, weights[...])
        for n in range(256 // SLOTS):
            store_packed(out, r // SLOTS + n, total[n * SLOTS : (n + 1) * SLOTS])


def combine_kernel(weighting, returned, keep, send):
    width = keep.shape[1]
    rows = jnp.concatenate([load_packed(returned, n) for n in range(returned.shape[0])], axis=0)
    top = weighting[...].astype(bf16)
    rest = (weighting[...] - top.astype(f32)).astype(bf16)
    mixture = jnp.dot(top, rows, preferred_element_type=f32) + jnp.dot(
        rest, rows, preferred_element_type=f32
    )
    tail = mixture[:, 256:320] + mixture[:, 320:384]
    keep[...] = mixture[:, :width]
    send[...] = jnp.concatenate([mixture[:, width:256], tail], axis=1).astype(bf16)


def call(kernel, outs, scratch=(), smem_first=False, count=0):
    specs = [pl.BlockSpec(memory_space=pltpu.VMEM)] * count
    if smem_first:
        specs[0] = pl.BlockSpec(memory_space=pltpu.SMEM)
    out_specs = [pl.BlockSpec(memory_space=pltpu.VMEM)] * len(outs)
    single = len(outs) == 1
    return pl.pallas_call(
        kernel,
        in_specs=specs,
        out_specs=out_specs[0] if single else out_specs,
        out_shape=outs[0] if single else outs,
        scratch_shapes=list(scratch),
        compiler_params=BIG_VMEM,
    )


def sds(shape, dtype):
    return jax.ShapeDtypeStruct(shape, dtype)


def on_device(
    queries,
    latent,
    segment_ids,
    value_up,
    out_proj,
    residual,
    norm_gain,
    route_ids,
    route_gates,
    expert_gate,
    expert_up,
    expert_down,
):
    block_len, local_heads, width_key = queries.shape
    width_model = residual.shape[1]
    width_out = width_model // 16
    width_pair = 2 * width_out
    ff = expert_gate.shape[2]
    ff_half = ff // 2
    y, xl, xh, core = (lax.axis_index(a) for a in ("y", "xl", "xh", "core"))
    half = block_len // 2

    segment_axis = jnp.arange(SEGMENTS, dtype=i32)
    own_segment = segment_ids[:, None] == segment_axis[None, :]
    pad = KEYW - width_key - SEGMENTS
    keys_own = jnp.concatenate(
        [latent, own_segment.astype(bf16), jnp.zeros((block_len, pad), bf16)], axis=1
    )
    mine = lax.dynamic_slice_in_dim(keys_own, core * half, half, 0)

    def along_y(near, far):
        pairs = [
            (2 * i + h, 2 * ((i + (near, far)[h]) % 8) + h) for i in range(8) for h in range(2)
        ]
        return lax.ppermute(mine, ("y", "xh"), pairs)

    column = jnp.stack([along_y(1, 2), along_y(3, 4)])
    to_other = jnp.where(
        (xl == 0) & (xh == 1), jnp.stack([mine, column[0]]), column
    )
    diagonal = [(0, 3), (1, 2), (2, 1), (3, 0)]
    pieces = [
        column,
        lax.ppermute(column, "xh", SWAP),
        lax.ppermute(to_other, "xl", SWAP),
        lax.ppermute(to_other, ("xl", "xh"), diagonal),
    ]

    def blocks_of(x, h):
        return [2 * (y - 1 - h) + x, 2 * (y - 3 - h) + x]

    def blocks_sent(x, h):
        near, far = blocks_of(x, h)
        odd = (x == 0) & (h == 1)
        return [jnp.where(odd, 2 * y, near), jnp.where(odd, near, far)]

    info = jnp.stack(
        blocks_of(xl, xh)
        + blocks_of(xl, 1 - xh)
        + blocks_sent(1 - xl, xh)
        + blocks_sent(1 - xl, 1 - xh)
        + [core, xl]
    ).astype(i32)

    masks = jnp.where(own_segment, 0.0, -FAR).astype(bf16)
    query_rows = jnp.concatenate(
        [
            queries,
            jnp.broadcast_to(masks[:, None, :], (block_len, local_heads, SEGMENTS)),
            jnp.zeros((block_len, local_heads, pad), bf16),
        ],
        axis=2,
    )
    query_rows = query_rows.reshape(16, 2, 8, local_heads, KEYW).transpose(3, 1, 0, 2, 4)
    query_rows = query_rows.reshape(local_heads, block_len, KEYW)
    state_out = [
        sds((2, 256, 128), f32),
        sds((2, 256, 128), f32),
        sds((2, 256, LATENT), f32),
    ]
    state = call(
        first_attention_kernel, state_out, [pltpu.VMEM((256, 2 * 256), f32)], True, 4
    )(info, query_rows, keys_own, column)
    piece_x, peak = lax.optimization_barrier((pieces[1], state[0]))
    pieces[1], state = piece_x, [peak] + list(state[1:])
    peak, proj_send = lax.optimization_barrier((state[0], out_proj))
    state = [peak] + list(state[1:])
    first_other = lax.ppermute(column, "core", SWAP)
    proj_got = lax.ppermute(proj_send, "core", SWAP)
    pieces[2], proj_got = lax.optimization_barrier((pieces[2], proj_got))
    three = call(gather_kernel, [sds((6, half, KEYW), bf16)], count=3)(*pieces[1:])
    others = lax.ppermute(three, "core", SWAP)
    state = call(
        second_attention_kernel, state_out, [pltpu.VMEM((256, 4 * 256), f32)], True, 9
    )(info, query_rows, pieces[1], pieces[2], pieces[3], first_other, *state)
    values_out = sds((half, local_heads * VDIM), bf16)
    send, keep = call(
        last_attention_kernel,
        [values_out, values_out],
        [pltpu.VMEM((256, 3 * 256), f32), pltpu.VMEM((2, 256, VDIM), bf16)],
        True,
        7,
    )(info, query_rows, others, *state, value_up)
    got = lax.ppermute(send, "core", SWAP)
    pair_sum = call(project_kernel, [sds((16, 8, width_model), bf16)], count=4)(
        keep, got, out_proj, proj_got
    )

    weights_out = sds((3, width_out, 3 * ff_half), bf16)
    w_send, w_keep = call(split_weights_kernel, [weights_out, weights_out], (), True, 4)(
        info, expert_gate, expert_up, jnp.transpose(expert_down, (0, 2, 1))
    )
    pair_sum, w_send = lax.optimization_barrier((pair_sum, w_send))
    w_got = lax.ppermute(w_send, "xl", SWAP)

    spread = lax.all_to_all(pair_sum, ("z", "xh"), split_axis=0, concat_axis=0, tiled=True)
    packed = call(norm_kernel, [sds((16, 8, 512), bf16)], count=3)(
        spread, residual, norm_gain[None, :]
    )
    split = lax.all_to_all(packed, CTX, split_axis=0, concat_axis=0, tiled=True)
    split, w_got = lax.optimization_barrier((split, w_got))
    split = split.reshape(128, 512)
    w_in, w_down = call(
        join_weights_kernel,
        [sds((3 * 384, 2 * ff_half), bf16), sds((384, 3 * ff_half), bf16)],
        count=2,
    )(w_keep, w_got)

    routes = jnp.transpose(route_ids, (1, 0, 2)).reshape(128, TOPK)
    expert_axis = jnp.arange(EXPERTS, dtype=i32)
    named = jnp.any(routes[:, :, None] == expert_axis[None, None, :], axis=1)
    earlier_tokens = jnp.tril(jnp.ones((128, 128), bf16), -1)
    slot_all = jnp.dot(earlier_tokens, named.astype(bf16), preferred_element_type=f32).astype(i32)
    slot_of = jnp.sum(
        jnp.where(routes[:, :, None] == expert_axis[None, None, :], slot_all[:, None, :], 0), axis=2
    )
    target = (routes // 3) * SLOTS + (routes % 3) * CAP + slot_of
    slot_axis = jnp.arange(32 * SLOTS, dtype=i32)
    picker = jnp.any(target.T[None, :, :] == slot_axis[:, None, None], axis=1).astype(bf16)
    order = jnp.arange(128, dtype=i32)
    back_order = ((order % 16) * 8 + order // 16)[:, None] == order[None, :]
    target_rb = jnp.transpose(target.reshape(16, 8, TOPK), (1, 0, 2)).reshape(128, TOPK)
    gates_rb = route_gates.reshape(128, TOPK)
    weighting = jnp.sum(
        jnp.where(target_rb[:, :, None] == slot_axis[None, None, :], gates_rb[:, :, None], 0.0),
        axis=1,
    )

    travel = sds((32, 80, 128), bf16)
    outgoing = call(pick_kernel, [travel], count=2)(picker, split)
    received = lax.all_to_all(outgoing, EXP, split_axis=0, concat_axis=0, tiled=True)
    pre = call(gate_up_kernel, [sds((32 * SLOTS, 2 * ff_half), bf16)], count=2)(received, w_in)
    pre_parts = lax.all_to_all(
        pre.reshape(8, 128, 2 * ff_half), "y", split_axis=0, concat_axis=0, tiled=True
    )
    hidden = call(hidden_kernel, [sds((8, 128, ff_half), bf16)], count=1)(pre_parts)
    hidden_all = lax.all_to_all(hidden, "y", split_axis=0, concat_axis=0, tiled=True)
    expert_out = call(down_kernel, [travel], count=2)(
        hidden_all.reshape(32 * SLOTS, ff_half), w_down
    )
    returned = lax.all_to_all(expert_out, EXP, split_axis=0, concat_axis=0, tiled=True)
    mix_keep, mix_send = call(
        combine_kernel, [sds((128, width_out), f32), sds((128, width_out), bf16)], count=2
    )(weighting, returned)
    mix_got = lax.ppermute(mix_send, "xl", SWAP)
    stream_rb = jnp.dot(
        back_order.astype(bf16),
        split[:, width_pair : width_pair + width_out],
        preferred_element_type=f32,
    )
    result = (stream_rb + mix_keep + mix_got.astype(f32)).astype(bf16)
    return result.reshape(8, 16, width_out)


def solution(mesh):
    grid = Mesh(mesh.devices.reshape(8, 2, 8, 2, 2), ("y", "xl", "z", "xh", "core"))
    return jax.shard_map(
        on_device,
        mesh=grid,
        in_specs=(
            P(CTX, EXP, None),
            P(CTX, None),
            P(CTX),
            P(EXP, None, None),
            P(EXP, None),
            P(CTX + EXP, None),
            P(),
            P(EXP, None, None),
            P(EXP, None, None),
            P(EXP, CTX, None),
            P(EXP, CTX, None),
            P(EXP, None, CTX),
        ),
        out_specs=P(EXP, None, CTX),
        check_vma=False,
    )
```

```python
import jax
import jax.numpy as jnp
from jax import lax
from jax.experimental import pallas as pl
from jax.experimental.pallas import tpu as pltpu
from jax.sharding import Mesh, PartitionSpec as P

LATENT = 512
VDIM = 128
QKDIM = 192
EXPERTS = 96
TOPK = 6
CAP = 10
SLOTS = 32
SEGMENTS = 8
KEYW = 640
FAR = float(2**20)

CTX = ("y", "xl")
EXP = ("z", "xh", "core")
SWAP = [(0, 1), (1, 0)]
BIG_VMEM = pltpu.CompilerParams(vmem_limit_bytes=20 * 2**20)
f32, bf16, i32 = jnp.float32, jnp.bfloat16, jnp.int32


def nt_dot(a, b):
    return lax.dot_general(a, b, (((1,), (1,)), ((), ())), preferred_element_type=f32)


def attend_chunks(rows, chunks, biases, scores, old):
    scale = QKDIM ** (-0.5)
    peak = jnp.full((256, 128), -FAR, f32) if old is None else old[0]
    for n, (chunk, bias) in enumerate(zip(chunks, biases)):
        part = bias(nt_dot(rows, chunk[...].reshape(256, KEYW)) * scale)
        scores[:, n * 256 : (n + 1) * 256] = part
        peak = jnp.maximum(peak, jnp.maximum(part[:, :128], part[:, 128:]))
    peak = jnp.max(peak, axis=1, keepdims=True)
    if old is None:
        sums, mixed = jnp.zeros((256, 128), f32), jnp.zeros((256, LATENT), f32)
    else:
        factor = jnp.exp(old[0][:, :1] - peak)
        sums, mixed = old[1] * factor, old[2] * factor
    for n, chunk in enumerate(chunks):
        terms = jnp.exp(scores[:, n * 256 : (n + 1) * 256] - peak)
        sums = sums + terms[:, :128] + terms[:, 128:]
        keys = chunk[...].reshape(256, KEYW)
        mixed = mixed + jnp.dot(terms.astype(bf16), keys[:, :LATENT], preferred_element_type=f32)
    return jnp.broadcast_to(peak, (256, 128)), sums, mixed


def valid_bias(info, piece):
    def bias(part):
        lane = lax.broadcasted_iota(i32, (256, 256), 1)
        first = jnp.where(info[2 * piece] >= 0, 0.0, -FAR)
        second = jnp.where(info[2 * piece + 1] >= 0, 0.0, -FAR)
        return part + jnp.where(lane < 128, first, second)

    return bias


def causal_bias(part):
    lane = lax.broadcasted_iota(i32, (256, 256), 1)
    row = lax.broadcasted_iota(i32, (256, 256), 0)
    token = (row % 128) // 8 * 16 + row // 128 * 8 + row % 8
    return jnp.where(lane <= token, part, -FAR)


def first_attention_kernel(info, query, own, p0, peak, sums, mixed, scores):
    @pl.loop(0, 2)
    def _(head):
        state = attend_chunks(
            query[head], [own, p0], [causal_bias, valid_bias(info, 0)], scores, None
        )
        peak[head], sums[head], mixed[head] = state


def second_attention_kernel(
    info, query, p1, p2, p3, o0, old_peak, old_sums, old_mixed, peak, sums, mixed, scores
):
    @pl.loop(0, 2)
    def _(head):
        old = old_peak[head], old_sums[head], old_mixed[head]
        biases = [valid_bias(info, n) for n in (1, 2, 3, 0)]
        state = attend_chunks(query[head], [p1, p2, p3, o0], biases, scores, old)
        peak[head], sums[head], mixed[head] = state


def last_attention_kernel(
    info, query, others, old_peak, old_sums, old_mixed, value_up, out_proj, send, keep, scores, values
):
    core = info[8]

    @pl.loop(0, 2)
    def _(head):
        old = old_peak[head], old_sums[head], old_mixed[head]
        chunks = [others.at[2 * n : 2 * n + 2] for n in range(3)]
        biases = [valid_bias(info, n) for n in (1, 2, 3)]
        _, sums, mixed = attend_chunks(query[head], chunks, biases, scores, old)
        mixed = (mixed / jnp.sum(sums, axis=1, keepdims=True)).astype(bf16)
        values[head] = jnp.dot(mixed, value_up[head], preferred_element_type=f32).astype(bf16)

    def project(which, out):
        start = pl.multiple_of(which * 128, 128)
        both = jnp.concatenate([values[head, pl.ds(start, 128), :] for head in range(2)], axis=1)
        for c in range(0, out.shape[1], 640):
            out[:, c : c + 640] = jnp.dot(
                both, out_proj[:, c : c + 640], preferred_element_type=f32
            ).astype(out.dtype)

    project(1 - core, send)
    project(core, keep)


def add_kernel(keep, got, out):
    out[...] = (keep[...] + got[...].astype(f32)).reshape(out.shape).astype(bf16)


def gather_kernel(p1, p2, p3, out):
    for n, piece in enumerate((p1, p2, p3)):
        out[2 * n : 2 * n + 2] = piece[...]


def norm_kernel(spread, residual, gain, packed):
    attended = jnp.sum(spread[...].astype(f32), axis=0)
    stream = (residual[...].astype(f32) + attended).astype(bf16).astype(f32)
    mean_sq = jnp.mean(stream * stream, axis=1, keepdims=True)
    normed = (stream * lax.rsqrt(mean_sq + 1e-06) * gain[...]).astype(bf16).astype(f32)
    width = stream.shape[1] // 16
    fill = jnp.zeros((stream.shape[0], packed.shape[2] - 3 * width), f32)
    for c in range(16):
        mine, other = c * width, (c ^ 1) * width
        packed[c] = jnp.concatenate(
            [
                normed[:, mine : mine + width],
                normed[:, other : other + width],
                stream[:, mine : mine + width],
                fill,
            ],
            axis=1,
        ).astype(bf16)


def store_packed(out, n, rows):
    left = lax.broadcasted_iota(i32, (SLOTS // 2, 128), 1) < 64
    out[n, 0:32] = rows[:, :128].astype(bf16)
    out[n, 32:64] = rows[:, 128:256].astype(bf16)
    out[n, 64:80] = jnp.where(left, rows[:16, 256:], rows[16:, 256:]).astype(bf16)


def load_packed(ref, n):
    last = ref[n, 64:80]
    left = jnp.where(lax.broadcasted_iota(i32, (1, 128), 1) < 64, 1.0, 0.0).astype(bf16)
    last = jnp.concatenate([last * left, last * (1 - left)], axis=0)
    return jnp.concatenate([ref[n, 0:32], ref[n, 32:64], last], axis=1)


def pick_kernel(picker, split, out):
    values = split[:, :384]
    doubled = jnp.concatenate([values[:, :320], values[:, 256:320]], axis=1)
    for r in range(0, picker.shape[0], 256):
        rows = jnp.dot(picker[r : r + 256, :], doubled, preferred_element_type=f32)
        for n in range(256 // SLOTS):
            store_packed(out, r // SLOTS + n, rows[n * SLOTS : (n + 1) * SLOTS])


def row_mask(count, j):
    slot = lax.broadcasted_iota(i32, (count, 1), 0) % SLOTS
    return jnp.where((slot >= j * CAP) & (slot < (j + 1) * CAP), 1.0, 0.0).astype(bf16)


def spread_experts(rows, masks):
    return jnp.concatenate([rows * mask for mask in masks], axis=1)


def split_weights_kernel(info, gate, up, down, send, keep):
    half = gate.shape[2] // 2

    def move(out, start):
        for n, weights in enumerate((gate, up, down)):
            out[:, :, n * half : (n + 1) * half] = weights[:, :, start : start + half]

    @pl.when(info[9] == 0)
    def _():
        move(keep, 0)
        move(send, half)

    @pl.when(info[9] != 0)
    def _():
        move(keep, half)
        move(send, 0)


def join_weights_kernel(keep, got, into, down):
    rows = keep.shape[1]
    wide = into.shape[1]
    narrow = keep.shape[2] - wide
    for j in range(3):
        base = j * 384
        into[base : base + rows, :] = keep[j, :, :wide]
        into[base + rows : base + 2 * rows, :] = got[j, :, :wide]
        into[base + 2 * rows : base + 384, :] = got[j, 256 - rows :, :wide]
        lanes = slice(j * narrow, (j + 1) * narrow)
        down[:rows, lanes] = keep[j, :, wide:]
        down[rows : 2 * rows, lanes] = got[j, :, wide:]
        down[2 * rows :, lanes] = got[j, 256 - rows :, wide:]


def gate_up_kernel(received, weights, pre):
    masks = [row_mask(256, j) for j in range(3)]
    for r in range(0, received.shape[0], 8):
        rows = jnp.concatenate([load_packed(received, r + n) for n in range(8)], axis=0)
        total = jnp.dot(spread_experts(rows, masks), weights[...], preferred_element_type=f32)
        pre[r * SLOTS : (r + 8) * SLOTS, :] = total.astype(bf16)


def hidden_kernel(parts, out):
    total = jnp.sum(parts[...].astype(f32), axis=0)
    half = total.shape[1] // 2
    gate, up = total[:, :half], total[:, half:]
    hidden = (gate / (1.0 + jnp.exp(-gate)) * up).astype(bf16)
    for n in range(out.shape[0]):
        out[n] = hidden


def down_kernel(hidden, weights, out):
    masks = [row_mask(256, j) for j in range(3)]
    for r in range(0, hidden.shape[0], 256):
        rows = spread_experts(hidden[r : r + 256, :], masks)
        total = nt_dot(rows, weights[...])
        for n in range(256 // SLOTS):
            store_packed(out, r // SLOTS + n, total[n * SLOTS : (n + 1) * SLOTS])


def combine_kernel(weighting, returned, keep, send):
    width = keep.shape[1]
    rows = jnp.concatenate([load_packed(returned, n) for n in range(returned.shape[0])], axis=0)
    top = weighting[...].astype(bf16)
    rest = (weighting[...] - top.astype(f32)).astype(bf16)
    mixture = jnp.dot(top, rows, preferred_element_type=f32) + jnp.dot(
        rest, rows, preferred_element_type=f32
    )
    tail = mixture[:, 256:320] + mixture[:, 320:384]
    keep[...] = mixture[:, :width]
    send[...] = jnp.concatenate([mixture[:, width:256], tail], axis=1).astype(bf16)


def call(kernel, outs, scratch=(), smem_first=False, count=0):
    specs = [pl.BlockSpec(memory_space=pltpu.VMEM)] * count
    if smem_first:
        specs[0] = pl.BlockSpec(memory_space=pltpu.SMEM)
    out_specs = [pl.BlockSpec(memory_space=pltpu.VMEM)] * len(outs)
    single = len(outs) == 1
    return pl.pallas_call(
        kernel,
        in_specs=specs,
        out_specs=out_specs[0] if single else out_specs,
        out_shape=outs[0] if single else outs,
        scratch_shapes=list(scratch),
        compiler_params=BIG_VMEM,
    )


def sds(shape, dtype):
    return jax.ShapeDtypeStruct(shape, dtype)


def on_device(
    queries,
    latent,
    segment_ids,
    value_up,
    out_proj,
    residual,
    norm_gain,
    route_ids,
    route_gates,
    expert_gate,
    expert_up,
    expert_down,
):
    block_len, local_heads, width_key = queries.shape
    width_model = residual.shape[1]
    width_out = width_model // 16
    width_pair = 2 * width_out
    ff = expert_gate.shape[2]
    ff_half = ff // 2
    y, xl, xh, core = (lax.axis_index(a) for a in ("y", "xl", "xh", "core"))
    half = block_len // 2

    segment_axis = jnp.arange(SEGMENTS, dtype=i32)
    own_segment = segment_ids[:, None] == segment_axis[None, :]
    pad = KEYW - width_key - SEGMENTS
    keys_own = jnp.concatenate(
        [latent, own_segment.astype(bf16), jnp.zeros((block_len, pad), bf16)], axis=1
    )
    mine = lax.dynamic_slice_in_dim(keys_own, core * half, half, 0)

    def along_y(near, far):
        pairs = [
            (2 * i + h, 2 * ((i + (near, far)[h]) % 8) + h) for i in range(8) for h in range(2)
        ]
        return lax.ppermute(mine, ("y", "xh"), pairs)

    column = jnp.stack([along_y(1, 2), along_y(3, 4)])
    to_other = jnp.where(
        (xl == 0) & (xh == 1), jnp.stack([mine, column[0]]), column
    )
    diagonal = [(0, 3), (1, 2), (2, 1), (3, 0)]
    pieces = [
        column,
        lax.ppermute(column, "xh", SWAP),
        lax.ppermute(to_other, "xl", SWAP),
        lax.ppermute(to_other, ("xl", "xh"), diagonal),
    ]

    def blocks_of(x, h):
        return [2 * (y - 1 - h) + x, 2 * (y - 3 - h) + x]

    def blocks_sent(x, h):
        near, far = blocks_of(x, h)
        odd = (x == 0) & (h == 1)
        return [jnp.where(odd, 2 * y, near), jnp.where(odd, near, far)]

    info = jnp.stack(
        blocks_of(xl, xh)
        + blocks_of(xl, 1 - xh)
        + blocks_sent(1 - xl, xh)
        + blocks_sent(1 - xl, 1 - xh)
        + [core, xl]
    ).astype(i32)

    masks = jnp.where(own_segment, 0.0, -FAR).astype(bf16)
    query_rows = jnp.concatenate(
        [
            queries,
            jnp.broadcast_to(masks[:, None, :], (block_len, local_heads, SEGMENTS)),
            jnp.zeros((block_len, local_heads, pad), bf16),
        ],
        axis=2,
    )
    query_rows = query_rows.reshape(16, 2, 8, local_heads, KEYW).transpose(3, 1, 0, 2, 4)
    query_rows = query_rows.reshape(local_heads, block_len, KEYW)
    state_out = [
        sds((2, 256, 128), f32),
        sds((2, 256, 128), f32),
        sds((2, 256, LATENT), f32),
    ]
    state = call(
        first_attention_kernel, state_out, [pltpu.VMEM((256, 2 * 256), f32)], True, 4
    )(info, query_rows, keys_own, column)
    first_other = lax.ppermute(column, "core", SWAP)
    *pieces, first_other, peak = lax.optimization_barrier((*pieces, first_other, state[0]))
    state = [peak] + list(state[1:])
    three = call(gather_kernel, [sds((6, half, KEYW), bf16)], count=3)(*pieces[1:])
    others = lax.ppermute(three, "core", SWAP)
    state = call(
        second_attention_kernel, state_out, [pltpu.VMEM((256, 4 * 256), f32)], True, 9
    )(info, query_rows, pieces[1], pieces[2], pieces[3], first_other, *state)
    send, keep = call(
        last_attention_kernel,
        [sds((half, width_model), bf16), sds((half, width_model), f32)],
        [pltpu.VMEM((256, 3 * 256), f32), pltpu.VMEM((2, 256, VDIM), bf16)],
        True,
        8,
    )(info, query_rows, others, *state, value_up, out_proj)
    got = lax.ppermute(send, "core", SWAP)
    pair_sum = call(add_kernel, [sds((16, 8, width_model), bf16)], count=2)(keep, got)

    weights_out = sds((3, width_out, 3 * ff_half), bf16)
    w_send, w_keep = call(split_weights_kernel, [weights_out, weights_out], (), True, 4)(
        info, expert_gate, expert_up, jnp.transpose(expert_down, (0, 2, 1))
    )
    pair_sum, w_send = lax.optimization_barrier((pair_sum, w_send))
    w_got = lax.ppermute(w_send, "xl", SWAP)

    spread = lax.all_to_all(pair_sum, ("z", "xh"), split_axis=0, concat_axis=0, tiled=True)
    packed = call(norm_kernel, [sds((16, 8, 512), bf16)], count=3)(
        spread, residual, norm_gain[None, :]
    )
    split = lax.all_to_all(packed, CTX, split_axis=0, concat_axis=0, tiled=True)
    split, w_got = lax.optimization_barrier((split, w_got))
    split = split.reshape(128, 512)
    w_in, w_down = call(
        join_weights_kernel,
        [sds((3 * 384, 2 * ff_half), bf16), sds((384, 3 * ff_half), bf16)],
        count=2,
    )(w_keep, w_got)

    routes = jnp.transpose(route_ids, (1, 0, 2)).reshape(128, TOPK)
    expert_axis = jnp.arange(EXPERTS, dtype=i32)
    named = jnp.any(routes[:, :, None] == expert_axis[None, None, :], axis=1)
    earlier_tokens = jnp.tril(jnp.ones((128, 128), bf16), -1)
    slot_all = jnp.dot(earlier_tokens, named.astype(bf16), preferred_element_type=f32).astype(i32)
    slot_of = jnp.sum(
        jnp.where(routes[:, :, None] == expert_axis[None, None, :], slot_all[:, None, :], 0), axis=2
    )
    target = (routes // 3) * SLOTS + (routes % 3) * CAP + slot_of
    slot_axis = jnp.arange(32 * SLOTS, dtype=i32)
    picker = jnp.any(target.T[None, :, :] == slot_axis[:, None, None], axis=1).astype(bf16)
    order = jnp.arange(128, dtype=i32)
    back_order = ((order % 16) * 8 + order // 16)[:, None] == order[None, :]
    target_rb = jnp.transpose(target.reshape(16, 8, TOPK), (1, 0, 2)).reshape(128, TOPK)
    gates_rb = route_gates.reshape(128, TOPK)
    weighting = jnp.sum(
        jnp.where(target_rb[:, :, None] == slot_axis[None, None, :], gates_rb[:, :, None], 0.0),
        axis=1,
    )

    travel = sds((32, 80, 128), bf16)
    outgoing = call(pick_kernel, [travel], count=2)(picker, split)
    received = lax.all_to_all(outgoing, EXP, split_axis=0, concat_axis=0, tiled=True)
    pre = call(gate_up_kernel, [sds((32 * SLOTS, 2 * ff_half), bf16)], count=2)(received, w_in)
    pre_parts = lax.all_to_all(
        pre.reshape(8, 128, 2 * ff_half), "y", split_axis=0, concat_axis=0, tiled=True
    )
    hidden = call(hidden_kernel, [sds((8, 128, ff_half), bf16)], count=1)(pre_parts)
    hidden_all = lax.all_to_all(hidden, "y", split_axis=0, concat_axis=0, tiled=True)
    expert_out = call(down_kernel, [travel], count=2)(
        hidden_all.reshape(32 * SLOTS, ff_half), w_down
    )
    returned = lax.all_to_all(expert_out, EXP, split_axis=0, concat_axis=0, tiled=True)
    mix_keep, mix_send = call(
        combine_kernel, [sds((128, width_out), f32), sds((128, width_out), bf16)], count=2
    )(weighting, returned)
    mix_got = lax.ppermute(mix_send, "xl", SWAP)
    stream_rb = jnp.dot(
        back_order.astype(bf16),
        split[:, width_pair : width_pair + width_out],
        preferred_element_type=f32,
    )
    result = (stream_rb + mix_keep + mix_got.astype(f32)).astype(bf16)
    return result.reshape(8, 16, width_out)


def solution(mesh):
    grid = Mesh(mesh.devices.reshape(8, 2, 8, 2, 2), ("y", "xl", "z", "xh", "core"))
    return jax.shard_map(
        on_device,
        mesh=grid,
        in_specs=(
            P(CTX, EXP, None),
            P(CTX, None),
            P(CTX),
            P(EXP, None, None),
            P(EXP, None),
            P(CTX + EXP, None),
            P(),
            P(EXP, None, None),
            P(EXP, None, None),
            P(EXP, CTX, None),
            P(EXP, CTX, None),
            P(EXP, None, CTX),
        ),
        out_specs=P(EXP, None, CTX),
        check_vma=False,
    )
```

```python
import jax
import jax.numpy as jnp
from jax import lax
from jax.experimental import pallas as pl
from jax.experimental.pallas import tpu as pltpu
from jax.sharding import Mesh, PartitionSpec as P

LATENT = 512
VDIM = 128
QKDIM = 192
EXPERTS = 96
TOPK = 6
CAP = 10
SLOTS = 32
SEGMENTS = 8
KEYW = 592
FAR = float(2**20)

CTX = ("y", "xl")
EXP = ("z", "xh", "core")
SWAP = [(0, 1), (1, 0)]
BIG_VMEM = pltpu.CompilerParams(vmem_limit_bytes=20 * 2**20)
f32, bf16, i32 = jnp.float32, jnp.bfloat16, jnp.int32


def keys_kernel(latent, segments, own):
    width, tokens = latent.shape
    own[:width, :] = latent[...]
    mark = lax.broadcasted_iota(i32, (KEYW - width, tokens), 0)
    own[width:, :] = jnp.where(segments[...] == mark, 1.0, 0.0).astype(bf16)


def keys_of(chunk):
    return chunk[...] if len(chunk.shape) == 2 else jnp.concatenate([chunk[0], chunk[1]], axis=1)


def nt_dot(a, b):
    return lax.dot_general(a, b, (((1,), (1,)), ((), ())), preferred_element_type=f32)


def attend_chunks(rows, chunks, biases, scores, old):
    scale = QKDIM ** (-0.5)
    peak = jnp.full((256, 128), -FAR, f32) if old is None else old[0]
    for n, (chunk, bias) in enumerate(zip(chunks, biases)):
        part = bias(jnp.dot(rows, keys_of(chunk), preferred_element_type=f32) * scale)
        scores[:, n * 256 : (n + 1) * 256] = part
        peak = jnp.maximum(peak, jnp.maximum(part[:, :128], part[:, 128:]))
    peak = jnp.max(peak, axis=1, keepdims=True)
    if old is None:
        sums, mixed = jnp.zeros((256, 128), f32), jnp.zeros((256, LATENT), f32)
    else:
        factor = jnp.exp(old[0][:, :1] - peak)
        sums, mixed = old[1] * factor, old[2] * factor
    for n, chunk in enumerate(chunks):
        terms = jnp.exp(scores[:, n * 256 : (n + 1) * 256] - peak)
        sums = sums + terms[:, :128] + terms[:, 128:]
        mixed = mixed + nt_dot(terms.astype(bf16), keys_of(chunk)[:LATENT])
    return jnp.broadcast_to(peak, (256, 128)), sums, mixed


def valid_bias(info, piece):
    def bias(part):
        lane = lax.broadcasted_iota(i32, (256, 256), 1)
        first = jnp.where(info[2 * piece] >= 0, 0.0, -FAR)
        second = jnp.where(info[2 * piece + 1] >= 0, 0.0, -FAR)
        return part + jnp.where(lane < 128, first, second)

    return bias


def causal_bias(part):
    lane = lax.broadcasted_iota(i32, (256, 256), 1)
    row = lax.broadcasted_iota(i32, (256, 256), 0)
    token = (row % 128) // 8 * 16 + row // 128 * 8 + row % 8
    return jnp.where(lane <= token, part, -FAR)


def first_attention_kernel(info, query, own, p0, peak, sums, mixed, scores):
    @pl.loop(0, 2)
    def _(head):
        state = attend_chunks(
            query[head], [own, p0], [causal_bias, valid_bias(info, 0)], scores, None
        )
        peak[head], sums[head], mixed[head] = state


def second_attention_kernel(
    info, query, p1, p2, p3, o0, old_peak, old_sums, old_mixed, peak, sums, mixed, scores
):
    @pl.loop(0, 2)
    def _(head):
        old = old_peak[head], old_sums[head], old_mixed[head]
        biases = [valid_bias(info, n) for n in (1, 2, 3, 0)]
        state = attend_chunks(query[head], [p1, p2, p3, o0], biases, scores, old)
        peak[head], sums[head], mixed[head] = state


def last_attention_kernel(
    info, query, others, old_peak, old_sums, old_mixed, value_up, out_proj, send, keep, scores, values
):
    core = info[8]

    @pl.loop(0, 2)
    def _(head):
        old = old_peak[head], old_sums[head], old_mixed[head]
        chunks = [others.at[2 * n : 2 * n + 2] for n in range(3)]
        biases = [valid_bias(info, n) for n in (1, 2, 3)]
        _, sums, mixed = attend_chunks(query[head], chunks, biases, scores, old)
        mixed = (mixed / jnp.sum(sums, axis=1, keepdims=True)).astype(bf16)
        values[head] = jnp.dot(mixed, value_up[head], preferred_element_type=f32).astype(bf16)

    def project(which, out):
        start = pl.multiple_of(which * 128, 128)
        both = jnp.concatenate([values[head, pl.ds(start, 128), :] for head in range(2)], axis=1)
        for c in range(0, out.shape[1], 640):
            out[:, c : c + 640] = jnp.dot(
                both, out_proj[:, c : c + 640], preferred_element_type=f32
            ).astype(out.dtype)

    project(1 - core, send)
    project(core, keep)


def add_kernel(keep, got, out):
    out[...] = (keep[...] + got[...].astype(f32)).reshape(out.shape).astype(bf16)


def gather_kernel(p1, p2, p3, out):
    for n, piece in enumerate((p1, p2, p3)):
        out[2 * n : 2 * n + 2] = piece[...]


def norm_kernel(spread, residual, gain, packed):
    attended = jnp.sum(spread[...].astype(f32), axis=0)
    stream = (residual[...].astype(f32) + attended).astype(bf16).astype(f32)
    mean_sq = jnp.mean(stream * stream, axis=1, keepdims=True)
    normed = (stream * lax.rsqrt(mean_sq + 1e-06) * gain[...]).astype(bf16).astype(f32)
    width = stream.shape[1] // 16
    fill = jnp.zeros((stream.shape[0], packed.shape[2] - 3 * width), f32)
    for c in range(16):
        mine, other = c * width, (c ^ 1) * width
        packed[c] = jnp.concatenate(
            [
                normed[:, mine : mine + width],
                normed[:, other : other + width],
                stream[:, mine : mine + width],
                fill,
            ],
            axis=1,
        ).astype(bf16)


def store_packed(out, n, rows):
    left = lax.broadcasted_iota(i32, (SLOTS // 2, 128), 1) < 64
    out[n, 0:32] = rows[:, :128].astype(bf16)
    out[n, 32:64] = rows[:, 128:256].astype(bf16)
    out[n, 64:80] = jnp.where(left, rows[:16, 256:], rows[16:, 256:]).astype(bf16)


def load_packed(ref, n):
    last = ref[n, 64:80]
    left = jnp.where(lax.broadcasted_iota(i32, (1, 128), 1) < 64, 1.0, 0.0).astype(bf16)
    last = jnp.concatenate([last * left, last * (1 - left)], axis=0)
    return jnp.concatenate([ref[n, 0:32], ref[n, 32:64], last], axis=1)


def pick_kernel(picker, split, out):
    values = split[:, :384]
    doubled = jnp.concatenate([values[:, :320], values[:, 256:320]], axis=1)
    for r in range(0, picker.shape[0], 256):
        rows = jnp.dot(picker[r : r + 256, :], doubled, preferred_element_type=f32)
        for n in range(256 // SLOTS):
            store_packed(out, r // SLOTS + n, rows[n * SLOTS : (n + 1) * SLOTS])


def row_mask(count, j):
    slot = lax.broadcasted_iota(i32, (count, 1), 0) % SLOTS
    return jnp.where((slot >= j * CAP) & (slot < (j + 1) * CAP), 1.0, 0.0).astype(bf16)


def spread_experts(rows, masks):
    return jnp.concatenate([rows * mask for mask in masks], axis=1)


def split_weights_kernel(info, gate, up, down, send, keep):
    half = gate.shape[2] // 2

    def move(out, start):
        for n, weights in enumerate((gate, up, down)):
            out[:, :, n * half : (n + 1) * half] = weights[:, :, start : start + half]

    @pl.when(info[9] == 0)
    def _():
        move(keep, 0)
        move(send, half)

    @pl.when(info[9] != 0)
    def _():
        move(keep, half)
        move(send, 0)


def join_weights_kernel(keep, got, into, down):
    rows = keep.shape[1]
    wide = into.shape[1]
    narrow = keep.shape[2] - wide
    for j in range(3):
        base = j * 384
        into[base : base + rows, :] = keep[j, :, :wide]
        into[base + rows : base + 2 * rows, :] = got[j, :, :wide]
        into[base + 2 * rows : base + 384, :] = got[j, 256 - rows :, :wide]
        lanes = slice(j * narrow, (j + 1) * narrow)
        down[:rows, lanes] = keep[j, :, wide:]
        down[rows : 2 * rows, lanes] = got[j, :, wide:]
        down[2 * rows :, lanes] = got[j, 256 - rows :, wide:]


def gate_up_kernel(received, weights, pre):
    masks = [row_mask(256, j) for j in range(3)]
    for r in range(0, received.shape[0], 8):
        rows = jnp.concatenate([load_packed(received, r + n) for n in range(8)], axis=0)
        total = jnp.dot(spread_experts(rows, masks), weights[...], preferred_element_type=f32)
        pre[r * SLOTS : (r + 8) * SLOTS, :] = total.astype(bf16)


def hidden_kernel(parts, out):
    total = jnp.sum(parts[...].astype(f32), axis=0)
    half = total.shape[1] // 2
    gate, up = total[:, :half], total[:, half:]
    hidden = (gate / (1.0 + jnp.exp(-gate)) * up).astype(bf16)
    for n in range(out.shape[0]):
        out[n] = hidden


def down_kernel(hidden, weights, out):
    masks = [row_mask(256, j) for j in range(3)]
    for r in range(0, hidden.shape[0], 256):
        rows = spread_experts(hidden[r : r + 256, :], masks)
        total = nt_dot(rows, weights[...])
        for n in range(256 // SLOTS):
            store_packed(out, r // SLOTS + n, total[n * SLOTS : (n + 1) * SLOTS])


def combine_kernel(weighting, returned, keep, send):
    width = keep.shape[1]
    rows = jnp.concatenate([load_packed(returned, n) for n in range(returned.shape[0])], axis=0)
    top = weighting[...].astype(bf16)
    rest = (weighting[...] - top.astype(f32)).astype(bf16)
    mixture = jnp.dot(top, rows, preferred_element_type=f32) + jnp.dot(
        rest, rows, preferred_element_type=f32
    )
    tail = mixture[:, 256:320] + mixture[:, 320:384]
    keep[...] = mixture[:, :width]
    send[...] = jnp.concatenate([mixture[:, width:256], tail], axis=1).astype(bf16)


def call(kernel, outs, scratch=(), smem_first=False, count=0):
    specs = [pl.BlockSpec(memory_space=pltpu.VMEM)] * count
    if smem_first:
        specs[0] = pl.BlockSpec(memory_space=pltpu.SMEM)
    out_specs = [pl.BlockSpec(memory_space=pltpu.VMEM)] * len(outs)
    single = len(outs) == 1
    return pl.pallas_call(
        kernel,
        in_specs=specs,
        out_specs=out_specs[0] if single else out_specs,
        out_shape=outs[0] if single else outs,
        scratch_shapes=list(scratch),
        compiler_params=BIG_VMEM,
    )


def sds(shape, dtype):
    return jax.ShapeDtypeStruct(shape, dtype)


def on_device(
    queries,
    latent,
    segment_ids,
    value_up,
    out_proj,
    residual,
    norm_gain,
    route_ids,
    route_gates,
    expert_gate,
    expert_up,
    expert_down,
):
    block_len, local_heads, width_key = queries.shape
    width_model = residual.shape[1]
    width_out = width_model // 16
    width_pair = 2 * width_out
    ff = expert_gate.shape[2]
    ff_half = ff // 2
    y, xl, xh, core = (lax.axis_index(a) for a in ("y", "xl", "xh", "core"))
    half = block_len // 2

    segment_axis = jnp.arange(SEGMENTS, dtype=i32)
    own_segment = segment_ids[:, None] == segment_axis[None, :]
    pad = KEYW - width_key - SEGMENTS
    keys_own = call(keys_kernel, [sds((KEYW, block_len), bf16)], count=2)(
        latent.T, segment_ids[None, :]
    )
    mine = lax.dynamic_slice_in_dim(keys_own, core * half, half, 1)

    def along_y(near, far):
        pairs = [
            (2 * i + h, 2 * ((i + (near, far)[h]) % 8) + h) for i in range(8) for h in range(2)
        ]
        return lax.ppermute(mine, ("y", "xh"), pairs)

    column = jnp.stack([along_y(1, 2), along_y(3, 4)])
    to_other = jnp.where(
        (xl == 0) & (xh == 1), jnp.stack([mine, column[0]]), column
    )
    diagonal = [(0, 3), (1, 2), (2, 1), (3, 0)]
    pieces = [
        column,
        lax.ppermute(column, "xh", SWAP),
        lax.ppermute(to_other, "xl", SWAP),
        lax.ppermute(to_other, ("xl", "xh"), diagonal),
    ]

    def blocks_of(x, h):
        return [2 * (y - 1 - h) + x, 2 * (y - 3 - h) + x]

    def blocks_sent(x, h):
        near, far = blocks_of(x, h)
        odd = (x == 0) & (h == 1)
        return [jnp.where(odd, 2 * y, near), jnp.where(odd, near, far)]

    info = jnp.stack(
        blocks_of(xl, xh)
        + blocks_of(xl, 1 - xh)
        + blocks_sent(1 - xl, xh)
        + blocks_sent(1 - xl, 1 - xh)
        + [core, xl]
    ).astype(i32)

    masks = jnp.where(own_segment, 0.0, -FAR).astype(bf16)
    query_rows = jnp.concatenate(
        [
            queries,
            jnp.broadcast_to(masks[:, None, :], (block_len, local_heads, SEGMENTS)),
            jnp.zeros((block_len, local_heads, pad), bf16),
        ],
        axis=2,
    )
    query_rows = query_rows.reshape(16, 2, 8, local_heads, KEYW).transpose(3, 1, 0, 2, 4)
    query_rows = query_rows.reshape(local_heads, block_len, KEYW)
    state_out = [
        sds((2, 256, 128), f32),
        sds((2, 256, 128), f32),
        sds((2, 256, LATENT), f32),
    ]
    state = call(
        first_attention_kernel, state_out, [pltpu.VMEM((256, 2 * 256), f32)], True, 4
    )(info, query_rows, keys_own, column)
    pieces[1], column_late = lax.optimization_barrier((pieces[1], column))
    first_other = lax.ppermute(column_late, "core", SWAP)
    *pieces, first_other, peak = lax.optimization_barrier((*pieces, first_other, state[0]))
    state = [peak] + list(state[1:])
    three = call(gather_kernel, [sds((6, KEYW, half), bf16)], count=3)(*pieces[1:])
    others = lax.ppermute(three, "core", SWAP)
    state = call(
        second_attention_kernel, state_out, [pltpu.VMEM((256, 4 * 256), f32)], True, 9
    )(info, query_rows, pieces[1], pieces[2], pieces[3], first_other, *state)
    send, keep = call(
        last_attention_kernel,
        [sds((half, width_model), bf16), sds((half, width_model), f32)],
        [pltpu.VMEM((256, 3 * 256), f32), pltpu.VMEM((2, 256, VDIM), bf16)],
        True,
        8,
    )(info, query_rows, others, *state, value_up, out_proj)
    got = lax.ppermute(send, "core", SWAP)
    pair_sum = call(add_kernel, [sds((16, 8, width_model), bf16)], count=2)(keep, got)

    weights_out = sds((3, width_out, 3 * ff_half), bf16)
    w_send, w_keep = call(split_weights_kernel, [weights_out, weights_out], (), True, 4)(
        info, expert_gate, expert_up, jnp.transpose(expert_down, (0, 2, 1))
    )
    pair_sum, w_send = lax.optimization_barrier((pair_sum, w_send))
    w_got = lax.ppermute(w_send, "xl", SWAP)

    spread = lax.all_to_all(pair_sum, ("z", "xh"), split_axis=0, concat_axis=0, tiled=True)
    packed = call(norm_kernel, [sds((16, 8, 512), bf16)], count=3)(
        spread, residual, norm_gain[None, :]
    )
    split = lax.all_to_all(packed, CTX, split_axis=0, concat_axis=0, tiled=True)
    split, w_got = lax.optimization_barrier((split, w_got))
    split = split.reshape(128, 512)
    w_in, w_down = call(
        join_weights_kernel,
        [sds((3 * 384, 2 * ff_half), bf16), sds((384, 3 * ff_half), bf16)],
        count=2,
    )(w_keep, w_got)

    routes = jnp.transpose(route_ids, (1, 0, 2)).reshape(128, TOPK)
    expert_axis = jnp.arange(EXPERTS, dtype=i32)
    named = jnp.any(routes[:, :, None] == expert_axis[None, None, :], axis=1)
    earlier_tokens = jnp.tril(jnp.ones((128, 128), bf16), -1)
    slot_all = jnp.dot(earlier_tokens, named.astype(bf16), preferred_element_type=f32).astype(i32)
    slot_of = jnp.sum(
        jnp.where(routes[:, :, None] == expert_axis[None, None, :], slot_all[:, None, :], 0), axis=2
    )
    target = (routes // 3) * SLOTS + (routes % 3) * CAP + slot_of
    slot_axis = jnp.arange(32 * SLOTS, dtype=i32)
    picker = jnp.any(target.T[None, :, :] == slot_axis[:, None, None], axis=1).astype(bf16)
    order = jnp.arange(128, dtype=i32)
    back_order = ((order % 16) * 8 + order // 16)[:, None] == order[None, :]
    target_rb = jnp.transpose(target.reshape(16, 8, TOPK), (1, 0, 2)).reshape(128, TOPK)
    gates_rb = route_gates.reshape(128, TOPK)
    weighting = jnp.sum(
        jnp.where(target_rb[:, :, None] == slot_axis[None, None, :], gates_rb[:, :, None], 0.0),
        axis=1,
    )

    travel = sds((32, 80, 128), bf16)
    outgoing = call(pick_kernel, [travel], count=2)(picker, split)
    received = lax.all_to_all(outgoing, EXP, split_axis=0, concat_axis=0, tiled=True)
    pre = call(gate_up_kernel, [sds((32 * SLOTS, 2 * ff_half), bf16)], count=2)(received, w_in)
    pre_parts = lax.all_to_all(
        pre.reshape(8, 128, 2 * ff_half), "y", split_axis=0, concat_axis=0, tiled=True
    )
    hidden = call(hidden_kernel, [sds((8, 128, ff_half), bf16)], count=1)(pre_parts)
    hidden_all = lax.all_to_all(hidden, "y", split_axis=0, concat_axis=0, tiled=True)
    expert_out = call(down_kernel, [travel], count=2)(
        hidden_all.reshape(32 * SLOTS, ff_half), w_down
    )
    returned = lax.all_to_all(expert_out, EXP, split_axis=0, concat_axis=0, tiled=True)
    mix_keep, mix_send = call(
        combine_kernel, [sds((128, width_out), f32), sds((128, width_out), bf16)], count=2
    )(weighting, returned)
    mix_got = lax.ppermute(mix_send, "xl", SWAP)
    stream_rb = jnp.dot(
        back_order.astype(bf16),
        split[:, width_pair : width_pair + width_out],
        preferred_element_type=f32,
    )
    result = (stream_rb + mix_keep + mix_got.astype(f32)).astype(bf16)
    return result.reshape(8, 16, width_out)


def solution(mesh):
    grid = Mesh(mesh.devices.reshape(8, 2, 8, 2, 2), ("y", "xl", "z", "xh", "core"))
    return jax.shard_map(
        on_device,
        mesh=grid,
        in_specs=(
            P(CTX, EXP, None),
            P(CTX, None),
            P(CTX),
            P(EXP, None, None),
            P(EXP, None),
            P(CTX + EXP, None),
            P(),
            P(EXP, None, None),
            P(EXP, None, None),
            P(EXP, CTX, None),
            P(EXP, CTX, None),
            P(EXP, None, CTX),
        ),
        out_specs=P(EXP, None, CTX),
        check_vma=False,
    )
```

```python
import jax
import jax.numpy as jnp
from jax import lax
from jax.experimental import pallas as pl
from jax.experimental.pallas import tpu as pltpu
from jax.sharding import Mesh, PartitionSpec as P

LATENT = 512
VDIM = 128
QKDIM = 192
EXPERTS = 96
TOPK = 6
CAP = 10
SLOTS = 32
SEGMENTS = 8
KEYW = 592
FAR = float(2**20)

CTX = ("y", "xl")
EXP = ("z", "xh", "core")
SWAP = [(0, 1), (1, 0)]
BIG_VMEM = pltpu.CompilerParams(vmem_limit_bytes=20 * 2**20)
f32, bf16, i32 = jnp.float32, jnp.bfloat16, jnp.int32


def keys_kernel(latent, segments, own):
    width, tokens = latent.shape
    own[:width, :] = latent[...]
    mark = lax.broadcasted_iota(i32, (KEYW - width, tokens), 0)
    own[width:, :] = jnp.where(segments[...] == mark, 1.0, 0.0).astype(bf16)


def keys_of(chunk):
    return chunk[...] if len(chunk.shape) == 2 else jnp.concatenate([chunk[0], chunk[1]], axis=1)


def nt_dot(a, b):
    return lax.dot_general(a, b, (((1,), (1,)), ((), ())), preferred_element_type=f32)


def attend_chunks(rows, chunks, biases, scores, old):
    scale = QKDIM ** (-0.5)
    peak = jnp.full((256, 128), -FAR, f32) if old is None else old[0]
    for n, (chunk, bias) in enumerate(zip(chunks, biases)):
        part = bias(jnp.dot(rows, keys_of(chunk), preferred_element_type=f32) * scale)
        scores[:, n * 256 : (n + 1) * 256] = part
        peak = jnp.maximum(peak, jnp.maximum(part[:, :128], part[:, 128:]))
    peak = jnp.max(peak, axis=1, keepdims=True)
    if old is None:
        sums, mixed = jnp.zeros((256, 128), f32), jnp.zeros((256, LATENT), f32)
    else:
        factor = jnp.exp(old[0][:, :1] - peak)
        sums, mixed = old[1] * factor, old[2] * factor
    for n, chunk in enumerate(chunks):
        terms = jnp.exp(scores[:, n * 256 : (n + 1) * 256] - peak)
        sums = sums + terms[:, :128] + terms[:, 128:]
        mixed = mixed + nt_dot(terms.astype(bf16), keys_of(chunk)[:LATENT])
    return jnp.broadcast_to(peak, (256, 128)), sums, mixed


def valid_bias(info, piece):
    def bias(part):
        lane = lax.broadcasted_iota(i32, (256, 256), 1)
        first = jnp.where(info[2 * piece] >= 0, 0.0, -FAR)
        second = jnp.where(info[2 * piece + 1] >= 0, 0.0, -FAR)
        return part + jnp.where(lane < 128, first, second)

    return bias


def causal_bias(part):
    lane = lax.broadcasted_iota(i32, (256, 256), 1)
    row = lax.broadcasted_iota(i32, (256, 256), 0)
    token = (row % 128) // 8 * 16 + row // 128 * 8 + row % 8
    return jnp.where(lane <= token, part, -FAR)


def first_attention_kernel(info, query, own, p0, peak, sums, mixed, scores):
    @pl.loop(0, 2)
    def _(head):
        state = attend_chunks(
            query[head], [own, p0], [causal_bias, valid_bias(info, 0)], scores, None
        )
        peak[head], sums[head], mixed[head] = state


def second_attention_kernel(
    info, query, p1, p2, p3, o0, old_peak, old_sums, old_mixed, peak, sums, mixed, scores
):
    @pl.loop(0, 2)
    def _(head):
        old = old_peak[head], old_sums[head], old_mixed[head]
        biases = [valid_bias(info, n) for n in (1, 2, 3, 0)]
        state = attend_chunks(query[head], [p1, p2, p3, o0], biases, scores, old)
        peak[head], sums[head], mixed[head] = state


def last_attention_kernel(
    info, query, others, old_peak, old_sums, old_mixed, value_up, out_proj, send, keep, scores, values
):
    core = info[8]

    @pl.loop(0, 2)
    def _(head):
        old = old_peak[head], old_sums[head], old_mixed[head]
        chunks = [others.at[2 * n : 2 * n + 2] for n in range(3)]
        biases = [valid_bias(info, n) for n in (1, 2, 3)]
        _, sums, mixed = attend_chunks(query[head], chunks, biases, scores, old)
        mixed = (mixed / jnp.sum(sums, axis=1, keepdims=True)).astype(bf16)
        values[head] = jnp.dot(mixed, value_up[head], preferred_element_type=f32).astype(bf16)

    def project(which, out):
        start = pl.multiple_of(which * 128, 128)
        both = jnp.concatenate([values[head, pl.ds(start, 128), :] for head in range(2)], axis=1)
        for c in range(0, out.shape[1], 640):
            out[:, c : c + 640] = jnp.dot(
                both, out_proj[:, c : c + 640], preferred_element_type=f32
            ).astype(out.dtype)

    project(1 - core, send)
    project(core, keep)


def add_kernel(keep, got, out):
    out[...] = (keep[...] + got[...].astype(f32)).reshape(out.shape).astype(bf16)


def gather_kernel(p1, p2, p3, out):
    for n, piece in enumerate((p1, p2, p3)):
        out[2 * n : 2 * n + 2] = piece[...]


def norm_kernel(spread, residual, gain, packed):
    attended = jnp.sum(spread[...].astype(f32), axis=0)
    stream = (residual[...].astype(f32) + attended).astype(bf16).astype(f32)
    mean_sq = jnp.mean(stream * stream, axis=1, keepdims=True)
    normed = (stream * lax.rsqrt(mean_sq + 1e-06) * gain[...]).astype(bf16).astype(f32)
    width = stream.shape[1] // 16
    fill = jnp.zeros((stream.shape[0], packed.shape[2] - 3 * width), f32)
    for c in range(16):
        mine, other = c * width, (c ^ 1) * width
        packed[c] = jnp.concatenate(
            [
                normed[:, mine : mine + width],
                normed[:, other : other + width],
                stream[:, mine : mine + width],
                fill,
            ],
            axis=1,
        ).astype(bf16)


def store_packed(out, n, rows):
    left = lax.broadcasted_iota(i32, (SLOTS // 2, 128), 1) < 64
    out[n, 0:32] = rows[:, :128].astype(bf16)
    out[n, 32:64] = rows[:, 128:256].astype(bf16)
    out[n, 64:80] = jnp.where(left, rows[:16, 256:], rows[16:, 256:]).astype(bf16)


def load_packed(ref, n):
    last = ref[n, 64:80]
    left = jnp.where(lax.broadcasted_iota(i32, (1, 128), 1) < 64, 1.0, 0.0).astype(bf16)
    last = jnp.concatenate([last * left, last * (1 - left)], axis=0)
    return jnp.concatenate([ref[n, 0:32], ref[n, 32:64], last], axis=1)


def pick_kernel(picker, split, out):
    values = split[:, :384]
    doubled = jnp.concatenate([values[:, :320], values[:, 256:320]], axis=1)
    for r in range(0, picker.shape[0], 256):
        rows = jnp.dot(picker[r : r + 256, :], doubled, preferred_element_type=f32)
        for n in range(256 // SLOTS):
            store_packed(out, r // SLOTS + n, rows[n * SLOTS : (n + 1) * SLOTS])


def row_mask(count, j):
    slot = lax.broadcasted_iota(i32, (count, 1), 0) % SLOTS
    return jnp.where((slot >= j * CAP) & (slot < (j + 1) * CAP), 1.0, 0.0).astype(bf16)


def spread_experts(rows, masks):
    return jnp.concatenate([rows * mask for mask in masks], axis=1)


def split_weights_kernel(info, gate, up, down, in_send, in_keep, down_send, down_keep):
    half = gate.shape[2] // 2

    def move(into, onto, start):
        into[:, :, :half] = gate[:, :, start : start + half]
        into[:, :, half:] = up[:, :, start : start + half]
        onto[...] = down[:, :, start : start + half]

    @pl.when(info[9] == 0)
    def _():
        move(in_keep, down_keep, 0)
        move(in_send, down_send, half)

    @pl.when(info[9] != 0)
    def _():
        move(in_keep, down_keep, half)
        move(in_send, down_send, 0)


def join_in_kernel(keep, got, out):
    rows = keep.shape[1]
    for j in range(3):
        base = j * 384
        out[base : base + rows, :] = keep[j]
        out[base + rows : base + 2 * rows, :] = got[j]
        out[base + 2 * rows : base + 384, :] = got[j, 256 - rows :]


def join_down_kernel(keep, got, out):
    rows, width = keep.shape[1:]
    for j in range(3):
        lanes = slice(j * width, (j + 1) * width)
        out[:rows, lanes] = keep[j]
        out[rows : 2 * rows, lanes] = got[j]
        out[2 * rows :, lanes] = got[j, 256 - rows :]


def gate_up_kernel(received, weights, pre):
    masks = [row_mask(256, j) for j in range(3)]
    for r in range(0, received.shape[0], 8):
        rows = jnp.concatenate([load_packed(received, r + n) for n in range(8)], axis=0)
        total = jnp.dot(spread_experts(rows, masks), weights[...], preferred_element_type=f32)
        pre[r * SLOTS : (r + 8) * SLOTS, :] = total.astype(bf16)


def hidden_kernel(parts, out):
    total = jnp.sum(parts[...].astype(f32), axis=0)
    half = total.shape[1] // 2
    gate, up = total[:, :half], total[:, half:]
    hidden = (gate / (1.0 + jnp.exp(-gate)) * up).astype(bf16)
    for n in range(out.shape[0]):
        out[n] = hidden


def down_kernel(hidden, weights, out):
    masks = [row_mask(256, j) for j in range(3)]
    for r in range(0, hidden.shape[0], 256):
        rows = spread_experts(hidden[r : r + 256, :], masks)
        total = nt_dot(rows, weights[...])
        for n in range(256 // SLOTS):
            store_packed(out, r // SLOTS + n, total[n * SLOTS : (n + 1) * SLOTS])


def combine_kernel(weighting, returned, keep, send):
    width = keep.shape[1]
    rows = jnp.concatenate([load_packed(returned, n) for n in range(returned.shape[0])], axis=0)
    top = weighting[...].astype(bf16)
    rest = (weighting[...] - top.astype(f32)).astype(bf16)
    mixture = jnp.dot(top, rows, preferred_element_type=f32) + jnp.dot(
        rest, rows, preferred_element_type=f32
    )
    tail = mixture[:, 256:320] + mixture[:, 320:384]
    keep[...] = mixture[:, :width]
    send[...] = jnp.concatenate([mixture[:, width:256], tail], axis=1).astype(bf16)


def call(kernel, outs, scratch=(), smem_first=False, count=0):
    specs = [pl.BlockSpec(memory_space=pltpu.VMEM)] * count
    if smem_first:
        specs[0] = pl.BlockSpec(memory_space=pltpu.SMEM)
    out_specs = [pl.BlockSpec(memory_space=pltpu.VMEM)] * len(outs)
    single = len(outs) == 1
    return pl.pallas_call(
        kernel,
        in_specs=specs,
        out_specs=out_specs[0] if single else out_specs,
        out_shape=outs[0] if single else outs,
        scratch_shapes=list(scratch),
        compiler_params=BIG_VMEM,
    )


def sds(shape, dtype):
    return jax.ShapeDtypeStruct(shape, dtype)


def on_device(
    queries,
    latent,
    segment_ids,
    value_up,
    out_proj,
    residual,
    norm_gain,
    route_ids,
    route_gates,
    expert_gate,
    expert_up,
    expert_down,
):
    block_len, local_heads, width_key = queries.shape
    width_model = residual.shape[1]
    width_out = width_model // 16
    width_pair = 2 * width_out
    ff = expert_gate.shape[2]
    ff_half = ff // 2
    y, xl, xh, core = (lax.axis_index(a) for a in ("y", "xl", "xh", "core"))
    half = block_len // 2

    segment_axis = jnp.arange(SEGMENTS, dtype=i32)
    own_segment = segment_ids[:, None] == segment_axis[None, :]
    pad = KEYW - width_key - SEGMENTS
    keys_own = call(keys_kernel, [sds((KEYW, block_len), bf16)], count=2)(
        latent.T, segment_ids[None, :]
    )
    mine = lax.dynamic_slice_in_dim(keys_own, core * half, half, 1)

    def along_y(near, far):
        pairs = [
            (2 * i + h, 2 * ((i + (near, far)[h]) % 8) + h) for i in range(8) for h in range(2)
        ]
        return lax.ppermute(mine, ("y", "xh"), pairs)

    column = jnp.stack([along_y(1, 2), along_y(3, 4)])
    to_other = jnp.where(
        (xl == 0) & (xh == 1), jnp.stack([mine, column[0]]), column
    )
    diagonal = [(0, 3), (1, 2), (2, 1), (3, 0)]
    pieces = [
        column,
        lax.ppermute(column, "xh", SWAP),
        lax.ppermute(to_other, "xl", SWAP),
        lax.ppermute(to_other, ("xl", "xh"), diagonal),
    ]

    def blocks_of(x, h):
        return [2 * (y - 1 - h) + x, 2 * (y - 3 - h) + x]

    def blocks_sent(x, h):
        near, far = blocks_of(x, h)
        odd = (x == 0) & (h == 1)
        return [jnp.where(odd, 2 * y, near), jnp.where(odd, near, far)]

    info = jnp.stack(
        blocks_of(xl, xh)
        + blocks_of(xl, 1 - xh)
        + blocks_sent(1 - xl, xh)
        + blocks_sent(1 - xl, 1 - xh)
        + [core, xl]
    ).astype(i32)

    masks = jnp.where(own_segment, 0.0, -FAR).astype(bf16)
    query_rows = jnp.concatenate(
        [
            queries,
            jnp.broadcast_to(masks[:, None, :], (block_len, local_heads, SEGMENTS)),
            jnp.zeros((block_len, local_heads, pad), bf16),
        ],
        axis=2,
    )
    query_rows = query_rows.reshape(16, 2, 8, local_heads, KEYW).transpose(3, 1, 0, 2, 4)
    query_rows = query_rows.reshape(local_heads, block_len, KEYW)
    state_out = [
        sds((2, 256, 128), f32),
        sds((2, 256, 128), f32),
        sds((2, 256, LATENT), f32),
    ]
    state = call(
        first_attention_kernel, state_out, [pltpu.VMEM((256, 2 * 256), f32)], True, 4
    )(info, query_rows, keys_own, column)
    pieces[1], column_late, peak = lax.optimization_barrier((pieces[1], column, state[0]))
    state = [peak] + list(state[1:])
    first_other = lax.ppermute(column_late, "core", SWAP)
    *pieces, first_other = lax.optimization_barrier((*pieces, first_other))
    three = call(gather_kernel, [sds((6, KEYW, half), bf16)], count=3)(*pieces[1:])
    others = lax.ppermute(three, "core", SWAP)
    state = call(
        second_attention_kernel, state_out, [pltpu.VMEM((256, 4 * 256), f32)], True, 9
    )(info, query_rows, pieces[1], pieces[2], pieces[3], first_other, *state)
    send, keep = call(
        last_attention_kernel,
        [sds((half, width_model), bf16), sds((half, width_model), f32)],
        [pltpu.VMEM((256, 3 * 256), f32), pltpu.VMEM((2, 256, VDIM), bf16)],
        True,
        8,
    )(info, query_rows, others, *state, value_up, out_proj)
    got = lax.ppermute(send, "core", SWAP)
    pair_sum = call(add_kernel, [sds((16, 8, width_model), bf16)], count=2)(keep, got)

    in_out = sds((3, width_out, 2 * ff_half), bf16)
    down_out = sds((3, width_out, ff_half), bf16)
    in_send, in_keep, down_send, down_keep = call(
        split_weights_kernel, [in_out, in_out, down_out, down_out], (), True, 4
    )(info, expert_gate, expert_up, jnp.transpose(expert_down, (0, 2, 1)))
    pair_sum, in_send = lax.optimization_barrier((pair_sum, in_send))
    in_got = lax.ppermute(in_send, "xl", SWAP)

    spread = lax.all_to_all(pair_sum, ("z", "xh"), split_axis=0, concat_axis=0, tiled=True)
    packed = call(norm_kernel, [sds((16, 8, 512), bf16)], count=3)(
        spread, residual, norm_gain[None, :]
    )
    split = lax.all_to_all(packed, CTX, split_axis=0, concat_axis=0, tiled=True)
    split, in_got, down_send = lax.optimization_barrier((split, in_got, down_send))
    down_got = lax.ppermute(down_send, "xl", SWAP)
    split = split.reshape(128, 512)
    w_in = call(join_in_kernel, [sds((3 * 384, 2 * ff_half), bf16)], count=2)(in_keep, in_got)
    w_down = call(join_down_kernel, [sds((384, 3 * ff_half), bf16)], count=2)(down_keep, down_got)

    routes = jnp.transpose(route_ids, (1, 0, 2)).reshape(128, TOPK)
    expert_axis = jnp.arange(EXPERTS, dtype=i32)
    named = jnp.any(routes[:, :, None] == expert_axis[None, None, :], axis=1)
    earlier_tokens = jnp.tril(jnp.ones((128, 128), bf16), -1)
    slot_all = jnp.dot(earlier_tokens, named.astype(bf16), preferred_element_type=f32).astype(i32)
    slot_of = jnp.sum(
        jnp.where(routes[:, :, None] == expert_axis[None, None, :], slot_all[:, None, :], 0), axis=2
    )
    target = (routes // 3) * SLOTS + (routes % 3) * CAP + slot_of
    slot_axis = jnp.arange(32 * SLOTS, dtype=i32)
    picker = jnp.any(target.T[None, :, :] == slot_axis[:, None, None], axis=1).astype(bf16)
    order = jnp.arange(128, dtype=i32)
    back_order = ((order % 16) * 8 + order // 16)[:, None] == order[None, :]
    target_rb = jnp.transpose(target.reshape(16, 8, TOPK), (1, 0, 2)).reshape(128, TOPK)
    gates_rb = route_gates.reshape(128, TOPK)
    weighting = jnp.sum(
        jnp.where(target_rb[:, :, None] == slot_axis[None, None, :], gates_rb[:, :, None], 0.0),
        axis=1,
    )

    travel = sds((32, 80, 128), bf16)
    outgoing = call(pick_kernel, [travel], count=2)(picker, split)
    received = lax.all_to_all(outgoing, EXP, split_axis=0, concat_axis=0, tiled=True)
    received, w_in, w_down = lax.optimization_barrier((received, w_in, w_down))
    pre = call(gate_up_kernel, [sds((32 * SLOTS, 2 * ff_half), bf16)], count=2)(received, w_in)
    pre_parts = lax.all_to_all(
        pre.reshape(8, 128, 2 * ff_half), "y", split_axis=0, concat_axis=0, tiled=True
    )
    hidden = call(hidden_kernel, [sds((8, 128, ff_half), bf16)], count=1)(pre_parts)
    hidden_all = lax.all_to_all(hidden, "y", split_axis=0, concat_axis=0, tiled=True)
    expert_out = call(down_kernel, [travel], count=2)(
        hidden_all.reshape(32 * SLOTS, ff_half), w_down
    )
    returned = lax.all_to_all(expert_out, EXP, split_axis=0, concat_axis=0, tiled=True)
    mix_keep, mix_send = call(
        combine_kernel, [sds((128, width_out), f32), sds((128, width_out), bf16)], count=2
    )(weighting, returned)
    mix_got = lax.ppermute(mix_send, "xl", SWAP)
    stream_rb = jnp.dot(
        back_order.astype(bf16),
        split[:, width_pair : width_pair + width_out],
        preferred_element_type=f32,
    )
    result = (stream_rb + mix_keep + mix_got.astype(f32)).astype(bf16)
    return result.reshape(8, 16, width_out)


def solution(mesh):
    grid = Mesh(mesh.devices.reshape(8, 2, 8, 2, 2), ("y", "xl", "z", "xh", "core"))
    return jax.shard_map(
        on_device,
        mesh=grid,
        in_specs=(
            P(CTX, EXP, None),
            P(CTX, None),
            P(CTX),
            P(EXP, None, None),
            P(EXP, None),
            P(CTX + EXP, None),
            P(),
            P(EXP, None, None),
            P(EXP, None, None),
            P(EXP, CTX, None),
            P(EXP, CTX, None),
            P(EXP, None, CTX),
        ),
        out_specs=P(EXP, None, CTX),
        check_vma=False,
    )
```

```python
import jax
import jax.numpy as jnp
from jax import lax
from jax.experimental import pallas as pl
from jax.experimental.pallas import tpu as pltpu
from jax.sharding import Mesh, PartitionSpec as P

LATENT = 512
VDIM = 128
QKDIM = 192
EXPERTS = 96
TOPK = 6
CAP = 10
SLOTS = 32
SEGMENTS = 8
KEYW = 592
FAR = float(2**20)

CTX = ("yh", "yl", "xl")
YS = ("yh", "yl")
EXP = ("z", "xh", "core")
SWAP = [(0, 1), (1, 0)]
BIG_VMEM = pltpu.CompilerParams(vmem_limit_bytes=20 * 2**20)
f32, bf16, i32 = jnp.float32, jnp.bfloat16, jnp.int32


def keys_kernel(latent, segments, own):
    width, tokens = latent.shape
    own[:width, :] = latent[...]
    mark = lax.broadcasted_iota(i32, (KEYW - width, tokens), 0)
    own[width:, :] = jnp.where(segments[...] == mark, 1.0, 0.0).astype(bf16)


def keys_of(chunk):
    return chunk[...] if len(chunk.shape) == 2 else jnp.concatenate([chunk[0], chunk[1]], axis=1)


def nt_dot(a, b):
    return lax.dot_general(a, b, (((1,), (1,)), ((), ())), preferred_element_type=f32)


def attend_chunks(rows, chunks, biases, scores, old):
    scale = QKDIM ** (-0.5)
    peak = jnp.full((256, 128), -FAR, f32) if old is None else old[0]
    for n, (chunk, bias) in enumerate(zip(chunks, biases)):
        part = bias(jnp.dot(rows, keys_of(chunk), preferred_element_type=f32) * scale)
        scores[:, n * 256 : (n + 1) * 256] = part
        peak = jnp.maximum(peak, jnp.maximum(part[:, :128], part[:, 128:]))
    peak = jnp.max(peak, axis=1, keepdims=True)
    if old is None:
        sums, mixed = jnp.zeros((256, 128), f32), jnp.zeros((256, LATENT), f32)
    else:
        factor = jnp.exp(old[0][:, :1] - peak)
        sums, mixed = old[1] * factor, old[2] * factor
    for n, chunk in enumerate(chunks):
        terms = jnp.exp(scores[:, n * 256 : (n + 1) * 256] - peak)
        sums = sums + terms[:, :128] + terms[:, 128:]
        mixed = mixed + nt_dot(terms.astype(bf16), keys_of(chunk)[:LATENT])
    return jnp.broadcast_to(peak, (256, 128)), sums, mixed


def valid_bias(info, piece):
    def bias(part):
        lane = lax.broadcasted_iota(i32, (256, 256), 1)
        first = jnp.where(info[2 * piece] >= 0, 0.0, -FAR)
        second = jnp.where(info[2 * piece + 1] >= 0, 0.0, -FAR)
        return part + jnp.where(lane < 128, first, second)

    return bias


def causal_bias(part):
    lane = lax.broadcasted_iota(i32, (256, 256), 1)
    row = lax.broadcasted_iota(i32, (256, 256), 0)
    token = (row % 128) // 8 * 16 + row // 128 * 8 + row % 8
    return jnp.where(lane <= token, part, -FAR)


def first_attention_kernel(info, query, own, p0, peak, sums, mixed, scores):
    @pl.loop(0, 2)
    def _(head):
        state = attend_chunks(
            query[head], [own, p0], [causal_bias, valid_bias(info, 0)], scores, None
        )
        peak[head], sums[head], mixed[head] = state


def second_attention_kernel(
    info, query, p1, p2, p3, o0, old_peak, old_sums, old_mixed, peak, sums, mixed, scores
):
    @pl.loop(0, 2)
    def _(head):
        old = old_peak[head], old_sums[head], old_mixed[head]
        biases = [valid_bias(info, n) for n in (1, 2, 3, 0)]
        state = attend_chunks(query[head], [p1, p2, p3, o0], biases, scores, old)
        peak[head], sums[head], mixed[head] = state


def last_attention_kernel(
    info, query, others, old_peak, old_sums, old_mixed, value_up, out_proj, send, keep, scores, values
):
    core = info[8]

    @pl.loop(0, 2)
    def _(head):
        old = old_peak[head], old_sums[head], old_mixed[head]
        chunks = [others.at[2 * n : 2 * n + 2] for n in range(3)]
        biases = [valid_bias(info, n) for n in (1, 2, 3)]
        _, sums, mixed = attend_chunks(query[head], chunks, biases, scores, old)
        mixed = (mixed / jnp.sum(sums, axis=1, keepdims=True)).astype(bf16)
        values[head] = jnp.dot(mixed, value_up[head], preferred_element_type=f32).astype(bf16)

    def project(which, out):
        start = pl.multiple_of(which * 128, 128)
        both = jnp.concatenate([values[head, pl.ds(start, 128), :] for head in range(2)], axis=1)
        for c in range(0, out.shape[1], 640):
            out[:, c : c + 640] = jnp.dot(
                both, out_proj[:, c : c + 640], preferred_element_type=f32
            ).astype(out.dtype)

    project(1 - core, send)
    project(core, keep)


def add_kernel(keep, got, out):
    out[...] = (keep[...] + got[...].astype(f32)).reshape(out.shape).astype(bf16)


def gather_kernel(p1, p2, p3, out):
    for n, piece in enumerate((p1, p2, p3)):
        out[2 * n : 2 * n + 2] = piece[...]


def norm_kernel(spread, residual, gain, packed):
    attended = jnp.sum(spread[...].astype(f32), axis=0)
    stream = (residual[...].astype(f32) + attended).astype(bf16).astype(f32)
    mean_sq = jnp.mean(stream * stream, axis=1, keepdims=True)
    normed = (stream * lax.rsqrt(mean_sq + 1e-06) * gain[...]).astype(bf16).astype(f32)
    width = stream.shape[1] // 16
    fill = jnp.zeros((stream.shape[0], packed.shape[2] - 5 * width), f32)
    for c in range(16):
        parts = [normed[:, (c ^ k) * width : ((c ^ k) + 1) * width] for k in range(4)]
        parts += [stream[:, c * width : (c + 1) * width], fill]
        packed[c] = jnp.concatenate(parts, axis=1).astype(bf16)


def store_packed(out, n, rows):
    left = lax.broadcasted_iota(i32, (SLOTS // 2, 128), 1) < 64
    out[n, 0:32] = rows[:, :128].astype(bf16)
    out[n, 32:64] = rows[:, 128:256].astype(bf16)
    out[n, 64:80] = jnp.where(left, rows[:16, 256:], rows[16:, 256:]).astype(bf16)


def load_packed(ref, n):
    last = ref[n, 64:80]
    left = jnp.where(lax.broadcasted_iota(i32, (1, 128), 1) < 64, 1.0, 0.0).astype(bf16)
    last = jnp.concatenate([last * left, last * (1 - left)], axis=0)
    return jnp.concatenate([ref[n, 0:32], ref[n, 32:64], last], axis=1)


def pick_kernel(picker, split, out):
    width = out.shape[2]
    for r in range(0, picker.shape[0], 256):
        rows = jnp.dot(picker[r : r + 256, :], split[:, :width], preferred_element_type=f32)
        out[r // SLOTS : (r + 256) // SLOTS] = rows.reshape(256 // SLOTS, SLOTS, width).astype(bf16)


def row_mask(count, j):
    slot = lax.broadcasted_iota(i32, (count, 1), 0) % SLOTS
    return jnp.where((slot >= j * CAP) & (slot < (j + 1) * CAP), 1.0, 0.0).astype(bf16)


def spread_experts(rows, masks):
    return jnp.concatenate([rows * mask for mask in masks], axis=1)


def split_weights_kernel(info, gate, up, down, keep, send_x, send_y, send_d, down_keep, down_send):
    part = gate.shape[2] // 4

    def quarter(weights, q):
        return weights[:, :, q * part : (q + 1) * part]

    for own in range(4):

        @pl.when(info[10] == own)
        def _():
            for k, out in enumerate((keep, send_x, send_y, send_d)):
                q = own ^ k
                out[...] = jnp.concatenate([quarter(gate, q), quarter(up, q)], axis=2)

    for own in range(2):

        @pl.when(info[9] == own)
        def _():
            for q, out in ((own, down_keep), (1 - own, down_send)):
                out[...] = jnp.concatenate([quarter(down, q), quarter(down, q + 2)], axis=2)


def join_in_kernel(own, from_x, from_y, from_d, out):
    rows = own.shape[1]
    for j in range(3):
        for k, part in enumerate((own, from_x, from_y, from_d)):
            base = (4 * j + k) * rows
            out[base : base + rows, :] = part[j]


def join_down_kernel(keep, got, out):
    rows, width = keep.shape[1:]
    for j in range(3):
        lanes = slice(j * width, (j + 1) * width)
        out[:rows, lanes] = keep[j]
        out[rows : 2 * rows, lanes] = got[j]
        out[2 * rows :, lanes] = got[j, 256 - rows :]


def gate_up_kernel(received, weights, pre):
    masks = [row_mask(256, j) for j in range(3)]
    for r in range(0, received.shape[0], 8):
        rows = received[r : r + 8].reshape(256, received.shape[2])
        total = jnp.dot(spread_experts(rows, masks), weights[...], preferred_element_type=f32)
        pre[r * SLOTS // 256] = total.astype(bf16)


def hidden_kernel(parts, out):
    total = jnp.sum(parts[...].astype(f32), axis=0)
    half = total.shape[1] // 2
    gate, up = total[:, :half], total[:, half:]
    hidden = gate / (1.0 + jnp.exp(-gate)) * up
    hidden = jnp.concatenate([hidden[:128], hidden[128:]], axis=1).astype(bf16)
    for n in range(out.shape[0]):
        out[n] = hidden


def down_kernel(hidden, weights, out):
    masks = [row_mask(256, j) for j in range(3)]
    half = hidden.shape[2] // 2
    for r in range(0, hidden.shape[0], 2):
        first, second = hidden[r], hidden[r + 1]
        rows = jnp.concatenate(
            [
                jnp.concatenate([first[:, :half], second[:, :half]], axis=1),
                jnp.concatenate([first[:, half:], second[:, half:]], axis=1),
            ],
            axis=0,
        )
        total = nt_dot(spread_experts(rows, masks), weights[...])
        for n in range(256 // SLOTS):
            store_packed(out, r * 128 // SLOTS + n, total[n * SLOTS : (n + 1) * SLOTS])


def combine_kernel(weighting, returned, order, stream, keep, send):
    width = keep.shape[1]
    rows = jnp.concatenate([load_packed(returned, n) for n in range(returned.shape[0])], axis=0)
    top = weighting[...].astype(bf16)
    rest = (weighting[...] - top.astype(f32)).astype(bf16)
    mixture = jnp.dot(top, rows, preferred_element_type=f32) + jnp.dot(
        rest, rows, preferred_element_type=f32
    )
    tail = mixture[:, 256:320] + mixture[:, 320:384]
    kept = jnp.dot(order[...], stream[:, 4 * width : 5 * width], preferred_element_type=f32)
    keep[...] = kept + mixture[:, :width]
    send[...] = jnp.concatenate([mixture[:, width:256], tail], axis=1).astype(bf16)


def call(kernel, outs, scratch=(), smem_first=False, count=0):
    specs = [pl.BlockSpec(memory_space=pltpu.VMEM)] * count
    if smem_first:
        specs[0] = pl.BlockSpec(memory_space=pltpu.SMEM)
    out_specs = [pl.BlockSpec(memory_space=pltpu.VMEM)] * len(outs)
    single = len(outs) == 1
    return pl.pallas_call(
        kernel,
        in_specs=specs,
        out_specs=out_specs[0] if single else out_specs,
        out_shape=outs[0] if single else outs,
        scratch_shapes=list(scratch),
        compiler_params=BIG_VMEM,
    )


def sds(shape, dtype):
    return jax.ShapeDtypeStruct(shape, dtype)


def on_device(
    queries,
    latent,
    segment_ids,
    value_up,
    out_proj,
    residual,
    norm_gain,
    route_ids,
    route_gates,
    expert_gate,
    expert_up,
    expert_down,
):
    block_len, local_heads, width_key = queries.shape
    width_model = residual.shape[1]
    width_out = width_model // 16
    width_pair = 2 * width_out
    ff = expert_gate.shape[2]
    ff_half = ff // 2
    y = lax.axis_index(YS)
    yl, xl, xh, core = (lax.axis_index(a) for a in ("yl", "xl", "xh", "core"))
    half = block_len // 2

    segment_axis = jnp.arange(SEGMENTS, dtype=i32)
    own_segment = segment_ids[:, None] == segment_axis[None, :]
    pad = KEYW - width_key - SEGMENTS
    keys_own = call(keys_kernel, [sds((KEYW, block_len), bf16)], count=2)(
        latent.T, segment_ids[None, :]
    )
    mine = lax.dynamic_slice_in_dim(keys_own, core * half, half, 1)

    def along_y(near, far):
        pairs = [
            (2 * i + h, 2 * ((i + (near, far)[h]) % 8) + h) for i in range(8) for h in range(2)
        ]
        return lax.ppermute(mine, YS + ("xh",), pairs)

    column = jnp.stack([along_y(1, 2), along_y(3, 4)])
    to_other = jnp.where(
        (xl == 0) & (xh == 1), jnp.stack([mine, column[0]]), column
    )
    diagonal = [(0, 3), (1, 2), (2, 1), (3, 0)]
    pieces = [
        column,
        lax.ppermute(column, "xh", SWAP),
        lax.ppermute(to_other, "xl", SWAP),
        lax.ppermute(to_other, ("xl", "xh"), diagonal),
    ]

    def blocks_of(x, h):
        return [2 * (y - 1 - h) + x, 2 * (y - 3 - h) + x]

    def blocks_sent(x, h):
        near, far = blocks_of(x, h)
        odd = (x == 0) & (h == 1)
        return [jnp.where(odd, 2 * y, near), jnp.where(odd, near, far)]

    info = jnp.stack(
        blocks_of(xl, xh)
        + blocks_of(xl, 1 - xh)
        + blocks_sent(1 - xl, xh)
        + blocks_sent(1 - xl, 1 - xh)
        + [core, xl, 2 * yl + xl]
    ).astype(i32)

    masks = jnp.where(own_segment, 0.0, -FAR).astype(bf16)
    query_rows = jnp.concatenate(
        [
            queries,
            jnp.broadcast_to(masks[:, None, :], (block_len, local_heads, SEGMENTS)),
            jnp.zeros((block_len, local_heads, pad), bf16),
        ],
        axis=2,
    )
    query_rows = query_rows.reshape(16, 2, 8, local_heads, KEYW).transpose(3, 1, 0, 2, 4)
    query_rows = query_rows.reshape(local_heads, block_len, KEYW)
    state_out = [
        sds((2, 256, 128), f32),
        sds((2, 256, 128), f32),
        sds((2, 256, LATENT), f32),
    ]
    state = call(
        first_attention_kernel, state_out, [pltpu.VMEM((256, 2 * 256), f32)], True, 4
    )(info, query_rows, keys_own, column)
    pieces[1], column_late, peak = lax.optimization_barrier((pieces[1], column, state[0]))
    state = [peak] + list(state[1:])
    first_other = lax.ppermute(column_late, "core", SWAP)
    quarter_out = sds((3, width_out, 2 * (ff // 4)), bf16)
    in_keep, *in_sends, down_keep, down_send = call(
        split_weights_kernel, [quarter_out] * 6, (), True, 4
    )(info, expert_gate, expert_up, jnp.transpose(expert_down, (0, 2, 1)))
    *pieces, first_other, in_sends[0] = lax.optimization_barrier(
        (*pieces, first_other, in_sends[0])
    )
    three = call(gather_kernel, [sds((6, KEYW, half), bf16)], count=3)(*pieces[1:])
    others = lax.ppermute(three, "core", SWAP)
    state = call(
        second_attention_kernel, state_out, [pltpu.VMEM((256, 4 * 256), f32)], True, 9
    )(info, query_rows, pieces[1], pieces[2], pieces[3], first_other, *state)
    send, keep = call(
        last_attention_kernel,
        [sds((half, width_model), bf16), sds((half, width_model), f32)],
        [pltpu.VMEM((256, 3 * 256), f32), pltpu.VMEM((2, 256, VDIM), bf16)],
        True,
        8,
    )(info, query_rows, others, *state, value_up, out_proj)
    got = lax.ppermute(send, "core", SWAP)
    pair_sum = call(add_kernel, [sds((16, 8, width_model), bf16)], count=2)(keep, got)

    pair_sum, send_x, send_y, send_d = lax.optimization_barrier((pair_sum, *in_sends))
    in_parts = [
        in_keep,
        lax.ppermute(send_x, "xl", SWAP),
        lax.ppermute(send_y, "yl", SWAP),
        lax.ppermute(send_d, ("yl", "xl"), diagonal),
    ]

    spread = lax.all_to_all(pair_sum, ("z", "xh"), split_axis=0, concat_axis=0, tiled=True)
    spread, down_send, *in_parts = lax.optimization_barrier((spread, down_send, *in_parts))
    down_got = lax.ppermute(down_send, "xl", SWAP)
    packed = call(norm_kernel, [sds((16, 8, 896), bf16)], count=3)(
        spread, residual, norm_gain[None, :]
    )
    split = lax.all_to_all(packed, CTX, split_axis=0, concat_axis=0, tiled=True)
    split, down_got = lax.optimization_barrier((split, down_got))
    split = split.reshape(128, 896)
    w_in = call(join_in_kernel, [sds((12 * width_out, ff // 2), bf16)], count=4)(*in_parts)
    w_down = call(join_down_kernel, [sds((384, 3 * ff_half), bf16)], count=2)(down_keep, down_got)

    routes = jnp.transpose(route_ids, (1, 0, 2)).reshape(128, TOPK)
    expert_axis = jnp.arange(EXPERTS, dtype=i32)
    named = jnp.any(routes[:, :, None] == expert_axis[None, None, :], axis=1)
    earlier_tokens = jnp.tril(jnp.ones((128, 128), bf16), -1)
    slot_all = jnp.dot(earlier_tokens, named.astype(bf16), preferred_element_type=f32).astype(i32)
    slot_of = jnp.sum(
        jnp.where(routes[:, :, None] == expert_axis[None, None, :], slot_all[:, None, :], 0), axis=2
    )
    target = (routes // 3) * SLOTS + (routes % 3) * CAP + slot_of
    slot_axis = jnp.arange(32 * SLOTS, dtype=i32)
    picker = jnp.any(target.T[None, :, :] == slot_axis[:, None, None], axis=1).astype(bf16)
    order = jnp.arange(128, dtype=i32)
    back_order = ((order % 16) * 8 + order // 16)[:, None] == order[None, :]
    target_rb = jnp.transpose(target.reshape(16, 8, TOPK), (1, 0, 2)).reshape(128, TOPK)
    gates_rb = route_gates.reshape(128, TOPK)
    weighting = jnp.sum(
        jnp.where(target_rb[:, :, None] == slot_axis[None, None, :], gates_rb[:, :, None], 0.0),
        axis=1,
    )

    travel = sds((32, 80, 128), bf16)
    outgoing = call(pick_kernel, [sds((32, SLOTS, 4 * width_out), bf16)], count=2)(picker, split)
    received = lax.all_to_all(outgoing, EXP, split_axis=0, concat_axis=0, tiled=True)
    received, w_in, w_down = lax.optimization_barrier((received, w_in, w_down))
    pre = call(gate_up_kernel, [sds((4, 256, ff // 2), bf16)], count=2)(received, w_in)
    pre_parts = lax.all_to_all(pre, "yh", split_axis=0, concat_axis=0, tiled=True)
    hidden = call(hidden_kernel, [sds((8, 128, ff_half), bf16)], count=1)(pre_parts)
    hidden_all = lax.all_to_all(hidden, YS, split_axis=0, concat_axis=0, tiled=True)
    expert_out = call(down_kernel, [travel], count=2)(
        hidden_all, w_down
    )
    returned = lax.all_to_all(expert_out, EXP, split_axis=0, concat_axis=0, tiled=True)
    mix_keep, mix_send = call(
        combine_kernel, [sds((128, width_out), f32), sds((128, width_out), bf16)], count=4
    )(weighting, returned, back_order.astype(bf16), split)
    mix_got = lax.ppermute(mix_send, "xl", SWAP)
    result = (mix_keep + mix_got.astype(f32)).astype(bf16)
    return result.reshape(8, 16, width_out)


def solution(mesh):
    grid = Mesh(mesh.devices.reshape(4, 2, 2, 8, 2, 2), ("yh", "yl", "xl", "z", "xh", "core"))
    return jax.shard_map(
        on_device,
        mesh=grid,
        in_specs=(
            P(CTX, EXP, None),
            P(CTX, None),
            P(CTX),
            P(EXP, None, None),
            P(EXP, None),
            P(CTX + EXP, None),
            P(),
            P(EXP, None, None),
            P(EXP, None, None),
            P(EXP, CTX, None),
            P(EXP, CTX, None),
            P(EXP, None, CTX),
        ),
        out_specs=P(EXP, None, CTX),
        check_vma=False,
    )
```

```python
import jax
import jax.numpy as jnp
from jax import lax
from jax.experimental import pallas as pl
from jax.experimental.pallas import tpu as pltpu
from jax.sharding import Mesh, PartitionSpec as P

LATENT = 512
VDIM = 128
QKDIM = 192
EXPERTS = 96
TOPK = 6
CAP = 10
SLOTS = 32
SEGMENTS = 8
KEYW = 592
FAR = float(2**20)

CTX = ("y", "xl")
EXP = ("z", "xh", "core")
SWAP = [(0, 1), (1, 0)]
BIG_VMEM = pltpu.CompilerParams(vmem_limit_bytes=20 * 2**20)
f32, bf16, i32 = jnp.float32, jnp.bfloat16, jnp.int32


def keys_kernel(latent, segments, own):
    width, tokens = latent.shape
    own[:width, :] = latent[...]
    mark = lax.broadcasted_iota(i32, (KEYW - width, tokens), 0)
    own[width:, :] = jnp.where(segments[...] == mark, 1.0, 0.0).astype(bf16)


def keys_of(chunk):
    return chunk[...] if len(chunk.shape) == 2 else jnp.concatenate([chunk[0], chunk[1]], axis=1)


def nt_dot(a, b):
    return lax.dot_general(a, b, (((1,), (1,)), ((), ())), preferred_element_type=f32)


def attend_chunks(rows, chunks, biases, scores, old):
    scale = QKDIM ** (-0.5)
    count = rows.shape[0]
    peak = jnp.full((count, 128), -FAR, f32) if old is None else old[0]
    for n, (chunk, bias) in enumerate(zip(chunks, biases)):
        part = bias(jnp.dot(rows, keys_of(chunk), preferred_element_type=f32) * scale)
        scores[:, n * 256 : (n + 1) * 256] = part
        peak = jnp.maximum(peak, jnp.maximum(part[:, :128], part[:, 128:]))
    peak = jnp.max(peak, axis=1, keepdims=True)
    if old is None:
        sums, mixed = jnp.zeros((count, 128), f32), jnp.zeros((count, LATENT), f32)
    else:
        factor = jnp.exp(old[0][:, :1] - peak)
        sums, mixed = old[1] * factor, old[2] * factor
    for n, chunk in enumerate(chunks):
        terms = jnp.exp(scores[:, n * 256 : (n + 1) * 256] - peak)
        sums = sums + terms[:, :128] + terms[:, 128:]
        mixed = mixed + nt_dot(terms.astype(bf16), keys_of(chunk)[:LATENT])
    return jnp.broadcast_to(peak, (count, 128)), sums, mixed


def valid_bias(info, piece):
    def bias(part):
        lane = lax.broadcasted_iota(i32, (1, 256), 1)
        first = jnp.where(info[2 * piece] >= 0, 0.0, -FAR)
        second = jnp.where(info[2 * piece + 1] >= 0, 0.0, -FAR)
        return part + jnp.where(lane < 128, first, second)

    return bias


def causal_bias(part):
    lane = lax.broadcasted_iota(i32, part.shape, 1)
    row = lax.broadcasted_iota(i32, part.shape, 0)
    token = (row % 128) // 8 * 16 + row // 128 % 2 * 8 + row % 8
    return jnp.where(lane <= token, part, -FAR)


def first_attention_kernel(query, own, peak, sums, mixed, scores):
    peak[...], sums[...], mixed[...] = attend_chunks(
        query[...], [own], [causal_bias], scores, None
    )


def second_attention_kernel(
    info, query, p0, p1, p2, p3, o0, old_peak, old_sums, old_mixed, peak, sums, mixed, scores
):
    old = old_peak[...], old_sums[...], old_mixed[...]
    biases = [valid_bias(info, n) for n in (0, 1, 2, 3, 0)]
    peak[...], sums[...], mixed[...] = attend_chunks(
        query[...], [p0, p1, p2, p3, o0], biases, scores, old
    )


def last_attention_kernel(
    info, query, others, old_peak, old_sums, old_mixed, value_up, out_proj, send, keep, scores, values
):
    core = info[8]
    old = old_peak[...], old_sums[...], old_mixed[...]
    chunks = [others.at[2 * n : 2 * n + 2] for n in range(3)]
    biases = [valid_bias(info, n) for n in (1, 2, 3)]
    _, sums, mixed = attend_chunks(query[...], chunks, biases, scores, old)
    mixed = (mixed / jnp.sum(sums, axis=1, keepdims=True)).astype(bf16)
    for head in range(2):
        rows = mixed[head * 256 : (head + 1) * 256]
        values[head] = jnp.dot(rows, value_up[head], preferred_element_type=f32).astype(bf16)

    def project(which, out):
        start = pl.multiple_of(which * 128, 128)
        both = jnp.concatenate([values[head, pl.ds(start, 128), :] for head in range(2)], axis=1)
        for c in range(0, out.shape[1], 640):
            out[:, c : c + 640] = jnp.dot(
                both, out_proj[:, c : c + 640], preferred_element_type=f32
            ).astype(out.dtype)

    project(1 - core, send)
    project(core, keep)


def add_kernel(keep, got, out):
    out[...] = (keep[...] + got[...].astype(f32)).reshape(out.shape).astype(bf16)


def gather_kernel(p1, p2, p3, out):
    for n, piece in enumerate((p1, p2, p3)):
        out[2 * n : 2 * n + 2] = piece[...]


def norm_kernel(spread, residual, gain, packed):
    attended = jnp.sum(spread[...].astype(f32), axis=0)
    stream = (residual[...].astype(f32) + attended).astype(bf16).astype(f32)
    mean_sq = jnp.mean(stream * stream, axis=1, keepdims=True)
    normed = (stream * lax.rsqrt(mean_sq + 1e-06) * gain[...]).astype(bf16).astype(f32)
    width = stream.shape[1] // 16
    fill = jnp.zeros((stream.shape[0], packed.shape[2] - 3 * width), f32)
    for c in range(16):
        mine, other = c * width, (c ^ 1) * width
        packed[c] = jnp.concatenate(
            [
                normed[:, mine : mine + width],
                normed[:, other : other + width],
                stream[:, mine : mine + width],
                fill,
            ],
            axis=1,
        ).astype(bf16)


def store_packed(out, n, rows):
    left = lax.broadcasted_iota(i32, (SLOTS // 2, 128), 1) < 64
    out[n, 0:32] = rows[:, :128].astype(bf16)
    out[n, 32:64] = rows[:, 128:256].astype(bf16)
    out[n, 64:80] = jnp.where(left, rows[:16, 256:], rows[16:, 256:]).astype(bf16)


def load_packed(ref, n):
    last = ref[n, 64:80]
    left = jnp.where(lax.broadcasted_iota(i32, (1, 128), 1) < 64, 1.0, 0.0).astype(bf16)
    last = jnp.concatenate([last * left, last * (1 - left)], axis=0)
    return jnp.concatenate([ref[n, 0:32], ref[n, 32:64], last], axis=1)


def pick_kernel(picker, split, out):
    values = split[:, :384]
    doubled = jnp.concatenate([values[:, :320], values[:, 256:320]], axis=1)
    for r in range(0, picker.shape[0], 256):
        rows = jnp.dot(picker[r : r + 256, :], doubled, preferred_element_type=f32)
        for n in range(256 // SLOTS):
            store_packed(out, r // SLOTS + n, rows[n * SLOTS : (n + 1) * SLOTS])


def row_mask(count, j):
    slot = lax.broadcasted_iota(i32, (count, 1), 0) % SLOTS
    return jnp.where((slot >= j * CAP) & (slot < (j + 1) * CAP), 1.0, 0.0).astype(bf16)


def spread_experts(rows, masks):
    return jnp.concatenate([rows * mask for mask in masks], axis=1)


def split_weights_kernel(info, gate, up, down, in_send, in_keep, down_send, down_keep):
    half = gate.shape[2] // 2

    def move(into, onto, start):
        into[:, :, :half] = gate[:, :, start : start + half]
        into[:, :, half:] = up[:, :, start : start + half]
        onto[...] = down[:, :, start : start + half]

    @pl.when(info[9] == 0)
    def _():
        move(in_keep, down_keep, 0)
        move(in_send, down_send, half)

    @pl.when(info[9] != 0)
    def _():
        move(in_keep, down_keep, half)
        move(in_send, down_send, 0)


def join_in_kernel(keep, got, out):
    rows = keep.shape[1]
    for j in range(3):
        base = j * 384
        out[base : base + rows, :] = keep[j]
        out[base + rows : base + 2 * rows, :] = got[j]
        out[base + 2 * rows : base + 384, :] = got[j, 256 - rows :]


def join_down_kernel(keep, got, out):
    rows, width = keep.shape[1:]
    for j in range(3):
        lanes = slice(j * width, (j + 1) * width)
        out[:rows, lanes] = keep[j]
        out[rows : 2 * rows, lanes] = got[j]
        out[2 * rows :, lanes] = got[j, 256 - rows :]


def gate_up_kernel(received, weights, pre):
    masks = [row_mask(256, j) for j in range(3)]
    for r in range(0, received.shape[0], 8):
        rows = jnp.concatenate([load_packed(received, r + n) for n in range(8)], axis=0)
        total = jnp.dot(spread_experts(rows, masks), weights[...], preferred_element_type=f32)
        pre[r * SLOTS : (r + 8) * SLOTS, :] = total.astype(bf16)


def hidden_kernel(parts, out):
    total = jnp.sum(parts[...].astype(f32), axis=0)
    half = total.shape[1] // 2
    gate, up = total[:, :half], total[:, half:]
    hidden = (gate / (1.0 + jnp.exp(-gate)) * up).astype(bf16)
    for n in range(out.shape[0]):
        out[n] = hidden


def down_kernel(hidden, weights, out):
    masks = [row_mask(256, j) for j in range(3)]
    for r in range(0, hidden.shape[0], 256):
        rows = spread_experts(hidden[r : r + 256, :], masks)
        total = nt_dot(rows, weights[...])
        for n in range(256 // SLOTS):
            store_packed(out, r // SLOTS + n, total[n * SLOTS : (n + 1) * SLOTS])


def combine_kernel(weighting, returned, order, stream, keep, send):
    width = keep.shape[1]
    rows = jnp.concatenate([load_packed(returned, n) for n in range(returned.shape[0])], axis=0)
    top = weighting[...].astype(bf16)
    rest = (weighting[...] - top.astype(f32)).astype(bf16)
    mixture = jnp.dot(top, rows, preferred_element_type=f32) + jnp.dot(
        rest, rows, preferred_element_type=f32
    )
    tail = mixture[:, 256:320] + mixture[:, 320:384]
    kept = jnp.dot(order[...], stream[:, 2 * width : 3 * width], preferred_element_type=f32)
    keep[...] = kept + mixture[:, :width]
    send[...] = jnp.concatenate([mixture[:, width:256], tail], axis=1).astype(bf16)


def call(kernel, outs, scratch=(), smem_first=False, count=0):
    specs = [pl.BlockSpec(memory_space=pltpu.VMEM)] * count
    if smem_first:
        specs[0] = pl.BlockSpec(memory_space=pltpu.SMEM)
    out_specs = [pl.BlockSpec(memory_space=pltpu.VMEM)] * len(outs)
    single = len(outs) == 1
    return pl.pallas_call(
        kernel,
        in_specs=specs,
        out_specs=out_specs[0] if single else out_specs,
        out_shape=outs[0] if single else outs,
        scratch_shapes=list(scratch),
        compiler_params=BIG_VMEM,
    )


def sds(shape, dtype):
    return jax.ShapeDtypeStruct(shape, dtype)


def on_device(
    queries,
    latent,
    segment_ids,
    value_up,
    out_proj,
    residual,
    norm_gain,
    route_ids,
    route_gates,
    expert_gate,
    expert_up,
    expert_down,
):
    block_len, local_heads, width_key = queries.shape
    width_model = residual.shape[1]
    width_out = width_model // 16
    width_pair = 2 * width_out
    ff = expert_gate.shape[2]
    ff_half = ff // 2
    y, xl, xh, core = (lax.axis_index(a) for a in ("y", "xl", "xh", "core"))
    half = block_len // 2

    segment_axis = jnp.arange(SEGMENTS, dtype=i32)
    own_segment = segment_ids[:, None] == segment_axis[None, :]
    pad = KEYW - width_key - SEGMENTS
    keys_own = call(keys_kernel, [sds((KEYW, block_len), bf16)], count=2)(
        latent.T, segment_ids[None, :]
    )
    mine = lax.dynamic_slice_in_dim(keys_own, core * half, half, 1)

    def along_y(near, far):
        pairs = [
            (2 * i + h, 2 * ((i + (near, far)[h]) % 8) + h) for i in range(8) for h in range(2)
        ]
        return lax.ppermute(mine, ("y", "xh"), pairs)

    near, far = along_y(1, 2), along_y(3, 4)

    def blocks_of(x, h):
        return [2 * (y - 1 - h) + x, 2 * (y - 3 - h) + x]

    def blocks_sent(x, h):
        near, far = blocks_of(x, h)
        odd = (x == 0) & (h == 1)
        return [jnp.where(odd, 2 * y, near), jnp.where(odd, near, far)]

    info = jnp.stack(
        blocks_of(xl, xh)
        + blocks_of(xl, 1 - xh)
        + blocks_sent(1 - xl, xh)
        + blocks_sent(1 - xl, 1 - xh)
        + [core, xl]
    ).astype(i32)

    masks = jnp.where(own_segment, 0.0, -FAR).astype(bf16)
    query_rows = jnp.concatenate(
        [
            queries,
            jnp.broadcast_to(masks[:, None, :], (block_len, local_heads, SEGMENTS)),
            jnp.zeros((block_len, local_heads, pad), bf16),
        ],
        axis=2,
    )
    query_rows = query_rows.reshape(16, 2, 8, local_heads, KEYW).transpose(3, 1, 0, 2, 4)
    query_rows = query_rows.reshape(local_heads * block_len, KEYW)
    rows_all = local_heads * block_len
    state_out = [
        sds((rows_all, 128), f32),
        sds((rows_all, 128), f32),
        sds((rows_all, LATENT), f32),
    ]
    state = call(
        first_attention_kernel, state_out, [pltpu.VMEM((rows_all, 256), f32)], count=2
    )(query_rows, keys_own)

    in_out = sds((3, width_out, 2 * ff_half), bf16)
    down_out = sds((3, width_out, ff_half), bf16)
    in_send, in_keep, down_send, down_keep = call(
        split_weights_kernel, [in_out, in_out, down_out, down_out], (), True, 4
    )(info, expert_gate, expert_up, jnp.transpose(expert_down, (0, 2, 1)))
    near, far, peak, in_send = lax.optimization_barrier((near, far, state[0], in_send))
    state = [peak] + list(state[1:])

    column = jnp.stack([near, far])
    to_other = jnp.where(
        (xl == 0) & (xh == 1), jnp.stack([mine, column[0]]), column
    )
    diagonal = [(0, 3), (1, 2), (2, 1), (3, 0)]
    pieces = [
        column,
        lax.ppermute(column, "xh", SWAP),
        lax.ppermute(to_other, "xl", SWAP),
        lax.ppermute(to_other, ("xl", "xh"), diagonal),
    ]

    pieces[1], column_late = lax.optimization_barrier((pieces[1], column))
    first_other = lax.ppermute(column_late, "core", SWAP)
    *pieces, first_other = lax.optimization_barrier((*pieces, first_other))
    three = call(gather_kernel, [sds((6, KEYW, half), bf16)], count=3)(*pieces[1:])
    others = lax.ppermute(three, "core", SWAP)
    state = call(
        second_attention_kernel, state_out, [pltpu.VMEM((rows_all, 5 * 256), f32)], True, 10
    )(info, query_rows, *pieces, first_other, *state)
    send, keep = call(
        last_attention_kernel,
        [sds((half, width_model), bf16), sds((half, width_model), f32)],
        [pltpu.VMEM((rows_all, 3 * 256), f32), pltpu.VMEM((2, 256, VDIM), bf16)],
        True,
        8,
    )(info, query_rows, others, *state, value_up, out_proj)
    got = lax.ppermute(send, "core", SWAP)
    pair_sum = call(add_kernel, [sds((16, 8, width_model), bf16)], count=2)(keep, got)

    pair_sum, in_send = lax.optimization_barrier((pair_sum, in_send))
    in_got = lax.ppermute(in_send, "xl", SWAP)

    spread = lax.all_to_all(pair_sum, ("z", "xh"), split_axis=0, concat_axis=0, tiled=True)
    packed = call(norm_kernel, [sds((16, 8, 512), bf16)], count=3)(
        spread, residual, norm_gain[None, :]
    )
    split = lax.all_to_all(packed, CTX, split_axis=0, concat_axis=0, tiled=True)
    in_got, down_send = lax.optimization_barrier((in_got, down_send))
    down_got = lax.ppermute(down_send, "xl", SWAP)
    split, in_got = lax.optimization_barrier((split, in_got))
    split = split.reshape(128, 512)
    w_in = call(join_in_kernel, [sds((3 * 384, 2 * ff_half), bf16)], count=2)(in_keep, in_got)
    w_down = call(join_down_kernel, [sds((384, 3 * ff_half), bf16)], count=2)(down_keep, down_got)

    routes = jnp.transpose(route_ids, (1, 0, 2)).reshape(128, TOPK)
    expert_axis = jnp.arange(EXPERTS, dtype=i32)
    named = jnp.any(routes[:, :, None] == expert_axis[None, None, :], axis=1)
    earlier_tokens = jnp.tril(jnp.ones((128, 128), bf16), -1)
    slot_all = jnp.dot(earlier_tokens, named.astype(bf16), preferred_element_type=f32).astype(i32)
    slot_of = jnp.sum(
        jnp.where(routes[:, :, None] == expert_axis[None, None, :], slot_all[:, None, :], 0), axis=2
    )
    target = (routes // 3) * SLOTS + (routes % 3) * CAP + slot_of
    slot_axis = jnp.arange(32 * SLOTS, dtype=i32)
    picker = jnp.any(target.T[None, :, :] == slot_axis[:, None, None], axis=1).astype(bf16)
    order = jnp.arange(128, dtype=i32)
    back_order = ((order % 16) * 8 + order // 16)[:, None] == order[None, :]
    target_rb = jnp.transpose(target.reshape(16, 8, TOPK), (1, 0, 2)).reshape(128, TOPK)
    gates_rb = route_gates.reshape(128, TOPK)
    weighting = jnp.sum(
        jnp.where(target_rb[:, :, None] == slot_axis[None, None, :], gates_rb[:, :, None], 0.0),
        axis=1,
    )

    travel = sds((32, 80, 128), bf16)
    outgoing = call(pick_kernel, [travel], count=2)(picker, split)
    received = lax.all_to_all(outgoing, EXP, split_axis=0, concat_axis=0, tiled=True)
    received, w_in, w_down = lax.optimization_barrier((received, w_in, w_down))
    pre = call(gate_up_kernel, [sds((32 * SLOTS, 2 * ff_half), bf16)], count=2)(received, w_in)
    pre_parts = lax.all_to_all(
        pre.reshape(8, 128, 2 * ff_half), "y", split_axis=0, concat_axis=0, tiled=True
    )
    hidden = call(hidden_kernel, [sds((8, 128, ff_half), bf16)], count=1)(pre_parts)
    hidden_all = lax.all_to_all(hidden, "y", split_axis=0, concat_axis=0, tiled=True)
    expert_out = call(down_kernel, [travel], count=2)(
        hidden_all.reshape(32 * SLOTS, ff_half), w_down
    )
    returned = lax.all_to_all(expert_out, EXP, split_axis=0, concat_axis=0, tiled=True)
    mix_keep, mix_send = call(
        combine_kernel, [sds((128, width_out), f32), sds((128, width_out), bf16)], count=4
    )(weighting, returned, back_order.astype(bf16), split)
    mix_got = lax.ppermute(mix_send, "xl", SWAP)
    result = (mix_keep + mix_got.astype(f32)).astype(bf16)
    return result.reshape(8, 16, width_out)


def solution(mesh):
    grid = Mesh(mesh.devices.reshape(8, 2, 8, 2, 2), ("y", "xl", "z", "xh", "core"))
    return jax.shard_map(
        on_device,
        mesh=grid,
        in_specs=(
            P(CTX, EXP, None),
            P(CTX, None),
            P(CTX),
            P(EXP, None, None),
            P(EXP, None),
            P(CTX + EXP, None),
            P(),
            P(EXP, None, None),
            P(EXP, None, None),
            P(EXP, CTX, None),
            P(EXP, CTX, None),
            P(EXP, None, CTX),
        ),
        out_specs=P(EXP, None, CTX),
        check_vma=False,
    )
```

```python
import jax
import jax.numpy as jnp
from jax import lax
from jax.experimental import pallas as pl
from jax.experimental.pallas import tpu as pltpu
from jax.sharding import Mesh, PartitionSpec as P

LATENT = 512
VDIM = 128
QKDIM = 192
EXPERTS = 96
TOPK = 6
CAP = 10
SLOTS = 32
SEGMENTS = 8
KEYW = 592
FAR = float(2**20)

CTX = ("y", "xl")
EXP = ("z", "xh", "core")
SWAP = [(0, 1), (1, 0)]
BIG_VMEM = pltpu.CompilerParams(vmem_limit_bytes=20 * 2**20)
f32, bf16, i32 = jnp.float32, jnp.bfloat16, jnp.int32


def keys_kernel(latent, segments, own):
    width, tokens = latent.shape
    own[:width, :] = latent[...]
    mark = lax.broadcasted_iota(i32, (KEYW - width, tokens), 0)
    own[width:, :] = jnp.where(segments[...] == mark, 1.0, 0.0).astype(bf16)


def keys_of(chunk):
    return chunk[...] if len(chunk.shape) == 2 else jnp.concatenate([chunk[0], chunk[1]], axis=1)


def nt_dot(a, b):
    return lax.dot_general(a, b, (((1,), (1,)), ((), ())), preferred_element_type=f32)


def attend_chunks(rows, chunks, biases, scores, old):
    scale = QKDIM ** (-0.5)
    peak = jnp.full((256, 128), -FAR, f32) if old is None else old[0]
    for n, (chunk, bias) in enumerate(zip(chunks, biases)):
        part = bias(jnp.dot(rows, keys_of(chunk), preferred_element_type=f32) * scale)
        scores[:, n * 256 : (n + 1) * 256] = part
        peak = jnp.maximum(peak, jnp.maximum(part[:, :128], part[:, 128:]))
    peak = jnp.max(peak, axis=1, keepdims=True)
    if old is None:
        sums, mixed = jnp.zeros((256, 128), f32), jnp.zeros((256, LATENT), f32)
    else:
        factor = jnp.exp(old[0][:, :1] - peak)
        sums, mixed = old[1] * factor, old[2] * factor
    for n, chunk in enumerate(chunks):
        terms = jnp.exp(scores[:, n * 256 : (n + 1) * 256] - peak)
        sums = sums + terms[:, :128] + terms[:, 128:]
        mixed = mixed + nt_dot(terms.astype(bf16), keys_of(chunk)[:LATENT])
    return jnp.broadcast_to(peak, (256, 128)), sums, mixed


def valid_bias(info, piece):
    def bias(part):
        lane = lax.broadcasted_iota(i32, (256, 256), 1)
        first = jnp.where(info[2 * piece] >= 0, 0.0, -FAR)
        second = jnp.where(info[2 * piece + 1] >= 0, 0.0, -FAR)
        return part + jnp.where(lane < 128, first, second)

    return bias


def causal_bias(part):
    lane = lax.broadcasted_iota(i32, (256, 256), 1)
    row = lax.broadcasted_iota(i32, (256, 256), 0)
    token = (row % 128) // 8 * 16 + row // 128 * 8 + row % 8
    return jnp.where(lane <= token, part, -FAR)


def first_attention_kernel(info, query, own, p0, peak, sums, mixed, scores):
    @pl.loop(0, 2)
    def _(head):
        state = attend_chunks(
            query[head], [own, p0], [causal_bias, valid_bias(info, 0)], scores, None
        )
        peak[head], sums[head], mixed[head] = state


def second_attention_kernel(
    info, query, p1, p2, p3, o0, old_peak, old_sums, old_mixed, peak, sums, mixed, scores
):
    @pl.loop(0, 2)
    def _(head):
        old = old_peak[head], old_sums[head], old_mixed[head]
        biases = [valid_bias(info, n) for n in (1, 2, 3, 0)]
        state = attend_chunks(query[head], [p1, p2, p3, o0], biases, scores, old)
        peak[head], sums[head], mixed[head] = state


def last_attention_kernel(
    info, query, others, old_peak, old_sums, old_mixed, value_up, out_proj, send, keep, scores, values
):
    core = info[8]

    @pl.loop(0, 2)
    def _(head):
        old = old_peak[head], old_sums[head], old_mixed[head]
        chunks = [others.at[2 * n : 2 * n + 2] for n in range(3)]
        biases = [valid_bias(info, n) for n in (1, 2, 3)]
        _, sums, mixed = attend_chunks(query[head], chunks, biases, scores, old)
        mixed = (mixed / jnp.sum(sums, axis=1, keepdims=True)).astype(bf16)
        values[head] = jnp.dot(mixed, value_up[head], preferred_element_type=f32).astype(bf16)

    def project(which, out):
        start = pl.multiple_of(which * 128, 128)
        both = jnp.concatenate([values[head, pl.ds(start, 128), :] for head in range(2)], axis=1)
        for c in range(0, out.shape[1], 640):
            out[:, c : c + 640] = jnp.dot(
                both, out_proj[:, c : c + 640], preferred_element_type=f32
            ).astype(out.dtype)

    project(1 - core, send)
    project(core, keep)


def add_kernel(keep, got, out):
    out[...] = (keep[...] + got[...].astype(f32)).reshape(out.shape).astype(bf16)


def gather_kernel(p1, p2, p3, out):
    for n, piece in enumerate((p1, p2, p3)):
        out[2 * n : 2 * n + 2] = piece[...]


def norm_kernel(spread, residual, gain, packed):
    attended = jnp.sum(spread[...].astype(f32), axis=0)
    stream = (residual[...].astype(f32) + attended).astype(bf16).astype(f32)
    mean_sq = jnp.mean(stream * stream, axis=1, keepdims=True)
    normed = (stream * lax.rsqrt(mean_sq + 1e-06) * gain[...]).astype(bf16).astype(f32)
    width = stream.shape[1] // 16
    fill = jnp.zeros((stream.shape[0], packed.shape[2] - 3 * width), f32)
    for c in range(16):
        mine, other = c * width, (c ^ 1) * width
        packed[c] = jnp.concatenate(
            [
                normed[:, mine : mine + width],
                normed[:, other : other + width],
                stream[:, mine : mine + width],
                fill,
            ],
            axis=1,
        ).astype(bf16)


def store_packed(out, n, rows):
    left = lax.broadcasted_iota(i32, (SLOTS // 2, 128), 1) < 64
    out[n, 0:32] = rows[:, :128].astype(bf16)
    out[n, 32:64] = rows[:, 128:256].astype(bf16)
    out[n, 64:80] = jnp.where(left, rows[:16, 256:], rows[16:, 256:]).astype(bf16)


def load_packed(ref, n):
    last = ref[n, 64:80]
    left = jnp.where(lax.broadcasted_iota(i32, (1, 128), 1) < 64, 1.0, 0.0).astype(bf16)
    last = jnp.concatenate([last * left, last * (1 - left)], axis=0)
    return jnp.concatenate([ref[n, 0:32], ref[n, 32:64], last], axis=1)


def pick_kernel(picker, split, out):
    values = split[:, :384]
    doubled = jnp.concatenate([values[:, :320], values[:, 256:320]], axis=1)
    for r in range(0, picker.shape[0], 256):
        rows = jnp.dot(picker[r : r + 256, :], doubled, preferred_element_type=f32)
        for n in range(256 // SLOTS):
            store_packed(out, r // SLOTS + n, rows[n * SLOTS : (n + 1) * SLOTS])


def row_mask(count, j):
    slot = lax.broadcasted_iota(i32, (count, 1), 0) % SLOTS
    return jnp.where((slot >= j * CAP) & (slot < (j + 1) * CAP), 1.0, 0.0).astype(bf16)


def spread_experts(rows, masks):
    return jnp.concatenate([rows * mask for mask in masks], axis=1)


def split_weights_kernel(info, gate, up, down, in_send, in_keep, down_send, down_keep):
    half = gate.shape[2] // 2

    def move(into, onto, start):
        into[:, :, :half] = gate[:, :, start : start + half]
        into[:, :, half:] = up[:, :, start : start + half]
        onto[...] = down[:, :, start : start + half]

    @pl.when(info[9] == 0)
    def _():
        move(in_keep, down_keep, 0)
        move(in_send, down_send, half)

    @pl.when(info[9] != 0)
    def _():
        move(in_keep, down_keep, half)
        move(in_send, down_send, 0)


def join_in_kernel(keep, got, out):
    rows = keep.shape[1]
    for j in range(3):
        base = j * 384
        out[base : base + rows, :] = keep[j]
        out[base + rows : base + 2 * rows, :] = got[j]
        out[base + 2 * rows : base + 384, :] = got[j, 256 - rows :]


def join_down_kernel(keep, got, out):
    rows, width = keep.shape[1:]
    for j in range(3):
        lanes = slice(j * width, (j + 1) * width)
        out[:rows, lanes] = keep[j]
        out[rows : 2 * rows, lanes] = got[j]
        out[2 * rows :, lanes] = got[j, 256 - rows :]


def gate_up_kernel(received, weights, pre):
    masks = [row_mask(256, j) for j in range(3)]
    for r in range(0, received.shape[0], 8):
        rows = jnp.concatenate([load_packed(received, r + n) for n in range(8)], axis=0)
        total = jnp.dot(spread_experts(rows, masks), weights[...], preferred_element_type=f32)
        pre[r * SLOTS : (r + 8) * SLOTS, :] = total.astype(bf16)


def hidden_kernel(parts, out):
    total = jnp.sum(parts[...].astype(f32), axis=0)
    half = total.shape[1] // 2
    gate, up = total[:, :half], total[:, half:]
    hidden = (gate / (1.0 + jnp.exp(-gate)) * up).astype(bf16)
    for n in range(out.shape[0]):
        out[n] = hidden


def down_kernel(hidden, weights, out):
    masks = [row_mask(256, j) for j in range(3)]
    for r in range(0, hidden.shape[0], 256):
        rows = spread_experts(hidden[r : r + 256, :], masks)
        total = nt_dot(rows, weights[...])
        for n in range(256 // SLOTS):
            store_packed(out, r // SLOTS + n, total[n * SLOTS : (n + 1) * SLOTS])


def combine_kernel(weighting, returned, order, stream, keep, send):
    width = keep.shape[1]
    rows = jnp.concatenate([load_packed(returned, n) for n in range(returned.shape[0])], axis=0)
    top = weighting[...].astype(bf16)
    rest = (weighting[...] - top.astype(f32)).astype(bf16)
    mixture = jnp.dot(top, rows, preferred_element_type=f32) + jnp.dot(
        rest, rows, preferred_element_type=f32
    )
    tail = mixture[:, 256:320] + mixture[:, 320:384]
    kept = jnp.dot(order[...], stream[:, 2 * width : 3 * width], preferred_element_type=f32)
    keep[...] = kept + mixture[:, :width]
    send[...] = jnp.concatenate([mixture[:, width:256], tail], axis=1).astype(bf16)


def call(kernel, outs, scratch=(), smem_first=False, count=0):
    specs = [pl.BlockSpec(memory_space=pltpu.VMEM)] * count
    if smem_first:
        specs[0] = pl.BlockSpec(memory_space=pltpu.SMEM)
    out_specs = [pl.BlockSpec(memory_space=pltpu.VMEM)] * len(outs)
    single = len(outs) == 1
    return pl.pallas_call(
        kernel,
        in_specs=specs,
        out_specs=out_specs[0] if single else out_specs,
        out_shape=outs[0] if single else outs,
        scratch_shapes=list(scratch),
        compiler_params=BIG_VMEM,
    )


def sds(shape, dtype):
    return jax.ShapeDtypeStruct(shape, dtype)


def on_device(
    queries,
    latent,
    segment_ids,
    value_up,
    out_proj,
    residual,
    norm_gain,
    route_ids,
    route_gates,
    expert_gate,
    expert_up,
    expert_down,
):
    block_len, local_heads, width_key = queries.shape
    width_model = residual.shape[1]
    width_out = width_model // 16
    width_pair = 2 * width_out
    ff = expert_gate.shape[2]
    ff_half = ff // 2
    y, xl, xh, core = (lax.axis_index(a) for a in ("y", "xl", "xh", "core"))
    half = block_len // 2

    segment_axis = jnp.arange(SEGMENTS, dtype=i32)
    own_segment = segment_ids[:, None] == segment_axis[None, :]
    pad = KEYW - width_key - SEGMENTS
    keys_own = call(keys_kernel, [sds((KEYW, block_len), bf16)], count=2)(
        latent.T, segment_ids[None, :]
    )
    mine = lax.dynamic_slice_in_dim(keys_own, core * half, half, 1)

    def along_y(near, far):
        pairs = [
            (2 * i + h, 2 * ((i + (near, far)[h]) % 8) + h) for i in range(8) for h in range(2)
        ]
        return lax.ppermute(mine, ("y", "xh"), pairs)

    far = along_y(3, 4)
    near = along_y(1, 2)
    column = jnp.stack([far, near])
    to_other = jnp.where(
        (xl == 0) & (xh == 1), jnp.stack([mine, near]), column
    )
    diagonal = [(0, 3), (1, 2), (2, 1), (3, 0)]
    pieces = [
        column,
        lax.ppermute(column, "xh", SWAP),
        lax.ppermute(to_other, "xl", SWAP),
        lax.ppermute(to_other, ("xl", "xh"), diagonal),
    ]

    def blocks_of(x, h):
        return [2 * (y - 3 - h) + x, 2 * (y - 1 - h) + x]

    def blocks_sent(x, h):
        late, early = blocks_of(x, h)
        odd = (x == 0) & (h == 1)
        return [jnp.where(odd, 2 * y, late), early]

    info = jnp.stack(
        blocks_of(xl, xh)
        + blocks_of(xl, 1 - xh)
        + blocks_sent(1 - xl, xh)
        + blocks_sent(1 - xl, 1 - xh)
        + [core, xl]
    ).astype(i32)

    masks = jnp.where(own_segment, 0.0, -FAR).astype(bf16)
    query_rows = jnp.concatenate(
        [
            queries,
            jnp.broadcast_to(masks[:, None, :], (block_len, local_heads, SEGMENTS)),
            jnp.zeros((block_len, local_heads, pad), bf16),
        ],
        axis=2,
    )
    query_rows = query_rows.reshape(16, 2, 8, local_heads, KEYW).transpose(3, 1, 0, 2, 4)
    query_rows = query_rows.reshape(local_heads, block_len, KEYW)
    state_out = [
        sds((2, 256, 128), f32),
        sds((2, 256, 128), f32),
        sds((2, 256, LATENT), f32),
    ]
    state = call(
        first_attention_kernel, state_out, [pltpu.VMEM((256, 2 * 256), f32)], True, 4
    )(info, query_rows, keys_own, column)
    pieces[1], column_late, peak = lax.optimization_barrier((pieces[1], column, state[0]))
    state = [peak] + list(state[1:])
    first_other = lax.ppermute(column_late, "core", SWAP)
    *pieces, first_other = lax.optimization_barrier((*pieces, first_other))
    three = call(gather_kernel, [sds((6, KEYW, half), bf16)], count=3)(*pieces[1:])
    others = lax.ppermute(three, "core", SWAP)
    state = call(
        second_attention_kernel, state_out, [pltpu.VMEM((256, 4 * 256), f32)], True, 9
    )(info, query_rows, pieces[1], pieces[2], pieces[3], first_other, *state)
    send, keep = call(
        last_attention_kernel,
        [sds((half, width_model), bf16), sds((half, width_model), f32)],
        [pltpu.VMEM((256, 3 * 256), f32), pltpu.VMEM((2, 256, VDIM), bf16)],
        True,
        8,
    )(info, query_rows, others, *state, value_up, out_proj)
    got = lax.ppermute(send, "core", SWAP)
    pair_sum = call(add_kernel, [sds((16, 8, width_model), bf16)], count=2)(keep, got)

    in_out = sds((3, width_out, 2 * ff_half), bf16)
    down_out = sds((3, width_out, ff_half), bf16)
    in_send, in_keep, down_send, down_keep = call(
        split_weights_kernel, [in_out, in_out, down_out, down_out], (), True, 4
    )(info, expert_gate, expert_up, jnp.transpose(expert_down, (0, 2, 1)))
    pair_sum, in_send = lax.optimization_barrier((pair_sum, in_send))
    in_got = lax.ppermute(in_send, "xl", SWAP)

    spread = lax.all_to_all(pair_sum, ("z", "xh"), split_axis=0, concat_axis=0, tiled=True)
    packed = call(norm_kernel, [sds((16, 8, 512), bf16)], count=3)(
        spread, residual, norm_gain[None, :]
    )
    split = lax.all_to_all(packed, CTX, split_axis=0, concat_axis=0, tiled=True)
    split, in_got, down_send = lax.optimization_barrier((split, in_got, down_send))
    down_got = lax.ppermute(down_send, "xl", SWAP)
    split = split.reshape(128, 512)
    w_in = call(join_in_kernel, [sds((3 * 384, 2 * ff_half), bf16)], count=2)(in_keep, in_got)
    w_down = call(join_down_kernel, [sds((384, 3 * ff_half), bf16)], count=2)(down_keep, down_got)

    routes = jnp.transpose(route_ids, (1, 0, 2)).reshape(128, TOPK)
    expert_axis = jnp.arange(EXPERTS, dtype=i32)
    named = jnp.any(routes[:, :, None] == expert_axis[None, None, :], axis=1)
    earlier_tokens = jnp.tril(jnp.ones((128, 128), bf16), -1)
    slot_all = jnp.dot(earlier_tokens, named.astype(bf16), preferred_element_type=f32).astype(i32)
    slot_of = jnp.sum(
        jnp.where(routes[:, :, None] == expert_axis[None, None, :], slot_all[:, None, :], 0), axis=2
    )
    target = (routes // 3) * SLOTS + (routes % 3) * CAP + slot_of
    slot_axis = jnp.arange(32 * SLOTS, dtype=i32)
    picker = jnp.any(target.T[None, :, :] == slot_axis[:, None, None], axis=1).astype(bf16)
    order = jnp.arange(128, dtype=i32)
    back_order = ((order % 16) * 8 + order // 16)[:, None] == order[None, :]
    target_rb = jnp.transpose(target.reshape(16, 8, TOPK), (1, 0, 2)).reshape(128, TOPK)
    gates_rb = route_gates.reshape(128, TOPK)
    weighting = jnp.sum(
        jnp.where(target_rb[:, :, None] == slot_axis[None, None, :], gates_rb[:, :, None], 0.0),
        axis=1,
    )

    travel = sds((32, 80, 128), bf16)
    outgoing = call(pick_kernel, [travel], count=2)(picker, split)
    received = lax.all_to_all(outgoing, EXP, split_axis=0, concat_axis=0, tiled=True)
    received, w_in, w_down = lax.optimization_barrier((received, w_in, w_down))
    pre = call(gate_up_kernel, [sds((32 * SLOTS, 2 * ff_half), bf16)], count=2)(received, w_in)
    pre_parts = lax.all_to_all(
        pre.reshape(8, 128, 2 * ff_half), "y", split_axis=0, concat_axis=0, tiled=True
    )
    hidden = call(hidden_kernel, [sds((8, 128, ff_half), bf16)], count=1)(pre_parts)
    hidden_all = lax.all_to_all(hidden, "y", split_axis=0, concat_axis=0, tiled=True)
    expert_out = call(down_kernel, [travel], count=2)(
        hidden_all.reshape(32 * SLOTS, ff_half), w_down
    )
    returned = lax.all_to_all(expert_out, EXP, split_axis=0, concat_axis=0, tiled=True)
    mix_keep, mix_send = call(
        combine_kernel, [sds((128, width_out), f32), sds((128, width_out), bf16)], count=4
    )(weighting, returned, back_order.astype(bf16), split)
    mix_got = lax.ppermute(mix_send, "xl", SWAP)
    result = (mix_keep + mix_got.astype(f32)).astype(bf16)
    return result.reshape(8, 16, width_out)


def solution(mesh):
    grid = Mesh(mesh.devices.reshape(8, 2, 8, 2, 2), ("y", "xl", "z", "xh", "core"))
    return jax.shard_map(
        on_device,
        mesh=grid,
        in_specs=(
            P(CTX, EXP, None),
            P(CTX, None),
            P(CTX),
            P(EXP, None, None),
            P(EXP, None),
            P(CTX + EXP, None),
            P(),
            P(EXP, None, None),
            P(EXP, None, None),
            P(EXP, CTX, None),
            P(EXP, CTX, None),
            P(EXP, None, CTX),
        ),
        out_specs=P(EXP, None, CTX),
        check_vma=False,
    )
```

```python
import jax
import jax.numpy as jnp
from jax import lax
from jax.experimental import pallas as pl
from jax.experimental.pallas import tpu as pltpu
from jax.sharding import Mesh, PartitionSpec as P

LATENT = 512
VDIM = 128
QKDIM = 192
EXPERTS = 96
TOPK = 6
CAP = 10
SLOTS = 32
SEGMENTS = 8
KEYW = 592
FAR = float(2**20)

CTX = ("y", "xl")
EXP = ("z", "xh", "core")
SWAP = [(0, 1), (1, 0)]
BIG_VMEM = pltpu.CompilerParams(vmem_limit_bytes=20 * 2**20)
f32, bf16, i32 = jnp.float32, jnp.bfloat16, jnp.int32


def keys_kernel(latent, segments, own):
    width, tokens = latent.shape
    own[:width, :] = latent[...]
    mark = lax.broadcasted_iota(i32, (KEYW - width, tokens), 0)
    own[width:, :] = jnp.where(segments[...] == mark, 1.0, 0.0).astype(bf16)


def keys_of(chunk):
    return chunk[...] if len(chunk.shape) == 2 else jnp.concatenate([chunk[0], chunk[1]], axis=1)


def nt_dot(a, b):
    return lax.dot_general(a, b, (((1,), (1,)), ((), ())), preferred_element_type=f32)


def attend_chunks(rows, chunks, biases, scores, old):
    scale = QKDIM ** (-0.5)
    peak = jnp.full((256, 128), -FAR, f32) if old is None else old[0]
    for n, (chunk, bias) in enumerate(zip(chunks, biases)):
        part = bias(jnp.dot(rows, keys_of(chunk), preferred_element_type=f32) * scale)
        scores[:, n * 256 : (n + 1) * 256] = part
        peak = jnp.maximum(peak, jnp.maximum(part[:, :128], part[:, 128:]))
    peak = jnp.max(peak, axis=1, keepdims=True)
    if old is None:
        sums, mixed = jnp.zeros((256, 128), f32), jnp.zeros((256, LATENT), f32)
    else:
        factor = jnp.exp(old[0][:, :1] - peak)
        sums, mixed = old[1] * factor, old[2] * factor
    for n, chunk in enumerate(chunks):
        terms = jnp.exp(scores[:, n * 256 : (n + 1) * 256] - peak)
        sums = sums + terms[:, :128] + terms[:, 128:]
        mixed = mixed + nt_dot(terms.astype(bf16), keys_of(chunk)[:LATENT])
    return jnp.broadcast_to(peak, (256, 128)), sums, mixed


def valid_bias(info, piece):
    def bias(part):
        lane = lax.broadcasted_iota(i32, (256, 256), 1)
        first = jnp.where(info[2 * piece] >= 0, 0.0, -FAR)
        second = jnp.where(info[2 * piece + 1] >= 0, 0.0, -FAR)
        return part + jnp.where(lane < 128, first, second)

    return bias


def causal_bias(part):
    lane = lax.broadcasted_iota(i32, (256, 256), 1)
    row = lax.broadcasted_iota(i32, (256, 256), 0)
    token = (row % 128) // 8 * 16 + row // 128 * 8 + row % 8
    return jnp.where(lane <= token, part, -FAR)


def first_attention_kernel(info, query, own, p0, peak, sums, mixed, scores):
    for head in range(2):
        state = attend_chunks(
            query[head], [own, p0], [causal_bias, valid_bias(info, 0)], scores.at[head], None
        )
        peak[head], sums[head], mixed[head] = state


def second_attention_kernel(
    info, query, p1, p2, p3, o0, old_peak, old_sums, old_mixed, peak, sums, mixed, scores
):
    for head in range(2):
        old = old_peak[head], old_sums[head], old_mixed[head]
        biases = [valid_bias(info, n) for n in (1, 2, 3, 0)]
        state = attend_chunks(query[head], [p1, p2, p3, o0], biases, scores.at[head], old)
        peak[head], sums[head], mixed[head] = state


def last_attention_kernel(
    info, query, others, old_peak, old_sums, old_mixed, value_up, out_proj, send, keep, scores, values
):
    core = info[8]

    for head in range(2):
        old = old_peak[head], old_sums[head], old_mixed[head]
        chunks = [others.at[2 * n : 2 * n + 2] for n in range(3)]
        biases = [valid_bias(info, n) for n in (1, 2, 3)]
        _, sums, mixed = attend_chunks(query[head], chunks, biases, scores.at[head], old)
        mixed = (mixed / jnp.sum(sums, axis=1, keepdims=True)).astype(bf16)
        values[head] = jnp.dot(mixed, value_up[head], preferred_element_type=f32).astype(bf16)

    def project(which, out):
        start = pl.multiple_of(which * 128, 128)
        both = jnp.concatenate([values[head, pl.ds(start, 128), :] for head in range(2)], axis=1)
        for c in range(0, out.shape[1], 640):
            out[:, c : c + 640] = jnp.dot(
                both, out_proj[:, c : c + 640], preferred_element_type=f32
            ).astype(out.dtype)

    project(1 - core, send)
    project(core, keep)


def add_kernel(keep, got, out):
    out[...] = (keep[...] + got[...].astype(f32)).reshape(out.shape).astype(bf16)


def gather_kernel(p1, p2, p3, out):
    for n, piece in enumerate((p1, p2, p3)):
        out[2 * n : 2 * n + 2] = piece[...]


def norm_kernel(spread, residual, gain, packed):
    attended = jnp.sum(spread[...].astype(f32), axis=0)
    stream = (residual[...].astype(f32) + attended).astype(bf16).astype(f32)
    mean_sq = jnp.mean(stream * stream, axis=1, keepdims=True)
    normed = (stream * lax.rsqrt(mean_sq + 1e-06) * gain[...]).astype(bf16).astype(f32)
    width = stream.shape[1] // 16
    fill = jnp.zeros((stream.shape[0], packed.shape[2] - 3 * width), f32)
    for c in range(16):
        mine, other = c * width, (c ^ 1) * width
        packed[c] = jnp.concatenate(
            [
                normed[:, mine : mine + width],
                normed[:, other : other + width],
                stream[:, mine : mine + width],
                fill,
            ],
            axis=1,
        ).astype(bf16)


def store_packed(out, n, rows):
    left = lax.broadcasted_iota(i32, (SLOTS // 2, 128), 1) < 64
    out[n, 0:32] = rows[:, :128].astype(bf16)
    out[n, 32:64] = rows[:, 128:256].astype(bf16)
    out[n, 64:80] = jnp.where(left, rows[:16, 256:], rows[16:, 256:]).astype(bf16)


def load_packed(ref, n):
    last = ref[n, 64:80]
    left = jnp.where(lax.broadcasted_iota(i32, (1, 128), 1) < 64, 1.0, 0.0).astype(bf16)
    last = jnp.concatenate([last * left, last * (1 - left)], axis=0)
    return jnp.concatenate([ref[n, 0:32], ref[n, 32:64], last], axis=1)


def pick_kernel(picker, split, out):
    values = split[:, :384]
    doubled = jnp.concatenate([values[:, :320], values[:, 256:320]], axis=1)
    for r in range(0, picker.shape[0], 256):
        rows = jnp.dot(picker[r : r + 256, :], doubled, preferred_element_type=f32)
        for n in range(256 // SLOTS):
            store_packed(out, r // SLOTS + n, rows[n * SLOTS : (n + 1) * SLOTS])


def row_mask(count, j):
    slot = lax.broadcasted_iota(i32, (count, 1), 0) % SLOTS
    return jnp.where((slot >= j * CAP) & (slot < (j + 1) * CAP), 1.0, 0.0).astype(bf16)


def spread_experts(rows, masks):
    return jnp.concatenate([rows * mask for mask in masks], axis=1)


def split_weights_kernel(info, gate, up, down, in_send, in_keep, down_send, down_keep):
    half = gate.shape[2] // 2

    def move(into, onto, start):
        into[:, :, :half] = gate[:, :, start : start + half]
        into[:, :, half:] = up[:, :, start : start + half]
        onto[...] = down[:, :, start : start + half]

    @pl.when(info[9] == 0)
    def _():
        move(in_keep, down_keep, 0)
        move(in_send, down_send, half)

    @pl.when(info[9] != 0)
    def _():
        move(in_keep, down_keep, half)
        move(in_send, down_send, 0)


def join_in_kernel(keep, got, out):
    rows = keep.shape[1]
    for j in range(3):
        base = j * 384
        out[base : base + rows, :] = keep[j]
        out[base + rows : base + 2 * rows, :] = got[j]
        out[base + 2 * rows : base + 384, :] = got[j, 256 - rows :]


def join_down_kernel(keep, got, out):
    rows, width = keep.shape[1:]
    for j in range(3):
        lanes = slice(j * width, (j + 1) * width)
        out[:rows, lanes] = keep[j]
        out[rows : 2 * rows, lanes] = got[j]
        out[2 * rows :, lanes] = got[j, 256 - rows :]


def gate_up_kernel(received, weights, pre):
    masks = [row_mask(256, j) for j in range(3)]
    for r in range(0, received.shape[0], 8):
        rows = jnp.concatenate([load_packed(received, r + n) for n in range(8)], axis=0)
        total = jnp.dot(spread_experts(rows, masks), weights[...], preferred_element_type=f32)
        pre[r * SLOTS : (r + 8) * SLOTS, :] = total.astype(bf16)


def hidden_kernel(parts, out):
    total = jnp.sum(parts[...].astype(f32), axis=0)
    half = total.shape[1] // 2
    gate, up = total[:, :half], total[:, half:]
    hidden = (gate / (1.0 + jnp.exp(-gate)) * up).astype(bf16)
    for n in range(out.shape[0]):
        out[n] = hidden


def down_kernel(hidden, weights, out):
    masks = [row_mask(256, j) for j in range(3)]
    for r in range(0, hidden.shape[0], 256):
        rows = spread_experts(hidden[r : r + 256, :], masks)
        total = nt_dot(rows, weights[...])
        for n in range(256 // SLOTS):
            store_packed(out, r // SLOTS + n, total[n * SLOTS : (n + 1) * SLOTS])


def combine_kernel(weighting, returned, order, stream, keep, send):
    width = keep.shape[1]
    rows = jnp.concatenate([load_packed(returned, n) for n in range(returned.shape[0])], axis=0)
    top = weighting[...].astype(bf16)
    rest = (weighting[...] - top.astype(f32)).astype(bf16)
    mixture = jnp.dot(top, rows, preferred_element_type=f32) + jnp.dot(
        rest, rows, preferred_element_type=f32
    )
    tail = mixture[:, 256:320] + mixture[:, 320:384]
    kept = jnp.dot(order[...], stream[:, 2 * width : 3 * width], preferred_element_type=f32)
    keep[...] = kept + mixture[:, :width]
    send[...] = jnp.concatenate([mixture[:, width:256], tail], axis=1).astype(bf16)


def call(kernel, outs, scratch=(), smem_first=False, count=0):
    specs = [pl.BlockSpec(memory_space=pltpu.VMEM)] * count
    if smem_first:
        specs[0] = pl.BlockSpec(memory_space=pltpu.SMEM)
    out_specs = [pl.BlockSpec(memory_space=pltpu.VMEM)] * len(outs)
    single = len(outs) == 1
    return pl.pallas_call(
        kernel,
        in_specs=specs,
        out_specs=out_specs[0] if single else out_specs,
        out_shape=outs[0] if single else outs,
        scratch_shapes=list(scratch),
        compiler_params=BIG_VMEM,
    )


def sds(shape, dtype):
    return jax.ShapeDtypeStruct(shape, dtype)


def on_device(
    queries,
    latent,
    segment_ids,
    value_up,
    out_proj,
    residual,
    norm_gain,
    route_ids,
    route_gates,
    expert_gate,
    expert_up,
    expert_down,
):
    block_len, local_heads, width_key = queries.shape
    width_model = residual.shape[1]
    width_out = width_model // 16
    width_pair = 2 * width_out
    ff = expert_gate.shape[2]
    ff_half = ff // 2
    y, xl, xh, core = (lax.axis_index(a) for a in ("y", "xl", "xh", "core"))
    half = block_len // 2

    segment_axis = jnp.arange(SEGMENTS, dtype=i32)
    own_segment = segment_ids[:, None] == segment_axis[None, :]
    pad = KEYW - width_key - SEGMENTS
    keys_own = call(keys_kernel, [sds((KEYW, block_len), bf16)], count=2)(
        latent.T, segment_ids[None, :]
    )
    mine = lax.dynamic_slice_in_dim(keys_own, core * half, half, 1)

    def along_y(near, far):
        pairs = [
            (2 * i + h, 2 * ((i + (near, far)[h]) % 8) + h) for i in range(8) for h in range(2)
        ]
        return lax.ppermute(mine, ("y", "xh"), pairs)

    near, far = along_y(1, 2), along_y(3, 4)

    def blocks_of(x, h):
        return [2 * (y - 1 - h) + x, 2 * (y - 3 - h) + x]

    def blocks_sent(x, h):
        early, late = blocks_of(x, h)
        odd = (x == 0) & (h == 1)
        return [jnp.where(odd, 2 * y, early), jnp.where(odd, early, late)]

    info = jnp.stack(
        blocks_of(xl, xh)
        + blocks_of(xl, 1 - xh)
        + blocks_sent(1 - xl, xh)
        + blocks_sent(1 - xl, 1 - xh)
        + [core, xl]
    ).astype(i32)

    masks = jnp.where(own_segment, 0.0, -FAR).astype(bf16)
    query_rows = jnp.concatenate(
        [
            queries,
            jnp.broadcast_to(masks[:, None, :], (block_len, local_heads, SEGMENTS)),
            jnp.zeros((block_len, local_heads, pad), bf16),
        ],
        axis=2,
    )
    query_rows = query_rows.reshape(16, 2, 8, local_heads, KEYW).transpose(3, 1, 0, 2, 4)
    query_rows = query_rows.reshape(local_heads, block_len, KEYW)
    near, far, query_rows = lax.optimization_barrier((near, far, query_rows))

    column = jnp.stack([near, far])
    to_other = jnp.where(
        (xl == 0) & (xh == 1), jnp.stack([mine, column[0]]), column
    )
    diagonal = [(0, 3), (1, 2), (2, 1), (3, 0)]
    pieces = [
        column,
        lax.ppermute(column, "xh", SWAP),
        lax.ppermute(to_other, "xl", SWAP),
        lax.ppermute(to_other, ("xl", "xh"), diagonal),
    ]

    state_out = [
        sds((2, 256, 128), f32),
        sds((2, 256, 128), f32),
        sds((2, 256, LATENT), f32),
    ]
    state = call(
        first_attention_kernel, state_out, [pltpu.VMEM((2, 256, 2 * 256), f32)], True, 4
    )(info, query_rows, keys_own, column)
    pieces[1], column_late, peak = lax.optimization_barrier((pieces[1], column, state[0]))
    state = [peak] + list(state[1:])
    first_other = lax.ppermute(column_late, "core", SWAP)
    *pieces, first_other = lax.optimization_barrier((*pieces, first_other))
    three = call(gather_kernel, [sds((6, KEYW, half), bf16)], count=3)(*pieces[1:])
    others = lax.ppermute(three, "core", SWAP)
    state = call(
        second_attention_kernel, state_out, [pltpu.VMEM((2, 256, 4 * 256), f32)], True, 9
    )(info, query_rows, pieces[1], pieces[2], pieces[3], first_other, *state)
    send, keep = call(
        last_attention_kernel,
        [sds((half, width_model), bf16), sds((half, width_model), f32)],
        [pltpu.VMEM((2, 256, 3 * 256), f32), pltpu.VMEM((2, 256, VDIM), bf16)],
        True,
        8,
    )(info, query_rows, others, *state, value_up, out_proj)
    got = lax.ppermute(send, "core", SWAP)
    pair_sum = call(add_kernel, [sds((16, 8, width_model), bf16)], count=2)(keep, got)

    in_out = sds((3, width_out, 2 * ff_half), bf16)
    down_out = sds((3, width_out, ff_half), bf16)
    in_send, in_keep, down_send, down_keep = call(
        split_weights_kernel, [in_out, in_out, down_out, down_out], (), True, 4
    )(info, expert_gate, expert_up, jnp.transpose(expert_down, (0, 2, 1)))
    pair_sum, in_send = lax.optimization_barrier((pair_sum, in_send))
    in_got = lax.ppermute(in_send, "xl", SWAP)

    spread = lax.all_to_all(pair_sum, ("z", "xh"), split_axis=0, concat_axis=0, tiled=True)
    packed = call(norm_kernel, [sds((16, 8, 512), bf16)], count=3)(
        spread, residual, norm_gain[None, :]
    )
    split = lax.all_to_all(packed, CTX, split_axis=0, concat_axis=0, tiled=True)
    split, in_got, down_send = lax.optimization_barrier((split, in_got, down_send))
    down_got = lax.ppermute(down_send, "xl", SWAP)
    split = split.reshape(128, 512)
    w_in = call(join_in_kernel, [sds((3 * 384, 2 * ff_half), bf16)], count=2)(in_keep, in_got)
    w_down = call(join_down_kernel, [sds((384, 3 * ff_half), bf16)], count=2)(down_keep, down_got)

    routes = jnp.transpose(route_ids, (1, 0, 2)).reshape(128, TOPK)
    expert_axis = jnp.arange(EXPERTS, dtype=i32)
    named = jnp.any(routes[:, :, None] == expert_axis[None, None, :], axis=1)
    earlier_tokens = jnp.tril(jnp.ones((128, 128), bf16), -1)
    slot_all = jnp.dot(earlier_tokens, named.astype(bf16), preferred_element_type=f32).astype(i32)
    slot_of = jnp.sum(
        jnp.where(routes[:, :, None] == expert_axis[None, None, :], slot_all[:, None, :], 0), axis=2
    )
    target = (routes // 3) * SLOTS + (routes % 3) * CAP + slot_of
    slot_axis = jnp.arange(32 * SLOTS, dtype=i32)
    picker = jnp.any(target.T[None, :, :] == slot_axis[:, None, None], axis=1).astype(bf16)
    order = jnp.arange(128, dtype=i32)
    back_order = ((order % 16) * 8 + order // 16)[:, None] == order[None, :]
    target_rb = jnp.transpose(target.reshape(16, 8, TOPK), (1, 0, 2)).reshape(128, TOPK)
    gates_rb = route_gates.reshape(128, TOPK)
    weighting = jnp.sum(
        jnp.where(target_rb[:, :, None] == slot_axis[None, None, :], gates_rb[:, :, None], 0.0),
        axis=1,
    )

    travel = sds((32, 80, 128), bf16)
    outgoing = call(pick_kernel, [travel], count=2)(picker, split)
    received = lax.all_to_all(outgoing, EXP, split_axis=0, concat_axis=0, tiled=True)
    received, w_in, w_down = lax.optimization_barrier((received, w_in, w_down))
    pre = call(gate_up_kernel, [sds((32 * SLOTS, 2 * ff_half), bf16)], count=2)(received, w_in)
    pre_parts = lax.all_to_all(
        pre.reshape(8, 128, 2 * ff_half), "y", split_axis=0, concat_axis=0, tiled=True
    )
    hidden = call(hidden_kernel, [sds((8, 128, ff_half), bf16)], count=1)(pre_parts)
    hidden_all = lax.all_to_all(hidden, "y", split_axis=0, concat_axis=0, tiled=True)
    expert_out = call(down_kernel, [travel], count=2)(
        hidden_all.reshape(32 * SLOTS, ff_half), w_down
    )
    returned = lax.all_to_all(expert_out, EXP, split_axis=0, concat_axis=0, tiled=True)
    mix_keep, mix_send = call(
        combine_kernel, [sds((128, width_out), f32), sds((128, width_out), bf16)], count=4
    )(weighting, returned, back_order.astype(bf16), split)
    mix_got = lax.ppermute(mix_send, "xl", SWAP)
    result = (mix_keep + mix_got.astype(f32)).astype(bf16)
    return result.reshape(8, 16, width_out)


def solution(mesh):
    grid = Mesh(mesh.devices.reshape(8, 2, 8, 2, 2), ("y", "xl", "z", "xh", "core"))
    return jax.shard_map(
        on_device,
        mesh=grid,
        in_specs=(
            P(CTX, EXP, None),
            P(CTX, None),
            P(CTX),
            P(EXP, None, None),
            P(EXP, None),
            P(CTX + EXP, None),
            P(),
            P(EXP, None, None),
            P(EXP, None, None),
            P(EXP, CTX, None),
            P(EXP, CTX, None),
            P(EXP, None, CTX),
        ),
        out_specs=P(EXP, None, CTX),
        check_vma=False,
    )
```

```python
import jax
import jax.numpy as jnp
from jax import lax
from jax.experimental import pallas as pl
from jax.experimental.pallas import tpu as pltpu
from jax.sharding import Mesh, PartitionSpec as P

LATENT = 512
VDIM = 128
QKDIM = 192
EXPERTS = 96
TOPK = 6
CAP = 10
SLOTS = 32
SEGMENTS = 8
KEYW = 592
FAR = float(2**20)

CTX = ("y", "xl")
EXP = ("z", "xh", "core")
SWAP = [(0, 1), (1, 0)]
BIG_VMEM = pltpu.CompilerParams(vmem_limit_bytes=20 * 2**20)
f32, bf16, i32 = jnp.float32, jnp.bfloat16, jnp.int32


def keys_kernel(latent, segments, own):
    width, tokens = latent.shape
    own[:width, :] = latent[...]
    mark = lax.broadcasted_iota(i32, (KEYW - width, tokens), 0)
    own[width:, :] = jnp.where(segments[...] == mark, 1.0, 0.0).astype(bf16)


def nt_dot(a, b):
    return lax.dot_general(a, b, (((1,), (1,)), ((), ())), preferred_element_type=f32)


def attend_chunks(rows, chunks, biases, scores, old):
    scale = QKDIM ** (-0.5)
    peak = jnp.full((256, 128), -FAR, f32) if old is None else old[0]
    for n, (chunk, bias) in enumerate(zip(chunks, biases)):
        part = bias(jnp.dot(rows, chunk[...], preferred_element_type=f32) * scale)
        scores[:, n * 256 : (n + 1) * 256] = part
        peak = jnp.maximum(peak, jnp.maximum(part[:, :128], part[:, 128:]))
    peak = jnp.max(peak, axis=1, keepdims=True)
    if old is None:
        sums, mixed = jnp.zeros((256, 128), f32), jnp.zeros((256, LATENT), f32)
    else:
        factor = jnp.exp(old[0][:, :1] - peak)
        sums, mixed = old[1] * factor, old[2] * factor
    for n, chunk in enumerate(chunks):
        terms = jnp.exp(scores[:, n * 256 : (n + 1) * 256] - peak)
        sums = sums + terms[:, :128] + terms[:, 128:]
        mixed = mixed + nt_dot(terms.astype(bf16), chunk[:LATENT, :])
    return jnp.broadcast_to(peak, (256, 128)), sums, mixed


def valid_bias(info, n):
    return lambda part: part + jnp.where(info[n] >= 0, 0.0, -FAR)


def causal_bias(part):
    lane = lax.broadcasted_iota(i32, (256, 256), 1)
    row = lax.broadcasted_iota(i32, (256, 256), 0)
    token = (row % 128) // 8 * 16 + row // 128 * 8 + row % 8
    return jnp.where(lane <= token, part, -FAR)


def first_attention_kernel(info, query, own, p0, peak, sums, mixed, scores):
    for head in range(2):
        state = attend_chunks(
            query[head], [own, p0], [causal_bias, valid_bias(info, 0)], scores.at[head], None
        )
        peak[head], sums[head], mixed[head] = state


def second_attention_kernel(
    info, query, p1, p2, p3, o0, old_peak, old_sums, old_mixed, peak, sums, mixed, scores
):
    for head in range(2):
        old = old_peak[head], old_sums[head], old_mixed[head]
        biases = [valid_bias(info, n) for n in (1, 2, 3, 4)]
        state = attend_chunks(query[head], [p1, p2, p3, o0], biases, scores.at[head], old)
        peak[head], sums[head], mixed[head] = state


def last_attention_kernel(
    info, query, others, old_peak, old_sums, old_mixed, value_up, out_proj, send, keep, scores, values
):
    core = info[8]

    for head in range(2):
        old = old_peak[head], old_sums[head], old_mixed[head]
        chunks = [others.at[n] for n in range(3)]
        biases = [valid_bias(info, n) for n in (5, 6, 7)]
        _, sums, mixed = attend_chunks(query[head], chunks, biases, scores.at[head], old)
        mixed = (mixed / jnp.sum(sums, axis=1, keepdims=True)).astype(bf16)
        values[head] = jnp.dot(mixed, value_up[head], preferred_element_type=f32).astype(bf16)

    def project(which, out):
        start = pl.multiple_of(which * 128, 128)
        both = jnp.concatenate([values[head, pl.ds(start, 128), :] for head in range(2)], axis=1)
        for c in range(0, out.shape[1], 640):
            out[:, c : c + 640] = jnp.dot(
                both, out_proj[:, c : c + 640], preferred_element_type=f32
            ).astype(out.dtype)

    project(1 - core, send)
    project(core, keep)


def add_kernel(keep, got, out):
    out[...] = (keep[...] + got[...].astype(f32)).reshape(out.shape).astype(bf16)


def gather_kernel(p1, p2, p3, out):
    for n, piece in enumerate((p1, p2, p3)):
        out[n] = piece[...]


def norm_kernel(spread, residual, gain, packed):
    attended = jnp.sum(spread[...].astype(f32), axis=0)
    stream = (residual[...].astype(f32) + attended).astype(bf16).astype(f32)
    mean_sq = jnp.mean(stream * stream, axis=1, keepdims=True)
    normed = (stream * lax.rsqrt(mean_sq + 1e-06) * gain[...]).astype(bf16).astype(f32)
    width = stream.shape[1] // 16
    fill = jnp.zeros((stream.shape[0], packed.shape[2] - 3 * width), f32)
    for c in range(16):
        mine, other = c * width, (c ^ 1) * width
        packed[c] = jnp.concatenate(
            [
                normed[:, mine : mine + width],
                normed[:, other : other + width],
                stream[:, mine : mine + width],
                fill,
            ],
            axis=1,
        ).astype(bf16)


def store_packed(out, n, rows):
    left = lax.broadcasted_iota(i32, (SLOTS // 2, 128), 1) < 64
    out[n, 0:32] = rows[:, :128].astype(bf16)
    out[n, 32:64] = rows[:, 128:256].astype(bf16)
    out[n, 64:80] = jnp.where(left, rows[:16, 256:], rows[16:, 256:]).astype(bf16)


def load_packed(ref, n):
    last = ref[n, 64:80]
    left = jnp.where(lax.broadcasted_iota(i32, (1, 128), 1) < 64, 1.0, 0.0).astype(bf16)
    last = jnp.concatenate([last * left, last * (1 - left)], axis=0)
    return jnp.concatenate([ref[n, 0:32], ref[n, 32:64], last], axis=1)


def pick_kernel(picker, split, out):
    values = split[:, :384]
    doubled = jnp.concatenate([values[:, :320], values[:, 256:320]], axis=1)
    for r in range(0, picker.shape[0], 256):
        rows = jnp.dot(picker[r : r + 256, :], doubled, preferred_element_type=f32)
        for n in range(256 // SLOTS):
            store_packed(out, r // SLOTS + n, rows[n * SLOTS : (n + 1) * SLOTS])


def row_mask(count, j):
    slot = lax.broadcasted_iota(i32, (count, 1), 0) % SLOTS
    return jnp.where((slot >= j * CAP) & (slot < (j + 1) * CAP), 1.0, 0.0).astype(bf16)


def spread_experts(rows, masks):
    return jnp.concatenate([rows * mask for mask in masks], axis=1)


def split_weights_kernel(info, gate, up, down, in_send, in_keep, down_send, down_keep):
    half = gate.shape[2] // 2

    def move(into, onto, start):
        into[:, :, :half] = gate[:, :, start : start + half]
        into[:, :, half:] = up[:, :, start : start + half]
        onto[...] = down[:, :, start : start + half]

    @pl.when(info[9] == 0)
    def _():
        move(in_keep, down_keep, 0)
        move(in_send, down_send, half)

    @pl.when(info[9] != 0)
    def _():
        move(in_keep, down_keep, half)
        move(in_send, down_send, 0)


def join_in_kernel(keep, got, out):
    rows = keep.shape[1]
    for j in range(3):
        base = j * 384
        out[base : base + rows, :] = keep[j]
        out[base + rows : base + 2 * rows, :] = got[j]
        out[base + 2 * rows : base + 384, :] = got[j, 256 - rows :]


def join_down_kernel(keep, got, out):
    rows, width = keep.shape[1:]
    for j in range(3):
        lanes = slice(j * width, (j + 1) * width)
        out[:rows, lanes] = keep[j]
        out[rows : 2 * rows, lanes] = got[j]
        out[2 * rows :, lanes] = got[j, 256 - rows :]


def gate_up_kernel(received, weights, pre):
    masks = [row_mask(256, j) for j in range(3)]
    for r in range(0, received.shape[0], 8):
        rows = jnp.concatenate([load_packed(received, r + n) for n in range(8)], axis=0)
        total = jnp.dot(spread_experts(rows, masks), weights[...], preferred_element_type=f32)
        pre[r * SLOTS : (r + 8) * SLOTS, :] = total.astype(bf16)


def hidden_kernel(parts, out):
    total = jnp.sum(parts[...].astype(f32), axis=0)
    half = total.shape[1] // 2
    gate, up = total[:, :half], total[:, half:]
    hidden = (gate / (1.0 + jnp.exp(-gate)) * up).astype(bf16)
    for n in range(out.shape[0]):
        out[n] = hidden


def down_kernel(hidden, weights, out):
    masks = [row_mask(256, j) for j in range(3)]
    for r in range(0, hidden.shape[0], 256):
        rows = spread_experts(hidden[r : r + 256, :], masks)
        total = nt_dot(rows, weights[...])
        for n in range(256 // SLOTS):
            store_packed(out, r // SLOTS + n, total[n * SLOTS : (n + 1) * SLOTS])


def combine_kernel(weighting, returned, order, stream, keep, send):
    width = keep.shape[1]
    rows = jnp.concatenate([load_packed(returned, n) for n in range(returned.shape[0])], axis=0)
    top = weighting[...].astype(bf16)
    rest = (weighting[...] - top.astype(f32)).astype(bf16)
    mixture = jnp.dot(top, rows, preferred_element_type=f32) + jnp.dot(
        rest, rows, preferred_element_type=f32
    )
    tail = mixture[:, 256:320] + mixture[:, 320:384]
    kept = jnp.dot(order[...], stream[:, 2 * width : 3 * width], preferred_element_type=f32)
    keep[...] = kept + mixture[:, :width]
    send[...] = jnp.concatenate([mixture[:, width:256], tail], axis=1).astype(bf16)


def call(kernel, outs, scratch=(), smem_first=False, count=0):
    specs = [pl.BlockSpec(memory_space=pltpu.VMEM)] * count
    if smem_first:
        specs[0] = pl.BlockSpec(memory_space=pltpu.SMEM)
    out_specs = [pl.BlockSpec(memory_space=pltpu.VMEM)] * len(outs)
    single = len(outs) == 1
    return pl.pallas_call(
        kernel,
        in_specs=specs,
        out_specs=out_specs[0] if single else out_specs,
        out_shape=outs[0] if single else outs,
        scratch_shapes=list(scratch),
        compiler_params=BIG_VMEM,
    )


def sds(shape, dtype):
    return jax.ShapeDtypeStruct(shape, dtype)


def on_device(
    queries,
    latent,
    segment_ids,
    value_up,
    out_proj,
    residual,
    norm_gain,
    route_ids,
    route_gates,
    expert_gate,
    expert_up,
    expert_down,
):
    block_len, local_heads, width_key = queries.shape
    width_model = residual.shape[1]
    width_out = width_model // 16
    width_pair = 2 * width_out
    ff = expert_gate.shape[2]
    ff_half = ff // 2
    y, xl, xh, core = (lax.axis_index(a) for a in ("y", "xl", "xh", "core"))
    half = block_len // 2

    segment_axis = jnp.arange(SEGMENTS, dtype=i32)
    own_segment = segment_ids[:, None] == segment_axis[None, :]
    pad = KEYW - width_key - SEGMENTS
    keys_own = call(keys_kernel, [sds((KEYW, block_len), bf16)], count=2)(
        latent.T, segment_ids[None, :]
    )
    pairs = [
        (4 * i + j, 4 * ((i + 1 + j // 2 + 2 * (j % 2)) % 8) + j) for i in range(8) for j in range(4)
    ]
    fetched = lax.ppermute(keys_own, ("y", "xh", "core"), pairs)

    def block_of(x, h, c):
        return 2 * (y - 1 - h - 2 * c) + x

    def block_sent(x, h, c):
        return jnp.where((x == 0) & (h == 1) & (c == 1), 2 * y, block_of(x, h, c))

    def blocks_held(c):
        own = [block_of(xl, xh, c), block_of(xl, 1 - xh, c)]
        return own + [block_sent(1 - xl, xh, c), block_sent(1 - xl, 1 - xh, c)]

    info = jnp.stack(blocks_held(core) + blocks_held(1 - core) + [core, xl]).astype(i32)

    masks = jnp.where(own_segment, 0.0, -FAR).astype(bf16)
    query_rows = jnp.concatenate(
        [
            queries,
            jnp.broadcast_to(masks[:, None, :], (block_len, local_heads, SEGMENTS)),
            jnp.zeros((block_len, local_heads, pad), bf16),
        ],
        axis=2,
    )
    query_rows = query_rows.reshape(16, 2, 8, local_heads, KEYW).transpose(3, 1, 0, 2, 4)
    query_rows = query_rows.reshape(local_heads, block_len, KEYW)
    fetched, query_rows = lax.optimization_barrier((fetched, query_rows))

    to_other = jnp.where((xl == 0) & (xh == 1) & (core == 1), keys_own, fetched)
    diagonal = [(0, 3), (1, 2), (2, 1), (3, 0)]
    pieces = [
        fetched,
        lax.ppermute(fetched, "xh", SWAP),
        lax.ppermute(to_other, "xl", SWAP),
        lax.ppermute(to_other, ("xl", "xh"), diagonal),
    ]

    state_out = [
        sds((2, 256, 128), f32),
        sds((2, 256, 128), f32),
        sds((2, 256, LATENT), f32),
    ]
    state = call(
        first_attention_kernel, state_out, [pltpu.VMEM((2, 256, 2 * 256), f32)], True, 4
    )(info, query_rows, keys_own, fetched)
    pieces[1], fetched_late, peak = lax.optimization_barrier((pieces[1], fetched, state[0]))
    state = [peak] + list(state[1:])
    first_other = lax.ppermute(fetched_late, "core", SWAP)
    *pieces, first_other = lax.optimization_barrier((*pieces, first_other))
    three = call(gather_kernel, [sds((3, KEYW, block_len), bf16)], count=3)(*pieces[1:])
    others = lax.ppermute(three, "core", SWAP)
    state = call(
        second_attention_kernel, state_out, [pltpu.VMEM((2, 256, 4 * 256), f32)], True, 9
    )(info, query_rows, pieces[1], pieces[2], pieces[3], first_other, *state)
    send, keep = call(
        last_attention_kernel,
        [sds((half, width_model), bf16), sds((half, width_model), f32)],
        [pltpu.VMEM((2, 256, 3 * 256), f32), pltpu.VMEM((2, 256, VDIM), bf16)],
        True,
        8,
    )(info, query_rows, others, *state, value_up, out_proj)
    got = lax.ppermute(send, "core", SWAP)
    pair_sum = call(add_kernel, [sds((16, 8, width_model), bf16)], count=2)(keep, got)

    in_out = sds((3, width_out, 2 * ff_half), bf16)
    down_out = sds((3, width_out, ff_half), bf16)
    in_send, in_keep, down_send, down_keep = call(
        split_weights_kernel, [in_out, in_out, down_out, down_out], (), True, 4
    )(info, expert_gate, expert_up, jnp.transpose(expert_down, (0, 2, 1)))
    pair_sum, in_send = lax.optimization_barrier((pair_sum, in_send))
    in_got = lax.ppermute(in_send, "xl", SWAP)

    spread = lax.all_to_all(pair_sum, ("z", "xh"), split_axis=0, concat_axis=0, tiled=True)
    packed = call(norm_kernel, [sds((16, 8, 512), bf16)], count=3)(
        spread, residual, norm_gain[None, :]
    )
    split = lax.all_to_all(packed, CTX, split_axis=0, concat_axis=0, tiled=True)
    split, in_got, down_send = lax.optimization_barrier((split, in_got, down_send))
    down_got = lax.ppermute(down_send, "xl", SWAP)
    split = split.reshape(128, 512)
    w_in = call(join_in_kernel, [sds((3 * 384, 2 * ff_half), bf16)], count=2)(in_keep, in_got)
    w_down = call(join_down_kernel, [sds((384, 3 * ff_half), bf16)], count=2)(down_keep, down_got)

    routes = jnp.transpose(route_ids, (1, 0, 2)).reshape(128, TOPK)
    expert_axis = jnp.arange(EXPERTS, dtype=i32)
    named = jnp.any(routes[:, :, None] == expert_axis[None, None, :], axis=1)
    earlier_tokens = jnp.tril(jnp.ones((128, 128), bf16), -1)
    slot_all = jnp.dot(earlier_tokens, named.astype(bf16), preferred_element_type=f32).astype(i32)
    slot_of = jnp.sum(
        jnp.where(routes[:, :, None] == expert_axis[None, None, :], slot_all[:, None, :], 0), axis=2
    )
    target = (routes // 3) * SLOTS + (routes % 3) * CAP + slot_of
    slot_axis = jnp.arange(32 * SLOTS, dtype=i32)
    picker = jnp.any(target.T[None, :, :] == slot_axis[:, None, None], axis=1).astype(bf16)
    order = jnp.arange(128, dtype=i32)
    back_order = ((order % 16) * 8 + order // 16)[:, None] == order[None, :]
    target_rb = jnp.transpose(target.reshape(16, 8, TOPK), (1, 0, 2)).reshape(128, TOPK)
    gates_rb = route_gates.reshape(128, TOPK)
    weighting = jnp.sum(
        jnp.where(target_rb[:, :, None] == slot_axis[None, None, :], gates_rb[:, :, None], 0.0),
        axis=1,
    )

    travel = sds((32, 80, 128), bf16)
    outgoing = call(pick_kernel, [travel], count=2)(picker, split)
    received = lax.all_to_all(outgoing, EXP, split_axis=0, concat_axis=0, tiled=True)
    received, w_in, w_down = lax.optimization_barrier((received, w_in, w_down))
    pre = call(gate_up_kernel, [sds((32 * SLOTS, 2 * ff_half), bf16)], count=2)(received, w_in)
    pre_parts = lax.all_to_all(
        pre.reshape(8, 128, 2 * ff_half), "y", split_axis=0, concat_axis=0, tiled=True
    )
    hidden = call(hidden_kernel, [sds((8, 128, ff_half), bf16)], count=1)(pre_parts)
    hidden_all = lax.all_to_all(hidden, "y", split_axis=0, concat_axis=0, tiled=True)
    expert_out = call(down_kernel, [travel], count=2)(
        hidden_all.reshape(32 * SLOTS, ff_half), w_down
    )
    returned = lax.all_to_all(expert_out, EXP, split_axis=0, concat_axis=0, tiled=True)
    mix_keep, mix_send = call(
        combine_kernel, [sds((128, width_out), f32), sds((128, width_out), bf16)], count=4
    )(weighting, returned, back_order.astype(bf16), split)
    mix_got = lax.ppermute(mix_send, "xl", SWAP)
    result = (mix_keep + mix_got.astype(f32)).astype(bf16)
    return result.reshape(8, 16, width_out)


def solution(mesh):
    grid = Mesh(mesh.devices.reshape(8, 2, 8, 2, 2), ("y", "xl", "z", "xh", "core"))
    return jax.shard_map(
        on_device,
        mesh=grid,
        in_specs=(
            P(CTX, EXP, None),
            P(CTX, None),
            P(CTX),
            P(EXP, None, None),
            P(EXP, None),
            P(CTX + EXP, None),
            P(),
            P(EXP, None, None),
            P(EXP, None, None),
            P(EXP, CTX, None),
            P(EXP, CTX, None),
            P(EXP, None, CTX),
        ),
        out_specs=P(EXP, None, CTX),
        check_vma=False,
    )
```

```python
import jax
import jax.numpy as jnp
from jax import lax
from jax.experimental import pallas as pl
from jax.experimental.pallas import tpu as pltpu
from jax.sharding import Mesh, PartitionSpec as P

LATENT = 512
VDIM = 128
QKDIM = 192
EXPERTS = 96
TOPK = 6
CAP = 10
SLOTS = 32
SEGMENTS = 8
KEYW = 592
FAR = float(2**20)

CTX = ("y", "xl")
EXP = ("z", "xh", "core")
SWAP = [(0, 1), (1, 0)]
BIG_VMEM = pltpu.CompilerParams(vmem_limit_bytes=20 * 2**20)
f32, bf16, i32 = jnp.float32, jnp.bfloat16, jnp.int32


def keys_kernel(latent, segments, own):
    width, tokens = latent.shape
    own[:width, :] = latent[...]
    mark = lax.broadcasted_iota(i32, (KEYW - width, tokens), 0)
    own[width:, :] = jnp.where(segments[...] == mark, 1.0, 0.0).astype(bf16)


def nt_dot(a, b):
    return lax.dot_general(a, b, (((1,), (1,)), ((), ())), preferred_element_type=f32)


def attend_chunks(rows, chunks, biases, scores, old):
    scale = QKDIM ** (-0.5)
    peak = jnp.full((256, 128), -FAR, f32) if old is None else old[0]
    for n, (chunk, bias) in enumerate(zip(chunks, biases)):
        part = bias(jnp.dot(rows, chunk[...], preferred_element_type=f32) * scale)
        scores[:, n * 256 : (n + 1) * 256] = part
        peak = jnp.maximum(peak, jnp.maximum(part[:, :128], part[:, 128:]))
    peak = jnp.max(peak, axis=1, keepdims=True)
    if old is None:
        sums, mixed = jnp.zeros((256, 128), f32), jnp.zeros((256, LATENT), f32)
    else:
        factor = jnp.exp(old[0][:, :1] - peak)
        sums, mixed = old[1] * factor, old[2] * factor
    for n, chunk in enumerate(chunks):
        terms = jnp.exp(scores[:, n * 256 : (n + 1) * 256] - peak)
        sums = sums + terms[:, :128] + terms[:, 128:]
        mixed = mixed + nt_dot(terms.astype(bf16), chunk[:LATENT, :])
    return jnp.broadcast_to(peak, (256, 128)), sums, mixed


def valid_bias(info, n):
    return lambda part: part + jnp.where(info[n] >= 0, 0.0, -FAR)


def causal_bias(part):
    lane = lax.broadcasted_iota(i32, (256, 256), 1)
    row = lax.broadcasted_iota(i32, (256, 256), 0)
    token = (row % 128) // 8 * 16 + row // 128 * 8 + row % 8
    return jnp.where(lane <= token, part, -FAR)


def first_attention_kernel(info, query, own, p0, peak, sums, mixed, scores):
    for head in range(2):
        state = attend_chunks(
            query[head], [own, p0], [causal_bias, valid_bias(info, 0)], scores.at[head], None
        )
        peak[head], sums[head], mixed[head] = state


def second_attention_kernel(
    info, query, p1, p2, p3, o0, old_peak, old_sums, old_mixed, peak, sums, mixed, scores
):
    for head in range(2):
        old = old_peak[head], old_sums[head], old_mixed[head]
        biases = [valid_bias(info, n) for n in (1, 2, 3, 4)]
        state = attend_chunks(query[head], [p1, p2, p3, o0], biases, scores.at[head], old)
        peak[head], sums[head], mixed[head] = state


def last_attention_kernel(
    info, query, others, old_peak, old_sums, old_mixed, value_up, out_proj, send, keep, scores, values
):
    core = info[8]

    for head in range(2):
        old = old_peak[head], old_sums[head], old_mixed[head]
        chunks = [others.at[n] for n in range(3)]
        biases = [valid_bias(info, n) for n in (5, 6, 7)]
        _, sums, mixed = attend_chunks(query[head], chunks, biases, scores.at[head], old)
        mixed = (mixed / jnp.sum(sums, axis=1, keepdims=True)).astype(bf16)
        values[head] = jnp.dot(mixed, value_up[head], preferred_element_type=f32).astype(bf16)

    def project(which, out):
        start = pl.multiple_of(which * 128, 128)
        both = jnp.concatenate([values[head, pl.ds(start, 128), :] for head in range(2)], axis=1)
        for c in range(0, out.shape[1], 640):
            out[:, c : c + 640] = jnp.dot(
                both, out_proj[:, c : c + 640], preferred_element_type=f32
            ).astype(out.dtype)

    project(1 - core, send)
    project(core, keep)


def add_kernel(keep, got, out):
    out[...] = (keep[...] + got[...].astype(f32)).reshape(out.shape).astype(bf16)


def gather_kernel(p1, p2, p3, out):
    for n, piece in enumerate((p1, p2, p3)):
        out[n] = piece[...]


def norm_kernel(spread, residual, gain, packed):
    attended = jnp.sum(spread[...].astype(f32), axis=0)
    stream = (residual[...].astype(f32) + attended).astype(bf16).astype(f32)
    mean_sq = jnp.mean(stream * stream, axis=1, keepdims=True)
    normed = (stream * lax.rsqrt(mean_sq + 1e-06) * gain[...]).astype(bf16).astype(f32)
    width = stream.shape[1] // 16
    fill = jnp.zeros((stream.shape[0], packed.shape[2] - 3 * width), f32)
    for c in range(16):
        mine, other = c * width, (c ^ 1) * width
        packed[c] = jnp.concatenate(
            [
                normed[:, mine : mine + width],
                normed[:, other : other + width],
                stream[:, mine : mine + width],
                fill,
            ],
            axis=1,
        ).astype(bf16)


def store_packed(out, n, rows):
    left = lax.broadcasted_iota(i32, (SLOTS // 2, 128), 1) < 64
    out[n, 0:32] = rows[:, :128].astype(bf16)
    out[n, 32:64] = rows[:, 128:256].astype(bf16)
    out[n, 64:80] = jnp.where(left, rows[:16, 256:], rows[16:, 256:]).astype(bf16)


def load_packed(ref, n):
    last = ref[n, 64:80]
    left = jnp.where(lax.broadcasted_iota(i32, (1, 128), 1) < 64, 1.0, 0.0).astype(bf16)
    last = jnp.concatenate([last * left, last * (1 - left)], axis=0)
    return jnp.concatenate([ref[n, 0:32], ref[n, 32:64], last], axis=1)


def pick_kernel(picker, split, out):
    values = split[:, :384]
    doubled = jnp.concatenate([values[:, :320], values[:, 256:320]], axis=1)
    for r in range(0, picker.shape[0], 256):
        rows = jnp.dot(picker[r : r + 256, :], doubled, preferred_element_type=f32)
        for n in range(256 // SLOTS):
            store_packed(out, r // SLOTS + n, rows[n * SLOTS : (n + 1) * SLOTS])


def row_mask(count, j):
    slot = lax.broadcasted_iota(i32, (count, 1), 0) % SLOTS
    return jnp.where((slot >= j * CAP) & (slot < (j + 1) * CAP), 1.0, 0.0).astype(bf16)


def spread_experts(rows, masks):
    return jnp.concatenate([rows * mask for mask in masks], axis=1)


def split_weights_kernel(info, gate, up, down, in_send, in_keep, down_send, down_keep):
    half = gate.shape[2] // 2

    def move(into, onto, start):
        into[:, :, :half] = gate[:, :, start : start + half]
        into[:, :, half:] = up[:, :, start : start + half]
        onto[...] = down[:, :, start : start + half]

    @pl.when(info[9] == 0)
    def _():
        move(in_keep, down_keep, 0)
        move(in_send, down_send, half)

    @pl.when(info[9] != 0)
    def _():
        move(in_keep, down_keep, half)
        move(in_send, down_send, 0)


def join_in_kernel(keep, got, out):
    rows = keep.shape[1]
    for j in range(3):
        base = j * 384
        out[base : base + rows, :] = keep[j]
        out[base + rows : base + 2 * rows, :] = got[j]
        out[base + 2 * rows : base + 384, :] = got[j, 256 - rows :]


def join_down_kernel(keep, got, out):
    rows, width = keep.shape[1:]
    for j in range(3):
        lanes = slice(j * width, (j + 1) * width)
        out[:rows, lanes] = keep[j]
        out[rows : 2 * rows, lanes] = got[j]
        out[2 * rows :, lanes] = got[j, 256 - rows :]


def gate_up_kernel(received, weights, pre):
    masks = [row_mask(256, j) for j in range(3)]
    for r in range(0, received.shape[0], 8):
        rows = jnp.concatenate([load_packed(received, r + n) for n in range(8)], axis=0)
        total = jnp.dot(spread_experts(rows, masks), weights[...], preferred_element_type=f32)
        pre[r * SLOTS : (r + 8) * SLOTS, :] = total.astype(bf16)


def hidden_kernel(parts, out):
    total = jnp.sum(parts[...].astype(f32), axis=0)
    half = total.shape[1] // 2
    gate, up = total[:, :half], total[:, half:]
    hidden = (gate / (1.0 + jnp.exp(-gate)) * up).astype(bf16)
    for n in range(out.shape[0]):
        out[n] = hidden


def down_kernel(hidden, weights, out):
    masks = [row_mask(256, j) for j in range(3)]
    for r in range(0, hidden.shape[0], 256):
        rows = spread_experts(hidden[r : r + 256, :], masks)
        total = nt_dot(rows, weights[...])
        for n in range(256 // SLOTS):
            store_packed(out, r // SLOTS + n, total[n * SLOTS : (n + 1) * SLOTS])


def combine_kernel(weighting, returned, order, stream, keep, send):
    width = keep.shape[1]
    rows = jnp.concatenate([load_packed(returned, n) for n in range(returned.shape[0])], axis=0)
    top = weighting[...].astype(bf16)
    rest = (weighting[...] - top.astype(f32)).astype(bf16)
    mixture = jnp.dot(top, rows, preferred_element_type=f32) + jnp.dot(
        rest, rows, preferred_element_type=f32
    )
    tail = mixture[:, 256:320] + mixture[:, 320:384]
    kept = jnp.dot(order[...], stream[:, 2 * width : 3 * width], preferred_element_type=f32)
    keep[...] = kept + mixture[:, :width]
    send[...] = jnp.concatenate([mixture[:, width:256], tail], axis=1).astype(bf16)


def call(kernel, outs, scratch=(), smem_first=False, count=0):
    specs = [pl.BlockSpec(memory_space=pltpu.VMEM)] * count
    if smem_first:
        specs[0] = pl.BlockSpec(memory_space=pltpu.SMEM)
    out_specs = [pl.BlockSpec(memory_space=pltpu.VMEM)] * len(outs)
    single = len(outs) == 1
    return pl.pallas_call(
        kernel,
        in_specs=specs,
        out_specs=out_specs[0] if single else out_specs,
        out_shape=outs[0] if single else outs,
        scratch_shapes=list(scratch),
        compiler_params=BIG_VMEM,
    )


def sds(shape, dtype):
    return jax.ShapeDtypeStruct(shape, dtype)


def on_device(
    queries,
    latent,
    segment_ids,
    value_up,
    out_proj,
    residual,
    norm_gain,
    route_ids,
    route_gates,
    expert_gate,
    expert_up,
    expert_down,
):
    block_len, local_heads, width_key = queries.shape
    width_model = residual.shape[1]
    width_out = width_model // 16
    width_pair = 2 * width_out
    ff = expert_gate.shape[2]
    ff_half = ff // 2
    y, xl, xh, core = (lax.axis_index(a) for a in ("y", "xl", "xh", "core"))
    half = block_len // 2

    segment_axis = jnp.arange(SEGMENTS, dtype=i32)
    own_segment = segment_ids[:, None] == segment_axis[None, :]
    pad = KEYW - width_key - SEGMENTS
    keys_own = call(keys_kernel, [sds((KEYW, block_len), bf16)], count=2)(
        latent.T, segment_ids[None, :]
    )
    pairs = [
        (4 * i + j, 4 * ((i + 1 + j // 2 + 2 * (j % 2)) % 8) + j) for i in range(8) for j in range(4)
    ]
    fetched = lax.ppermute(keys_own, ("y", "xh", "core"), pairs)

    def block_of(x, h, c):
        return 2 * (y - 1 - h - 2 * c) + x

    def block_sent(x, h, c):
        return jnp.where((x == 0) & (h == 1) & (c == 1), 2 * y, block_of(x, h, c))

    def blocks_held(c):
        own = [block_of(xl, xh, c), block_of(xl, 1 - xh, c)]
        return own + [block_sent(1 - xl, xh, c), block_sent(1 - xl, 1 - xh, c)]

    info = jnp.stack(blocks_held(core) + blocks_held(1 - core) + [core, xl]).astype(i32)

    masks = jnp.where(own_segment, 0.0, -FAR).astype(bf16)
    query_rows = jnp.concatenate(
        [
            queries,
            jnp.broadcast_to(masks[:, None, :], (block_len, local_heads, SEGMENTS)),
            jnp.zeros((block_len, local_heads, pad), bf16),
        ],
        axis=2,
    )
    query_rows = query_rows.reshape(16, 2, 8, local_heads, KEYW).transpose(3, 1, 0, 2, 4)
    query_rows = query_rows.reshape(local_heads, block_len, KEYW)
    in_out = sds((3, width_out, 2 * ff_half), bf16)
    down_out = sds((3, width_out, ff_half), bf16)
    in_send, in_keep, down_send, down_keep = call(
        split_weights_kernel, [in_out, in_out, down_out, down_out], (), True, 4
    )(info, expert_gate, expert_up, jnp.transpose(expert_down, (0, 2, 1)))
    fetched, query_rows, in_send = lax.optimization_barrier((fetched, query_rows, in_send))

    to_other = jnp.where((xl == 0) & (xh == 1) & (core == 1), keys_own, fetched)
    diagonal = [(0, 3), (1, 2), (2, 1), (3, 0)]
    pieces = [
        fetched,
        lax.ppermute(fetched, "xh", SWAP),
        lax.ppermute(to_other, "xl", SWAP),
        lax.ppermute(to_other, ("xl", "xh"), diagonal),
    ]

    state_out = [
        sds((2, 256, 128), f32),
        sds((2, 256, 128), f32),
        sds((2, 256, LATENT), f32),
    ]
    state = call(
        first_attention_kernel, state_out, [pltpu.VMEM((2, 256, 2 * 256), f32)], True, 4
    )(info, query_rows, keys_own, fetched)
    pieces[2], fetched_late, peak = lax.optimization_barrier((pieces[2], fetched, state[0]))
    state = [peak] + list(state[1:])
    first_other = lax.ppermute(fetched_late, "core", SWAP)
    *pieces, first_other = lax.optimization_barrier((*pieces, first_other))
    three = call(gather_kernel, [sds((3, KEYW, block_len), bf16)], count=3)(*pieces[1:])
    others = lax.ppermute(three, "core", SWAP)
    state = call(
        second_attention_kernel, state_out, [pltpu.VMEM((2, 256, 4 * 256), f32)], True, 9
    )(info, query_rows, pieces[1], pieces[2], pieces[3], first_other, *state)
    send, keep = call(
        last_attention_kernel,
        [sds((half, width_model), bf16), sds((half, width_model), f32)],
        [pltpu.VMEM((2, 256, 3 * 256), f32), pltpu.VMEM((2, 256, VDIM), bf16)],
        True,
        8,
    )(info, query_rows, others, *state, value_up, out_proj)
    got = lax.ppermute(send, "core", SWAP)
    pair_sum = call(add_kernel, [sds((16, 8, width_model), bf16)], count=2)(keep, got)

    pair_sum, in_send = lax.optimization_barrier((pair_sum, in_send))
    in_got = lax.ppermute(in_send, "xl", SWAP)

    spread = lax.all_to_all(pair_sum, ("z", "xh"), split_axis=0, concat_axis=0, tiled=True)
    packed = call(norm_kernel, [sds((16, 8, 512), bf16)], count=3)(
        spread, residual, norm_gain[None, :]
    )
    split = lax.all_to_all(packed, CTX, split_axis=0, concat_axis=0, tiled=True)
    split, in_got, down_send = lax.optimization_barrier((split, in_got, down_send))
    down_got = lax.ppermute(down_send, "xl", SWAP)
    split = split.reshape(128, 512)
    w_in = call(join_in_kernel, [sds((3 * 384, 2 * ff_half), bf16)], count=2)(in_keep, in_got)
    w_down = call(join_down_kernel, [sds((384, 3 * ff_half), bf16)], count=2)(down_keep, down_got)

    routes = jnp.transpose(route_ids, (1, 0, 2)).reshape(128, TOPK)
    expert_axis = jnp.arange(EXPERTS, dtype=i32)
    named = jnp.any(routes[:, :, None] == expert_axis[None, None, :], axis=1)
    earlier_tokens = jnp.tril(jnp.ones((128, 128), bf16), -1)
    slot_all = jnp.dot(earlier_tokens, named.astype(bf16), preferred_element_type=f32).astype(i32)
    slot_of = jnp.sum(
        jnp.where(routes[:, :, None] == expert_axis[None, None, :], slot_all[:, None, :], 0), axis=2
    )
    target = (routes // 3) * SLOTS + (routes % 3) * CAP + slot_of
    slot_axis = jnp.arange(32 * SLOTS, dtype=i32)
    picker = jnp.any(target.T[None, :, :] == slot_axis[:, None, None], axis=1).astype(bf16)
    order = jnp.arange(128, dtype=i32)
    back_order = ((order % 16) * 8 + order // 16)[:, None] == order[None, :]
    target_rb = jnp.transpose(target.reshape(16, 8, TOPK), (1, 0, 2)).reshape(128, TOPK)
    gates_rb = route_gates.reshape(128, TOPK)
    weighting = jnp.sum(
        jnp.where(target_rb[:, :, None] == slot_axis[None, None, :], gates_rb[:, :, None], 0.0),
        axis=1,
    )

    travel = sds((32, 80, 128), bf16)
    outgoing = call(pick_kernel, [travel], count=2)(picker, split)
    received = lax.all_to_all(outgoing, EXP, split_axis=0, concat_axis=0, tiled=True)
    received, w_in, w_down = lax.optimization_barrier((received, w_in, w_down))
    pre = call(gate_up_kernel, [sds((32 * SLOTS, 2 * ff_half), bf16)], count=2)(received, w_in)
    pre_parts = lax.all_to_all(
        pre.reshape(8, 128, 2 * ff_half), "y", split_axis=0, concat_axis=0, tiled=True
    )
    hidden = call(hidden_kernel, [sds((8, 128, ff_half), bf16)], count=1)(pre_parts)
    hidden_all = lax.all_to_all(hidden, "y", split_axis=0, concat_axis=0, tiled=True)
    expert_out = call(down_kernel, [travel], count=2)(
        hidden_all.reshape(32 * SLOTS, ff_half), w_down
    )
    returned = lax.all_to_all(expert_out, EXP, split_axis=0, concat_axis=0, tiled=True)
    mix_keep, mix_send = call(
        combine_kernel, [sds((128, width_out), f32), sds((128, width_out), bf16)], count=4
    )(weighting, returned, back_order.astype(bf16), split)
    mix_got = lax.ppermute(mix_send, "xl", SWAP)
    result = (mix_keep + mix_got.astype(f32)).astype(bf16)
    return result.reshape(8, 16, width_out)


def solution(mesh):
    grid = Mesh(mesh.devices.reshape(8, 2, 8, 2, 2), ("y", "xl", "z", "xh", "core"))
    return jax.shard_map(
        on_device,
        mesh=grid,
        in_specs=(
            P(CTX, EXP, None),
            P(CTX, None),
            P(CTX),
            P(EXP, None, None),
            P(EXP, None),
            P(CTX + EXP, None),
            P(),
            P(EXP, None, None),
            P(EXP, None, None),
            P(EXP, CTX, None),
            P(EXP, CTX, None),
            P(EXP, None, CTX),
        ),
        out_specs=P(EXP, None, CTX),
        check_vma=False,
    )
```

```python
import jax
import jax.numpy as jnp
from jax import lax
from jax.experimental import pallas as pl
from jax.experimental.pallas import tpu as pltpu
from jax.sharding import Mesh, PartitionSpec as P

LATENT = 512
VDIM = 128
QKDIM = 192
EXPERTS = 96
TOPK = 6
CAP = 10
SLOTS = 32
SEGMENTS = 8
KEYW = 592
FAR = float(2**20)

CTX = ("y", "xl")
EXP = ("z", "xh", "core")
SWAP = [(0, 1), (1, 0)]
BIG_VMEM = pltpu.CompilerParams(vmem_limit_bytes=20 * 2**20)
f32, bf16, i32 = jnp.float32, jnp.bfloat16, jnp.int32


def keys_kernel(latent, segments, own):
    width, tokens = latent.shape
    own[:width, :] = latent[...]
    mark = lax.broadcasted_iota(i32, (KEYW - width, tokens), 0)
    own[width:, :] = jnp.where(segments[...] == mark, 1.0, 0.0).astype(bf16)


def nt_dot(a, b):
    return lax.dot_general(a, b, (((1,), (1,)), ((), ())), preferred_element_type=f32)


def attend_chunks(rows, chunks, biases, scores, old):
    scale = QKDIM ** (-0.5)
    peak = jnp.full((256, 128), -FAR, f32) if old is None else old[0]
    for n, (chunk, bias) in enumerate(zip(chunks, biases)):
        part = bias(jnp.dot(rows, chunk[...], preferred_element_type=f32) * scale)
        scores[:, n * 256 : (n + 1) * 256] = part
        peak = jnp.maximum(peak, jnp.maximum(part[:, :128], part[:, 128:]))
    peak = jnp.max(peak, axis=1, keepdims=True)
    if old is None:
        sums, mixed = jnp.zeros((256, 128), f32), jnp.zeros((256, LATENT), f32)
    else:
        factor = jnp.exp(old[0][:, :1] - peak)
        sums, mixed = old[1] * factor, old[2] * factor
    for n, chunk in enumerate(chunks):
        terms = jnp.exp(scores[:, n * 256 : (n + 1) * 256] - peak)
        sums = sums + terms[:, :128] + terms[:, 128:]
        mixed = mixed + nt_dot(terms.astype(bf16), chunk[:LATENT, :])
    return jnp.broadcast_to(peak, (256, 128)), sums, mixed


def valid_bias(info, n):
    return lambda part: part + jnp.where(info[n] >= 0, 0.0, -FAR)


def causal_bias(part):
    lane = lax.broadcasted_iota(i32, (256, 256), 1)
    row = lax.broadcasted_iota(i32, (256, 256), 0)
    token = (row % 128) // 8 * 16 + row // 128 * 8 + row % 8
    return jnp.where(lane <= token, part, -FAR)


def first_attention_kernel(info, query, own, p0, peak, sums, mixed, scores):
    for head in range(2):
        state = attend_chunks(
            query[head], [own, p0], [causal_bias, valid_bias(info, 0)], scores.at[head], None
        )
        peak[head], sums[head], mixed[head] = state


def second_attention_kernel(
    info, query, p1, p2, p3, o0, old_peak, old_sums, old_mixed, peak, sums, mixed, scores
):
    for head in range(2):
        old = old_peak[head], old_sums[head], old_mixed[head]
        biases = [valid_bias(info, n) for n in (1, 2, 3, 4)]
        state = attend_chunks(query[head], [p1, p2, p3, o0], biases, scores.at[head], old)
        peak[head], sums[head], mixed[head] = state


def last_attention_kernel(
    info, query, others, old_peak, old_sums, old_mixed, value_up, out_proj, send, keep, scores, values
):
    core = info[8]

    for head in range(2):
        old = old_peak[head], old_sums[head], old_mixed[head]
        chunks = [others.at[n] for n in range(3)]
        biases = [valid_bias(info, n) for n in (5, 6, 7)]
        _, sums, mixed = attend_chunks(query[head], chunks, biases, scores.at[head], old)
        mixed = (mixed / jnp.sum(sums, axis=1, keepdims=True)).astype(bf16)
        values[head] = jnp.dot(mixed, value_up[head], preferred_element_type=f32).astype(bf16)

    def project(which, out):
        start = pl.multiple_of(which * 128, 128)
        both = jnp.concatenate([values[head, pl.ds(start, 128), :] for head in range(2)], axis=1)
        for c in range(0, out.shape[1], 640):
            out[:, c : c + 640] = jnp.dot(
                both, out_proj[:, c : c + 640], preferred_element_type=f32
            ).astype(out.dtype)

    project(1 - core, send)
    project(core, keep)


def add_kernel(keep, got, out):
    out[...] = (keep[...] + got[...].astype(f32)).reshape(out.shape).astype(bf16)


def gather_kernel(p1, p2, p3, out):
    for n, piece in enumerate((p1, p2, p3)):
        out[n] = piece[...]


def norm_kernel(spread, residual, gain, packed):
    attended = jnp.sum(spread[...].astype(f32), axis=0)
    stream = (residual[...].astype(f32) + attended).astype(bf16).astype(f32)
    mean_sq = jnp.mean(stream * stream, axis=1, keepdims=True)
    normed = (stream * lax.rsqrt(mean_sq + 1e-06) * gain[...]).astype(bf16).astype(f32)
    width = stream.shape[1] // 16
    fill = jnp.zeros((stream.shape[0], packed.shape[2] - 3 * width), f32)
    for c in range(16):
        mine, other = c * width, (c ^ 1) * width
        packed[c] = jnp.concatenate(
            [
                normed[:, mine : mine + width],
                normed[:, other : other + width],
                stream[:, mine : mine + width],
                fill,
            ],
            axis=1,
        ).astype(bf16)


def store_packed(out, n, rows):
    left = lax.broadcasted_iota(i32, (SLOTS // 2, 128), 1) < 64
    out[n, 0:32] = rows[:, :128].astype(bf16)
    out[n, 32:64] = rows[:, 128:256].astype(bf16)
    out[n, 64:80] = jnp.where(left, rows[:16, 256:], rows[16:, 256:]).astype(bf16)


def load_packed(ref, n):
    last = ref[n, 64:80]
    left = jnp.where(lax.broadcasted_iota(i32, (1, 128), 1) < 64, 1.0, 0.0).astype(bf16)
    last = jnp.concatenate([last * left, last * (1 - left)], axis=0)
    return jnp.concatenate([ref[n, 0:32], ref[n, 32:64], last], axis=1)


def pick_kernel(picker, split, out):
    values = split[:, :384]
    doubled = jnp.concatenate([values[:, :320], values[:, 256:320]], axis=1)
    step = 512
    for r in range(0, picker.shape[0], step):
        rows = jnp.dot(picker[r : r + step, :], doubled, preferred_element_type=f32)
        for n in range(step // SLOTS):
            store_packed(out, r // SLOTS + n, rows[n * SLOTS : (n + 1) * SLOTS])


def row_mask(count, j):
    slot = lax.broadcasted_iota(i32, (count, 1), 0) % SLOTS
    return jnp.where((slot >= j * CAP) & (slot < (j + 1) * CAP), 1.0, 0.0).astype(bf16)


def spread_experts(rows, masks):
    return jnp.concatenate([rows * mask for mask in masks], axis=1)


def split_weights_kernel(info, gate, up, down, in_send, in_keep, down_send, down_keep):
    half = gate.shape[2] // 2

    def move(into, onto, start):
        into[:, :, :half] = gate[:, :, start : start + half]
        into[:, :, half:] = up[:, :, start : start + half]
        onto[...] = down[:, :, start : start + half]

    @pl.when(info[9] == 0)
    def _():
        move(in_keep, down_keep, 0)
        move(in_send, down_send, half)

    @pl.when(info[9] != 0)
    def _():
        move(in_keep, down_keep, half)
        move(in_send, down_send, 0)


def join_in_kernel(keep, got, out):
    rows = keep.shape[1]
    for j in range(3):
        base = j * 384
        out[base : base + rows, :] = keep[j]
        out[base + rows : base + 2 * rows, :] = got[j]
        out[base + 2 * rows : base + 384, :] = got[j, 256 - rows :]


def join_down_kernel(keep, got, out):
    rows, width = keep.shape[1:]
    for j in range(3):
        lanes = slice(j * width, (j + 1) * width)
        out[:rows, lanes] = keep[j]
        out[rows : 2 * rows, lanes] = got[j]
        out[2 * rows :, lanes] = got[j, 256 - rows :]


def gate_up_kernel(received, weights, pre):
    masks = [row_mask(256, j) for j in range(3)]
    for r in range(0, received.shape[0], 8):
        rows = jnp.concatenate([load_packed(received, r + n) for n in range(8)], axis=0)
        total = jnp.dot(spread_experts(rows, masks), weights[...], preferred_element_type=f32)
        pre[r * SLOTS : (r + 8) * SLOTS, :] = total.astype(bf16)


def hidden_kernel(parts, out):
    total = jnp.sum(parts[...].astype(f32), axis=0)
    half = total.shape[1] // 2
    gate, up = total[:, :half], total[:, half:]
    hidden = (gate / (1.0 + jnp.exp(-gate)) * up).astype(bf16)
    for n in range(out.shape[0]):
        out[n] = hidden


def down_kernel(hidden, weights, out):
    step = 512
    masks = [row_mask(step, j) for j in range(3)]
    for r in range(0, hidden.shape[0], step):
        rows = spread_experts(hidden[r : r + step, :], masks)
        total = nt_dot(rows, weights[...])
        for n in range(step // SLOTS):
            store_packed(out, r // SLOTS + n, total[n * SLOTS : (n + 1) * SLOTS])


def combine_kernel(weighting, returned, order, stream, keep, send):
    width = keep.shape[1]
    rows = jnp.concatenate([load_packed(returned, n) for n in range(returned.shape[0])], axis=0)
    top = weighting[...].astype(bf16)
    rest = (weighting[...] - top.astype(f32)).astype(bf16)
    mixture = jnp.dot(top, rows, preferred_element_type=f32) + jnp.dot(
        rest, rows, preferred_element_type=f32
    )
    tail = mixture[:, 256:320] + mixture[:, 320:384]
    kept = jnp.dot(order[...], stream[:, 2 * width : 3 * width], preferred_element_type=f32)
    keep[...] = kept + mixture[:, :width]
    send[...] = jnp.concatenate([mixture[:, width:256], tail], axis=1).astype(bf16)


def call(kernel, outs, scratch=(), smem_first=False, count=0):
    specs = [pl.BlockSpec(memory_space=pltpu.VMEM)] * count
    if smem_first:
        specs[0] = pl.BlockSpec(memory_space=pltpu.SMEM)
    out_specs = [pl.BlockSpec(memory_space=pltpu.VMEM)] * len(outs)
    single = len(outs) == 1
    return pl.pallas_call(
        kernel,
        in_specs=specs,
        out_specs=out_specs[0] if single else out_specs,
        out_shape=outs[0] if single else outs,
        scratch_shapes=list(scratch),
        compiler_params=BIG_VMEM,
    )


def sds(shape, dtype):
    return jax.ShapeDtypeStruct(shape, dtype)


def on_device(
    queries,
    latent,
    segment_ids,
    value_up,
    out_proj,
    residual,
    norm_gain,
    route_ids,
    route_gates,
    expert_gate,
    expert_up,
    expert_down,
):
    block_len, local_heads, width_key = queries.shape
    width_model = residual.shape[1]
    width_out = width_model // 16
    width_pair = 2 * width_out
    ff = expert_gate.shape[2]
    ff_half = ff // 2
    y, xl, xh, core = (lax.axis_index(a) for a in ("y", "xl", "xh", "core"))
    half = block_len // 2

    segment_axis = jnp.arange(SEGMENTS, dtype=i32)
    own_segment = segment_ids[:, None] == segment_axis[None, :]
    pad = KEYW - width_key - SEGMENTS
    keys_own = call(keys_kernel, [sds((KEYW, block_len), bf16)], count=2)(
        latent.T, segment_ids[None, :]
    )
    pairs = [
        (4 * i + j, 4 * ((i + 1 + j // 2 + 2 * (j % 2)) % 8) + j) for i in range(8) for j in range(4)
    ]
    fetched = lax.ppermute(keys_own, ("y", "xh", "core"), pairs)

    def block_of(x, h, c):
        return 2 * (y - 1 - h - 2 * c) + x

    def block_sent(x, h, c):
        return jnp.where((x == 0) & (h == 1) & (c == 1), 2 * y, block_of(x, h, c))

    def blocks_held(c):
        own = [block_of(xl, xh, c), block_of(xl, 1 - xh, c)]
        return own + [block_sent(1 - xl, xh, c), block_sent(1 - xl, 1 - xh, c)]

    info = jnp.stack(blocks_held(core) + blocks_held(1 - core) + [core, xl]).astype(i32)

    masks = jnp.where(own_segment, 0.0, -FAR).astype(bf16)
    query_rows = jnp.concatenate(
        [
            queries,
            jnp.broadcast_to(masks[:, None, :], (block_len, local_heads, SEGMENTS)),
            jnp.zeros((block_len, local_heads, pad), bf16),
        ],
        axis=2,
    )
    query_rows = query_rows.reshape(16, 2, 8, local_heads, KEYW).transpose(3, 1, 0, 2, 4)
    query_rows = query_rows.reshape(local_heads, block_len, KEYW)
    fetched, query_rows = lax.optimization_barrier((fetched, query_rows))

    to_other = jnp.where((xl == 0) & (xh == 1) & (core == 1), keys_own, fetched)
    diagonal = [(0, 3), (1, 2), (2, 1), (3, 0)]
    pieces = [
        fetched,
        lax.ppermute(fetched, "xh", SWAP),
        lax.ppermute(to_other, "xl", SWAP),
        lax.ppermute(to_other, ("xl", "xh"), diagonal),
    ]

    state_out = [
        sds((2, 256, 128), f32),
        sds((2, 256, 128), f32),
        sds((2, 256, LATENT), f32),
    ]
    state = call(
        first_attention_kernel, state_out, [pltpu.VMEM((2, 256, 2 * 256), f32)], True, 4
    )(info, query_rows, keys_own, fetched)
    pieces[1], fetched_late, peak = lax.optimization_barrier((pieces[1], fetched, state[0]))
    state = [peak] + list(state[1:])
    first_other = lax.ppermute(fetched_late, "core", SWAP)
    *pieces, first_other = lax.optimization_barrier((*pieces, first_other))
    three = call(gather_kernel, [sds((3, KEYW, block_len), bf16)], count=3)(*pieces[1:])
    others = lax.ppermute(three, "core", SWAP)
    state = call(
        second_attention_kernel, state_out, [pltpu.VMEM((2, 256, 4 * 256), f32)], True, 9
    )(info, query_rows, pieces[1], pieces[2], pieces[3], first_other, *state)
    send, keep = call(
        last_attention_kernel,
        [sds((half, width_model), bf16), sds((half, width_model), f32)],
        [pltpu.VMEM((2, 256, 3 * 256), f32), pltpu.VMEM((2, 256, VDIM), bf16)],
        True,
        8,
    )(info, query_rows, others, *state, value_up, out_proj)
    got = lax.ppermute(send, "core", SWAP)
    pair_sum = call(add_kernel, [sds((16, 8, width_model), bf16)], count=2)(keep, got)

    in_out = sds((3, width_out, 2 * ff_half), bf16)
    down_out = sds((3, width_out, ff_half), bf16)
    in_send, in_keep, down_send, down_keep = call(
        split_weights_kernel, [in_out, in_out, down_out, down_out], (), True, 4
    )(info, expert_gate, expert_up, jnp.transpose(expert_down, (0, 2, 1)))
    pair_sum, in_send = lax.optimization_barrier((pair_sum, in_send))
    in_got = lax.ppermute(in_send, "xl", SWAP)

    spread = lax.all_to_all(pair_sum, ("z", "xh"), split_axis=0, concat_axis=0, tiled=True)
    packed = call(norm_kernel, [sds((16, 8, 512), bf16)], count=3)(
        spread, residual, norm_gain[None, :]
    )
    split = lax.all_to_all(packed, CTX, split_axis=0, concat_axis=0, tiled=True)
    split, in_got, down_send = lax.optimization_barrier((split, in_got, down_send))
    down_got = lax.ppermute(down_send, "xl", SWAP)
    split = split.reshape(128, 512)
    w_in = call(join_in_kernel, [sds((3 * 384, 2 * ff_half), bf16)], count=2)(in_keep, in_got)
    w_down = call(join_down_kernel, [sds((384, 3 * ff_half), bf16)], count=2)(down_keep, down_got)

    routes = jnp.transpose(route_ids, (1, 0, 2)).reshape(128, TOPK)
    expert_axis = jnp.arange(EXPERTS, dtype=i32)
    named = jnp.any(routes[:, :, None] == expert_axis[None, None, :], axis=1)
    earlier_tokens = jnp.tril(jnp.ones((128, 128), bf16), -1)
    slot_all = jnp.dot(earlier_tokens, named.astype(bf16), preferred_element_type=f32).astype(i32)
    slot_of = jnp.sum(
        jnp.where(routes[:, :, None] == expert_axis[None, None, :], slot_all[:, None, :], 0), axis=2
    )
    target = (routes // 3) * SLOTS + (routes % 3) * CAP + slot_of
    slot_axis = jnp.arange(32 * SLOTS, dtype=i32)
    picker = jnp.any(target.T[None, :, :] == slot_axis[:, None, None], axis=1).astype(bf16)
    order = jnp.arange(128, dtype=i32)
    back_order = ((order % 16) * 8 + order // 16)[:, None] == order[None, :]
    target_rb = jnp.transpose(target.reshape(16, 8, TOPK), (1, 0, 2)).reshape(128, TOPK)
    gates_rb = route_gates.reshape(128, TOPK)
    weighting = jnp.sum(
        jnp.where(target_rb[:, :, None] == slot_axis[None, None, :], gates_rb[:, :, None], 0.0),
        axis=1,
    )

    travel = sds((32, 80, 128), bf16)
    outgoing = call(pick_kernel, [travel], count=2)(picker, split)
    received = lax.all_to_all(outgoing, EXP, split_axis=0, concat_axis=0, tiled=True)
    received, w_in, w_down = lax.optimization_barrier((received, w_in, w_down))
    pre = call(gate_up_kernel, [sds((32 * SLOTS, 2 * ff_half), bf16)], count=2)(received, w_in)
    pre_parts = lax.all_to_all(
        pre.reshape(8, 128, 2 * ff_half), "y", split_axis=0, concat_axis=0, tiled=True
    )
    hidden = call(hidden_kernel, [sds((8, 128, ff_half), bf16)], count=1)(pre_parts)
    hidden_all = lax.all_to_all(hidden, "y", split_axis=0, concat_axis=0, tiled=True)
    expert_out = call(down_kernel, [travel], count=2)(
        hidden_all.reshape(32 * SLOTS, ff_half), w_down
    )
    returned = lax.all_to_all(expert_out, EXP, split_axis=0, concat_axis=0, tiled=True)
    mix_keep, mix_send = call(
        combine_kernel, [sds((128, width_out), f32), sds((128, width_out), bf16)], count=4
    )(weighting, returned, back_order.astype(bf16), split)
    mix_got = lax.ppermute(mix_send, "xl", SWAP)
    result = (mix_keep + mix_got.astype(f32)).astype(bf16)
    return result.reshape(8, 16, width_out)


def solution(mesh):
    grid = Mesh(mesh.devices.reshape(8, 2, 8, 2, 2), ("y", "xl", "z", "xh", "core"))
    return jax.shard_map(
        on_device,
        mesh=grid,
        in_specs=(
            P(CTX, EXP, None),
            P(CTX, None),
            P(CTX),
            P(EXP, None, None),
            P(EXP, None),
            P(CTX + EXP, None),
            P(),
            P(EXP, None, None),
            P(EXP, None, None),
            P(EXP, CTX, None),
            P(EXP, CTX, None),
            P(EXP, None, CTX),
        ),
        out_specs=P(EXP, None, CTX),
        check_vma=False,
    )
```

```python
import jax
import jax.numpy as jnp
from jax import lax
from jax.experimental import pallas as pl
from jax.experimental.pallas import tpu as pltpu
from jax.sharding import Mesh, PartitionSpec as P

LATENT = 512
VDIM = 128
QKDIM = 192
EXPERTS = 96
TOPK = 6
CAP = 10
SLOTS = 32
SEGMENTS = 8
KEYW = 592
FAR = float(2**20)

CTX = ("y", "xl")
EXP = ("z", "xh", "core")
SWAP = [(0, 1), (1, 0)]
BIG_VMEM = pltpu.CompilerParams(vmem_limit_bytes=20 * 2**20)
f32, bf16, i32 = jnp.float32, jnp.bfloat16, jnp.int32


def keys_kernel(latent, segments, own):
    width, tokens = latent.shape
    own[:width, :] = latent[...]
    mark = lax.broadcasted_iota(i32, (KEYW - width, tokens), 0)
    own[width:, :] = jnp.where(segments[...] == mark, 1.0, 0.0).astype(bf16)


def nt_dot(a, b):
    return lax.dot_general(a, b, (((1,), (1,)), ((), ())), preferred_element_type=f32)


def attend_chunks(rows, chunks, biases, scores, old):
    scale = QKDIM ** (-0.5)
    peak = jnp.full((256, 128), -FAR, f32) if old is None else old[0]
    for n, (chunk, bias) in enumerate(zip(chunks, biases)):
        part = bias(jnp.dot(rows, chunk[...], preferred_element_type=f32) * scale)
        scores[:, n * 256 : (n + 1) * 256] = part
        peak = jnp.maximum(peak, jnp.maximum(part[:, :128], part[:, 128:]))
    peak = jnp.max(peak, axis=1, keepdims=True)
    if old is None:
        sums, mixed = jnp.zeros((256, 128), f32), jnp.zeros((256, LATENT), f32)
    else:
        factor = jnp.exp(old[0][:, :1] - peak)
        sums, mixed = old[1] * factor, old[2] * factor
    for n, chunk in enumerate(chunks):
        terms = jnp.exp(scores[:, n * 256 : (n + 1) * 256] - peak)
        sums = sums + terms[:, :128] + terms[:, 128:]
        mixed = mixed + nt_dot(terms.astype(bf16), chunk[:LATENT, :])
    return jnp.broadcast_to(peak, (256, 128)), sums, mixed


def valid_bias(info, n):
    return lambda part: part + jnp.where(info[n] >= 0, 0.0, -FAR)


def causal_bias(part):
    lane = lax.broadcasted_iota(i32, (256, 256), 1)
    row = lax.broadcasted_iota(i32, (256, 256), 0)
    token = (row % 128) // 8 * 16 + row // 128 * 8 + row % 8
    return jnp.where(lane <= token, part, -FAR)


def first_attention_kernel(info, query, own, p0, peak, sums, mixed, scores):
    for head in range(2):
        state = attend_chunks(
            query[head], [own, p0], [causal_bias, valid_bias(info, 0)], scores.at[head], None
        )
        peak[head], sums[head], mixed[head] = state


def second_attention_kernel(
    info, query, p1, p2, p3, o0, old_peak, old_sums, old_mixed, peak, sums, mixed, scores
):
    for head in range(2):
        old = old_peak[head], old_sums[head], old_mixed[head]
        biases = [valid_bias(info, n) for n in (1, 2, 3, 4)]
        state = attend_chunks(query[head], [p1, p2, p3, o0], biases, scores.at[head], old)
        peak[head], sums[head], mixed[head] = state


def last_attention_kernel(
    info, query, others, old_peak, old_sums, old_mixed, value_up, out_proj, send, keep, scores, values
):
    core = info[8]

    for head in range(2):
        old = old_peak[head], old_sums[head], old_mixed[head]
        chunks = [others.at[n] for n in range(3)]
        biases = [valid_bias(info, n) for n in (5, 6, 7)]
        _, sums, mixed = attend_chunks(query[head], chunks, biases, scores.at[head], old)
        mixed = (mixed / jnp.sum(sums, axis=1, keepdims=True)).astype(bf16)
        values[head] = jnp.dot(mixed, value_up[head], preferred_element_type=f32).astype(bf16)

    def project(which, out):
        start = pl.multiple_of(which * 128, 128)
        both = jnp.concatenate([values[head, pl.ds(start, 128), :] for head in range(2)], axis=1)
        for c in range(0, out.shape[1], 640):
            out[:, c : c + 640] = jnp.dot(
                both, out_proj[:, c : c + 640], preferred_element_type=f32
            ).astype(out.dtype)

    project(1 - core, send)
    project(core, keep)


def add_kernel(keep, got, out):
    out[...] = (keep[...].astype(f32) + got[...].astype(f32)).reshape(out.shape).astype(bf16)


def gather_kernel(p1, p2, p3, out):
    for n, piece in enumerate((p1, p2, p3)):
        out[n] = piece[...]


def norm_kernel(spread, residual, gain, packed):
    attended = jnp.sum(spread[...].astype(f32), axis=0)
    stream = (residual[...].astype(f32) + attended).astype(bf16).astype(f32)
    mean_sq = jnp.mean(stream * stream, axis=1, keepdims=True)
    normed = (stream * lax.rsqrt(mean_sq + 1e-06) * gain[...]).astype(bf16).astype(f32)
    width = stream.shape[1] // 16
    fill = jnp.zeros((stream.shape[0], packed.shape[2] - 3 * width), f32)
    for c in range(16):
        mine, other = c * width, (c ^ 1) * width
        packed[c] = jnp.concatenate(
            [
                normed[:, mine : mine + width],
                normed[:, other : other + width],
                stream[:, mine : mine + width],
                fill,
            ],
            axis=1,
        ).astype(bf16)


def store_packed(out, n, rows):
    left = lax.broadcasted_iota(i32, (SLOTS // 2, 128), 1) < 64
    out[n, 0:32] = rows[:, :128].astype(bf16)
    out[n, 32:64] = rows[:, 128:256].astype(bf16)
    out[n, 64:80] = jnp.where(left, rows[:16, 256:], rows[16:, 256:]).astype(bf16)


def load_packed(ref, n):
    last = ref[n, 64:80]
    left = jnp.where(lax.broadcasted_iota(i32, (1, 128), 1) < 64, 1.0, 0.0).astype(bf16)
    last = jnp.concatenate([last * left, last * (1 - left)], axis=0)
    return jnp.concatenate([ref[n, 0:32], ref[n, 32:64], last], axis=1)


def pick_kernel(picker, split, out):
    values = split[:, :384]
    doubled = jnp.concatenate([values[:, :320], values[:, 256:320]], axis=1)
    step = 512
    for r in range(0, picker.shape[0], step):
        rows = jnp.dot(picker[r : r + step, :], doubled, preferred_element_type=f32)
        for n in range(step // SLOTS):
            store_packed(out, r // SLOTS + n, rows[n * SLOTS : (n + 1) * SLOTS])


def row_mask(count, j):
    slot = lax.broadcasted_iota(i32, (count, 1), 0) % SLOTS
    return jnp.where((slot >= j * CAP) & (slot < (j + 1) * CAP), 1.0, 0.0).astype(bf16)


def spread_experts(rows, masks):
    return jnp.concatenate([rows * mask for mask in masks], axis=1)


def split_weights_kernel(info, gate, up, down, in_send, in_keep, down_send, down_keep):
    half = gate.shape[2] // 2

    def move(into, onto, start):
        into[:, :, :half] = gate[:, :, start : start + half]
        into[:, :, half:] = up[:, :, start : start + half]
        onto[...] = down[:, :, start : start + half]

    @pl.when(info[9] == 0)
    def _():
        move(in_keep, down_keep, 0)
        move(in_send, down_send, half)

    @pl.when(info[9] != 0)
    def _():
        move(in_keep, down_keep, half)
        move(in_send, down_send, 0)


def join_in_kernel(keep, got, out):
    rows = keep.shape[1]
    for j in range(3):
        base = j * 384
        out[base : base + rows, :] = keep[j]
        out[base + rows : base + 2 * rows, :] = got[j]
        out[base + 2 * rows : base + 384, :] = got[j, 256 - rows :]


def join_down_kernel(keep, got, out):
    rows, width = keep.shape[1:]
    for j in range(3):
        parts = [keep[j], got[j], got[j, 256 - rows :]]
        joined = jnp.concatenate([part.astype(f32) for part in parts], axis=0)
        out[j * width : (j + 1) * width, :] = joined.T.astype(bf16)


def gate_up_kernel(received, weights, pre):
    masks = [row_mask(256, j) for j in range(3)]
    for r in range(0, received.shape[0], 8):
        rows = jnp.concatenate([load_packed(received, r + n) for n in range(8)], axis=0)
        total = jnp.dot(spread_experts(rows, masks), weights[...], preferred_element_type=f32)
        pre[r * SLOTS : (r + 8) * SLOTS, :] = total.astype(bf16)


def hidden_kernel(parts, out):
    total = jnp.sum(parts[...].astype(f32), axis=0)
    half = total.shape[1] // 2
    gate, up = total[:, :half], total[:, half:]
    hidden = (gate / (1.0 + jnp.exp(-gate)) * up).astype(bf16)
    for n in range(out.shape[0]):
        out[n] = hidden


def down_kernel(hidden, weights, out):
    step = 512
    masks = [row_mask(step, j) for j in range(3)]
    for r in range(0, hidden.shape[0], step):
        rows = spread_experts(hidden[r : r + step, :], masks)
        total = jnp.dot(rows, weights[...], preferred_element_type=f32)
        for n in range(step // SLOTS):
            store_packed(out, r // SLOTS + n, total[n * SLOTS : (n + 1) * SLOTS])


def combine_kernel(weighting, returned, order, stream, keep, send):
    width = keep.shape[1]
    rows = jnp.concatenate([load_packed(returned, n) for n in range(returned.shape[0])], axis=0)
    top = weighting[...].astype(bf16)
    rest = (weighting[...] - top.astype(f32)).astype(bf16)
    mixture = jnp.dot(top, rows, preferred_element_type=f32) + jnp.dot(
        rest, rows, preferred_element_type=f32
    )
    tail = mixture[:, 256:320] + mixture[:, 320:384]
    kept = jnp.dot(order[...], stream[:, 2 * width : 3 * width], preferred_element_type=f32)
    keep[...] = kept + mixture[:, :width]
    send[...] = jnp.concatenate([mixture[:, width:256], tail], axis=1).astype(bf16)


def call(kernel, outs, scratch=(), smem_first=False, count=0):
    specs = [pl.BlockSpec(memory_space=pltpu.VMEM)] * count
    if smem_first:
        specs[0] = pl.BlockSpec(memory_space=pltpu.SMEM)
    out_specs = [pl.BlockSpec(memory_space=pltpu.VMEM)] * len(outs)
    single = len(outs) == 1
    return pl.pallas_call(
        kernel,
        in_specs=specs,
        out_specs=out_specs[0] if single else out_specs,
        out_shape=outs[0] if single else outs,
        scratch_shapes=list(scratch),
        compiler_params=BIG_VMEM,
    )


def sds(shape, dtype):
    return jax.ShapeDtypeStruct(shape, dtype)


def on_device(
    queries,
    latent,
    segment_ids,
    value_up,
    out_proj,
    residual,
    norm_gain,
    route_ids,
    route_gates,
    expert_gate,
    expert_up,
    expert_down,
):
    block_len, local_heads, width_key = queries.shape
    width_model = residual.shape[1]
    width_out = width_model // 16
    width_pair = 2 * width_out
    ff = expert_gate.shape[2]
    ff_half = ff // 2
    y, xl, xh, core = (lax.axis_index(a) for a in ("y", "xl", "xh", "core"))
    half = block_len // 2

    segment_axis = jnp.arange(SEGMENTS, dtype=i32)
    own_segment = segment_ids[:, None] == segment_axis[None, :]
    pad = KEYW - width_key - SEGMENTS
    keys_own = call(keys_kernel, [sds((KEYW, block_len), bf16)], count=2)(
        latent.T, segment_ids[None, :]
    )
    pairs = [
        (4 * i + j, 4 * ((i + 1 + j // 2 + 2 * (j % 2)) % 8) + j) for i in range(8) for j in range(4)
    ]
    fetched = lax.ppermute(keys_own, ("y", "xh", "core"), pairs)

    def block_of(x, h, c):
        return 2 * (y - 1 - h - 2 * c) + x

    def block_sent(x, h, c):
        return jnp.where((x == 0) & (h == 1) & (c == 1), 2 * y, block_of(x, h, c))

    def blocks_held(c):
        own = [block_of(xl, xh, c), block_of(xl, 1 - xh, c)]
        return own + [block_sent(1 - xl, xh, c), block_sent(1 - xl, 1 - xh, c)]

    info = jnp.stack(blocks_held(core) + blocks_held(1 - core) + [core, xl]).astype(i32)

    masks = jnp.where(own_segment, 0.0, -FAR).astype(bf16)
    query_rows = jnp.concatenate(
        [
            queries,
            jnp.broadcast_to(masks[:, None, :], (block_len, local_heads, SEGMENTS)),
            jnp.zeros((block_len, local_heads, pad), bf16),
        ],
        axis=2,
    )
    query_rows = query_rows.reshape(16, 2, 8, local_heads, KEYW).transpose(3, 1, 0, 2, 4)
    query_rows = query_rows.reshape(local_heads, block_len, KEYW)
    fetched, query_rows = lax.optimization_barrier((fetched, query_rows))

    to_other = jnp.where((xl == 0) & (xh == 1) & (core == 1), keys_own, fetched)
    diagonal = [(0, 3), (1, 2), (2, 1), (3, 0)]
    pieces = [
        fetched,
        lax.ppermute(fetched, "xh", SWAP),
        lax.ppermute(to_other, "xl", SWAP),
        lax.ppermute(to_other, ("xl", "xh"), diagonal),
    ]

    state_out = [
        sds((2, 256, 128), f32),
        sds((2, 256, 128), f32),
        sds((2, 256, LATENT), f32),
    ]
    state = call(
        first_attention_kernel, state_out, [pltpu.VMEM((2, 256, 2 * 256), f32)], True, 4
    )(info, query_rows, keys_own, fetched)
    pieces[1], fetched_late, peak = lax.optimization_barrier((pieces[1], fetched, state[0]))
    state = [peak] + list(state[1:])
    first_other = lax.ppermute(fetched_late, "core", SWAP)
    *pieces, first_other = lax.optimization_barrier((*pieces, first_other))
    three = call(gather_kernel, [sds((3, KEYW, block_len), bf16)], count=3)(*pieces[1:])
    others = lax.ppermute(three, "core", SWAP)
    state = call(
        second_attention_kernel, state_out, [pltpu.VMEM((2, 256, 4 * 256), f32)], True, 9
    )(info, query_rows, pieces[1], pieces[2], pieces[3], first_other, *state)
    send, keep = call(
        last_attention_kernel,
        [sds((half, width_model), bf16), sds((half, width_model), bf16)],
        [pltpu.VMEM((2, 256, 3 * 256), f32), pltpu.VMEM((2, 256, VDIM), bf16)],
        True,
        8,
    )(info, query_rows, others, *state, value_up, out_proj)
    got = lax.ppermute(send, "core", SWAP)
    pair_sum = call(add_kernel, [sds((16, 8, width_model), bf16)], count=2)(keep, got)

    in_out = sds((3, width_out, 2 * ff_half), bf16)
    down_out = sds((3, width_out, ff_half), bf16)
    in_send, in_keep, down_send, down_keep = call(
        split_weights_kernel, [in_out, in_out, down_out, down_out], (), True, 4
    )(info, expert_gate, expert_up, jnp.transpose(expert_down, (0, 2, 1)))
    pair_sum, in_send = lax.optimization_barrier((pair_sum, in_send))
    in_got = lax.ppermute(in_send, "xl", SWAP)

    spread = lax.all_to_all(pair_sum, ("z", "xh"), split_axis=0, concat_axis=0, tiled=True)
    packed = call(norm_kernel, [sds((16, 8, 512), bf16)], count=3)(
        spread, residual, norm_gain[None, :]
    )
    split = lax.all_to_all(packed, CTX, split_axis=0, concat_axis=0, tiled=True)
    split, in_got, down_send = lax.optimization_barrier((split, in_got, down_send))
    down_got = lax.ppermute(down_send, "xl", SWAP)
    split = split.reshape(128, 512)
    w_in = call(join_in_kernel, [sds((3 * 384, 2 * ff_half), bf16)], count=2)(in_keep, in_got)
    w_down = call(join_down_kernel, [sds((3 * ff_half, 384), bf16)], count=2)(down_keep, down_got)

    routes = jnp.transpose(route_ids, (1, 0, 2)).reshape(128, TOPK)
    expert_axis = jnp.arange(EXPERTS, dtype=i32)
    named = jnp.any(routes[:, :, None] == expert_axis[None, None, :], axis=1)
    earlier_tokens = jnp.tril(jnp.ones((128, 128), bf16), -1)
    slot_all = jnp.dot(earlier_tokens, named.astype(bf16), preferred_element_type=f32).astype(i32)
    slot_of = jnp.sum(
        jnp.where(routes[:, :, None] == expert_axis[None, None, :], slot_all[:, None, :], 0), axis=2
    )
    target = (routes // 3) * SLOTS + (routes % 3) * CAP + slot_of
    slot_axis = jnp.arange(32 * SLOTS, dtype=i32)
    picker = jnp.any(target.T[None, :, :] == slot_axis[:, None, None], axis=1).astype(bf16)
    order = jnp.arange(128, dtype=i32)
    back_order = ((order % 16) * 8 + order // 16)[:, None] == order[None, :]
    target_rb = jnp.transpose(target.reshape(16, 8, TOPK), (1, 0, 2)).reshape(128, TOPK)
    gates_rb = route_gates.reshape(128, TOPK)
    weighting = jnp.sum(
        jnp.where(target_rb[:, :, None] == slot_axis[None, None, :], gates_rb[:, :, None], 0.0),
        axis=1,
    )

    travel = sds((32, 80, 128), bf16)
    outgoing = call(pick_kernel, [travel], count=2)(picker, split)
    received = lax.all_to_all(outgoing, EXP, split_axis=0, concat_axis=0, tiled=True)
    received, w_in, w_down = lax.optimization_barrier((received, w_in, w_down))
    pre = call(gate_up_kernel, [sds((32 * SLOTS, 2 * ff_half), bf16)], count=2)(received, w_in)
    pre_parts = lax.all_to_all(
        pre.reshape(8, 128, 2 * ff_half), "y", split_axis=0, concat_axis=0, tiled=True
    )
    hidden = call(hidden_kernel, [sds((8, 128, ff_half), bf16)], count=1)(pre_parts)
    hidden_all = lax.all_to_all(hidden, "y", split_axis=0, concat_axis=0, tiled=True)
    expert_out = call(down_kernel, [travel], count=2)(
        hidden_all.reshape(32 * SLOTS, ff_half), w_down
    )
    returned = lax.all_to_all(expert_out, EXP, split_axis=0, concat_axis=0, tiled=True)
    mix_keep, mix_send = call(
        combine_kernel, [sds((128, width_out), f32), sds((128, width_out), bf16)], count=4
    )(weighting, returned, back_order.astype(bf16), split)
    mix_got = lax.ppermute(mix_send, "xl", SWAP)
    result = (mix_keep + mix_got.astype(f32)).astype(bf16)
    return result.reshape(8, 16, width_out)


def solution(mesh):
    grid = Mesh(mesh.devices.reshape(8, 2, 8, 2, 2), ("y", "xl", "z", "xh", "core"))
    return jax.shard_map(
        on_device,
        mesh=grid,
        in_specs=(
            P(CTX, EXP, None),
            P(CTX, None),
            P(CTX),
            P(EXP, None, None),
            P(EXP, None),
            P(CTX + EXP, None),
            P(),
            P(EXP, None, None),
            P(EXP, None, None),
            P(EXP, CTX, None),
            P(EXP, CTX, None),
            P(EXP, None, CTX),
        ),
        out_specs=P(EXP, None, CTX),
        check_vma=False,
    )
```

```python
import jax
import jax.numpy as jnp
from jax import lax
from jax.experimental import pallas as pl
from jax.experimental.pallas import tpu as pltpu
from jax.sharding import Mesh, PartitionSpec as P

LATENT = 512
VDIM = 128
QKDIM = 192
EXPERTS = 96
TOPK = 6
CAP = 10
SLOTS = 32
SEGMENTS = 8
KEYW = 592
FAR = float(2**20)

CTX = ("y", "xl")
EXP = ("z", "xh", "core")
SWAP = [(0, 1), (1, 0)]
BIG_VMEM = pltpu.CompilerParams(vmem_limit_bytes=20 * 2**20)
f32, bf16, i32 = jnp.float32, jnp.bfloat16, jnp.int32


def keys_kernel(latent, segments, own):
    width, tokens = latent.shape
    own[:width, :] = latent[...]
    mark = lax.broadcasted_iota(i32, (KEYW - width, tokens), 0)
    own[width:, :] = jnp.where(segments[...] == mark, 1.0, 0.0).astype(bf16)


def nt_dot(a, b):
    return lax.dot_general(a, b, (((1,), (1,)), ((), ())), preferred_element_type=f32)


def attend_chunks(rows, chunks, biases, scores, old):
    scale = QKDIM ** (-0.5)
    peak = jnp.full((256, 128), -FAR, f32) if old is None else old[0]
    for n, (chunk, bias) in enumerate(zip(chunks, biases)):
        part = bias(jnp.dot(rows, chunk[...], preferred_element_type=f32) * scale)
        scores[:, n * 256 : (n + 1) * 256] = part
        peak = jnp.maximum(peak, jnp.maximum(part[:, :128], part[:, 128:]))
    peak = jnp.max(peak, axis=1, keepdims=True)
    if old is None:
        sums, mixed = jnp.zeros((256, 128), f32), jnp.zeros((256, LATENT), f32)
    else:
        factor = jnp.exp(old[0][:, :1] - peak)
        sums, mixed = old[1] * factor, old[2] * factor
    for n, chunk in enumerate(chunks):
        terms = jnp.exp(scores[:, n * 256 : (n + 1) * 256] - peak)
        sums = sums + terms[:, :128] + terms[:, 128:]
        mixed = mixed + nt_dot(terms.astype(bf16), chunk[:LATENT, :])
    return jnp.broadcast_to(peak, (256, 128)), sums, mixed


def valid_bias(info, n):
    return lambda part: part + jnp.where(info[n] >= 0, 0.0, -FAR)


def causal_bias(part):
    lane = lax.broadcasted_iota(i32, (256, 256), 1)
    row = lax.broadcasted_iota(i32, (256, 256), 0)
    token = (row % 128) // 8 * 16 + row // 128 * 8 + row % 8
    return jnp.where(lane <= token, part, -FAR)


def first_attention_kernel(info, query, own, p0, peak, sums, mixed, scores):
    for head in range(2):
        state = attend_chunks(
            query[head], [own, p0], [causal_bias, valid_bias(info, 0)], scores.at[head], None
        )
        peak[head], sums[head], mixed[head] = state


def second_attention_kernel(
    info, query, p1, p2, p3, o0, old_peak, old_sums, old_mixed, peak, sums, mixed, scores
):
    for head in range(2):
        old = old_peak[head], old_sums[head], old_mixed[head]
        biases = [valid_bias(info, n) for n in (1, 2, 3, 4)]
        state = attend_chunks(query[head], [p1, p2, p3, o0], biases, scores.at[head], old)
        peak[head], sums[head], mixed[head] = state


def last_attention_kernel(
    info, query, others, old_peak, old_sums, old_mixed, value_up, out_proj, send, keep, scores, values
):
    core = info[8]

    for head in range(2):
        old = old_peak[head], old_sums[head], old_mixed[head]
        chunks = [others.at[n] for n in range(3)]
        biases = [valid_bias(info, n) for n in (5, 6, 7)]
        _, sums, mixed = attend_chunks(query[head], chunks, biases, scores.at[head], old)
        mixed = (mixed / jnp.sum(sums, axis=1, keepdims=True)).astype(bf16)
        values[head] = jnp.dot(mixed, value_up[head], preferred_element_type=f32).astype(bf16)

    def project(which, out):
        start = pl.multiple_of(which * 128, 128)
        both = jnp.concatenate([values[head, pl.ds(start, 128), :] for head in range(2)], axis=1)
        for c in range(0, out.shape[1], 640):
            out[:, c : c + 640] = jnp.dot(
                both, out_proj[:, c : c + 640], preferred_element_type=f32
            ).astype(out.dtype)

    project(1 - core, send)
    project(core, keep)


def add_kernel(keep, got, out):
    out[...] = (keep[...] + got[...].astype(f32)).reshape(out.shape).astype(bf16)


def gather_kernel(p1, p2, p3, out):
    for n, piece in enumerate((p1, p2, p3)):
        out[n] = piece[...]


def norm_kernel(spread, residual, gain, packed):
    attended = jnp.sum(spread[...].astype(f32), axis=0)
    stream = (residual[...].astype(f32) + attended).astype(bf16).astype(f32)
    mean_sq = jnp.mean(stream * stream, axis=1, keepdims=True)
    normed = (stream * lax.rsqrt(mean_sq + 1e-06) * gain[...]).astype(bf16).astype(f32)
    width = stream.shape[1] // 16
    fill = jnp.zeros((stream.shape[0], packed.shape[2] - 3 * width), f32)
    for c in range(16):
        mine, other = c * width, (c ^ 1) * width
        packed[c] = jnp.concatenate(
            [
                normed[:, mine : mine + width],
                normed[:, other : other + width],
                stream[:, mine : mine + width],
                fill,
            ],
            axis=1,
        ).astype(bf16)


def store_packed(out, n, rows):
    left = lax.broadcasted_iota(i32, (SLOTS // 2, 128), 1) < 64
    out[n, 0:32] = rows[:, :128].astype(bf16)
    out[n, 32:64] = rows[:, 128:256].astype(bf16)
    out[n, 64:80] = jnp.where(left, rows[:16, 256:], rows[16:, 256:]).astype(bf16)


def load_packed(ref, n):
    last = ref[n, 64:80]
    left = jnp.where(lax.broadcasted_iota(i32, (1, 128), 1) < 64, 1.0, 0.0).astype(bf16)
    last = jnp.concatenate([last * left, last * (1 - left)], axis=0)
    return jnp.concatenate([ref[n, 0:32], ref[n, 32:64], last], axis=1)


def pick_kernel(picker, split, out):
    values = split[:, :384]
    doubled = jnp.concatenate([values[:, :320], values[:, 256:320]], axis=1)
    for r in range(0, picker.shape[0], 256):
        rows = jnp.dot(picker[r : r + 256, :], doubled, preferred_element_type=f32)
        for n in range(256 // SLOTS):
            store_packed(out, r // SLOTS + n, rows[n * SLOTS : (n + 1) * SLOTS])


def row_mask(count, j):
    slot = lax.broadcasted_iota(i32, (count, 1), 0) % SLOTS
    return jnp.where((slot >= j * CAP) & (slot < (j + 1) * CAP), 1.0, 0.0).astype(bf16)


def spread_experts(rows, masks):
    return jnp.concatenate([rows * mask for mask in masks], axis=1)


def split_weights_kernel(info, gate, up, down, in_send, in_keep, down_send, down_keep):
    half = gate.shape[2] // 2

    def move(into, onto, start):
        into[:, :, :half] = gate[:, :, start : start + half]
        into[:, :, half:] = up[:, :, start : start + half]
        onto[...] = down[:, :, start : start + half]

    @pl.when(info[9] == 0)
    def _():
        move(in_keep, down_keep, 0)
        move(in_send, down_send, half)

    @pl.when(info[9] != 0)
    def _():
        move(in_keep, down_keep, half)
        move(in_send, down_send, 0)


def join_in_kernel(keep, got, out):
    rows = keep.shape[1]
    for j in range(3):
        base = j * 384
        out[base : base + rows, :] = keep[j]
        out[base + rows : base + 2 * rows, :] = got[j]
        out[base + 2 * rows : base + 384, :] = got[j, 256 - rows :]


def join_down_kernel(keep, got, out):
    rows, width = keep.shape[1:]
    for j in range(3):
        lanes = slice(j * width, (j + 1) * width)
        out[:rows, lanes] = keep[j]
        out[rows : 2 * rows, lanes] = got[j]
        out[2 * rows :, lanes] = got[j, 256 - rows :]


def gate_up_kernel(received, weights, pre):
    masks = [row_mask(256, j) for j in range(3)]
    for r in range(0, received.shape[0], 8):
        rows = jnp.concatenate([load_packed(received, r + n) for n in range(8)], axis=0)
        total = jnp.dot(spread_experts(rows, masks), weights[...], preferred_element_type=f32)
        pre[r * SLOTS : (r + 8) * SLOTS, :] = total.astype(bf16)


def hidden_kernel(parts, out):
    total = jnp.sum(parts[...].astype(f32), axis=0)
    half = total.shape[1] // 2
    gate, up = total[:, :half], total[:, half:]
    hidden = (gate / (1.0 + jnp.exp(-gate)) * up).astype(bf16)
    for n in range(out.shape[0]):
        out[n] = hidden


def down_kernel(hidden, weights, out):
    masks = [row_mask(256, j) for j in range(3)]
    for r in range(0, hidden.shape[0], 256):
        rows = spread_experts(hidden[r : r + 256, :], masks)
        total = nt_dot(rows, weights[...])
        for n in range(256 // SLOTS):
            store_packed(out, r // SLOTS + n, total[n * SLOTS : (n + 1) * SLOTS])


def combine_kernel(weighting, returned, order, stream, keep, send):
    width = keep.shape[1]
    rows = jnp.concatenate([load_packed(returned, n) for n in range(returned.shape[0])], axis=0)
    top = weighting[...].astype(bf16)
    rest = (weighting[...] - top.astype(f32)).astype(bf16)
    mixture = jnp.dot(top, rows, preferred_element_type=f32) + jnp.dot(
        rest, rows, preferred_element_type=f32
    )
    tail = mixture[:, 256:320] + mixture[:, 320:384]
    kept = jnp.dot(order[...], stream[:, 2 * width : 3 * width], preferred_element_type=f32)
    keep[...] = kept + mixture[:, :width]
    send[...] = jnp.concatenate([mixture[:, width:256], tail], axis=1).astype(bf16)


def call(kernel, outs, scratch=(), smem_first=False, count=0):
    specs = [pl.BlockSpec(memory_space=pltpu.VMEM)] * count
    if smem_first:
        specs[0] = pl.BlockSpec(memory_space=pltpu.SMEM)
    out_specs = [pl.BlockSpec(memory_space=pltpu.VMEM)] * len(outs)
    single = len(outs) == 1
    return pl.pallas_call(
        kernel,
        in_specs=specs,
        out_specs=out_specs[0] if single else out_specs,
        out_shape=outs[0] if single else outs,
        scratch_shapes=list(scratch),
        compiler_params=BIG_VMEM,
    )


def sds(shape, dtype):
    return jax.ShapeDtypeStruct(shape, dtype)


def on_device(
    queries,
    latent,
    segment_ids,
    value_up,
    out_proj,
    residual,
    norm_gain,
    route_ids,
    route_gates,
    expert_gate,
    expert_up,
    expert_down,
):
    block_len, local_heads, width_key = queries.shape
    width_model = residual.shape[1]
    width_out = width_model // 16
    width_pair = 2 * width_out
    ff = expert_gate.shape[2]
    ff_half = ff // 2
    y, xl, xh, core = (lax.axis_index(a) for a in ("y", "xl", "xh", "core"))
    half = block_len // 2

    segment_axis = jnp.arange(SEGMENTS, dtype=i32)
    own_segment = segment_ids[:, None] == segment_axis[None, :]
    pad = KEYW - width_key - SEGMENTS
    keys_own = call(keys_kernel, [sds((KEYW, block_len), bf16)], count=2)(
        latent.T, segment_ids[None, :]
    )
    pairs = [
        (4 * i + j, 4 * ((i + 1 + j // 2 + 2 * (j % 2)) % 8) + j) for i in range(8) for j in range(4)
    ]
    fetched = lax.ppermute(keys_own, ("y", "xh", "core"), pairs)

    def block_of(x, h, c):
        return 2 * (y - 1 - h - 2 * c) + x

    def block_sent(x, h, c):
        return jnp.where((x == 0) & (h == 1) & (c == 1), 2 * y, block_of(x, h, c))

    def blocks_held(c):
        own = [block_of(xl, xh, c), block_of(xl, 1 - xh, c)]
        return own + [block_sent(1 - xl, xh, c), block_sent(1 - xl, 1 - xh, c)]

    info = jnp.stack(blocks_held(core) + blocks_held(1 - core) + [core, xl]).astype(i32)

    masks = jnp.where(own_segment, 0.0, -FAR).astype(bf16)
    query_rows = jnp.concatenate(
        [
            queries,
            jnp.broadcast_to(masks[:, None, :], (block_len, local_heads, SEGMENTS)),
            jnp.zeros((block_len, local_heads, pad), bf16),
        ],
        axis=2,
    )
    query_rows = query_rows.reshape(16, 2, 8, local_heads, KEYW).transpose(3, 1, 0, 2, 4)
    query_rows = query_rows.reshape(local_heads, block_len, KEYW)
    fetched, query_rows = lax.optimization_barrier((fetched, query_rows))

    to_other = jnp.where((xl == 0) & (xh == 1) & (core == 1), keys_own, fetched)
    diagonal = [(0, 3), (1, 2), (2, 1), (3, 0)]
    pieces = [
        fetched,
        lax.ppermute(fetched, "xh", SWAP),
        lax.ppermute(to_other, "xl", SWAP),
        lax.ppermute(to_other, ("xl", "xh"), diagonal),
    ]

    state_out = [
        sds((2, 256, 128), f32),
        sds((2, 256, 128), f32),
        sds((2, 256, LATENT), f32),
    ]
    state = call(
        first_attention_kernel, state_out, [pltpu.VMEM((2, 256, 2 * 256), f32)], True, 4
    )(info, query_rows, keys_own, fetched)
    pieces[1], fetched_late, peak = lax.optimization_barrier((pieces[1], fetched, state[0]))
    state = [peak] + list(state[1:])
    first_other = lax.ppermute(fetched_late, "core", SWAP)
    *pieces, first_other = lax.optimization_barrier((*pieces, first_other))
    three = call(gather_kernel, [sds((3, KEYW, block_len), bf16)], count=3)(*pieces[1:])
    others = lax.ppermute(three, "core", SWAP)
    state = call(
        second_attention_kernel, state_out, [pltpu.VMEM((2, 256, 4 * 256), f32)], True, 9
    )(info, query_rows, pieces[1], pieces[2], pieces[3], first_other, *state)
    send, keep = call(
        last_attention_kernel,
        [sds((half, width_model), bf16), sds((half, width_model), f32)],
        [pltpu.VMEM((2, 256, 3 * 256), f32), pltpu.VMEM((2, 256, VDIM), bf16)],
        True,
        8,
    )(info, query_rows, others, *state, value_up, out_proj)
    got = lax.ppermute(send, "core", SWAP)
    pair_sum = call(add_kernel, [sds((16, 8, width_model), bf16)], count=2)(keep, got)

    in_out = sds((3, width_out, 2 * ff_half), bf16)
    down_out = sds((3, width_out, ff_half), bf16)
    in_send, in_keep, down_send, down_keep = call(
        split_weights_kernel, [in_out, in_out, down_out, down_out], (), True, 4
    )(info, expert_gate, expert_up, jnp.transpose(expert_down, (0, 2, 1)))
    pair_sum, in_send = lax.optimization_barrier((pair_sum, in_send))
    in_got = lax.ppermute(in_send, "xl", SWAP)

    spread = lax.all_to_all(pair_sum, ("z", "xh"), split_axis=0, concat_axis=0, tiled=True)
    packed = call(norm_kernel, [sds((16, 8, 512), bf16)], count=3)(
        spread, residual, norm_gain[None, :]
    )
    split = lax.all_to_all(packed, CTX, split_axis=0, concat_axis=0, tiled=True)
    split, in_got = lax.optimization_barrier((split, in_got))
    split = split.reshape(128, 512)
    w_in = call(join_in_kernel, [sds((3 * 384, 2 * ff_half), bf16)], count=2)(in_keep, in_got)

    routes = jnp.transpose(route_ids, (1, 0, 2)).reshape(128, TOPK)
    expert_axis = jnp.arange(EXPERTS, dtype=i32)
    named = jnp.any(routes[:, :, None] == expert_axis[None, None, :], axis=1)
    earlier_tokens = jnp.tril(jnp.ones((128, 128), bf16), -1)
    slot_all = jnp.dot(earlier_tokens, named.astype(bf16), preferred_element_type=f32).astype(i32)
    slot_of = jnp.sum(
        jnp.where(routes[:, :, None] == expert_axis[None, None, :], slot_all[:, None, :], 0), axis=2
    )
    target = (routes // 3) * SLOTS + (routes % 3) * CAP + slot_of
    slot_axis = jnp.arange(32 * SLOTS, dtype=i32)
    picker = jnp.any(target.T[None, :, :] == slot_axis[:, None, None], axis=1).astype(bf16)
    order = jnp.arange(128, dtype=i32)
    back_order = ((order % 16) * 8 + order // 16)[:, None] == order[None, :]
    target_rb = jnp.transpose(target.reshape(16, 8, TOPK), (1, 0, 2)).reshape(128, TOPK)
    gates_rb = route_gates.reshape(128, TOPK)
    weighting = jnp.sum(
        jnp.where(target_rb[:, :, None] == slot_axis[None, None, :], gates_rb[:, :, None], 0.0),
        axis=1,
    )

    travel = sds((32, 80, 128), bf16)
    outgoing = call(pick_kernel, [travel], count=2)(picker, split)
    received = lax.all_to_all(outgoing, EXP, split_axis=0, concat_axis=0, tiled=True)
    received, w_in, down_send = lax.optimization_barrier((received, w_in, down_send))
    down_got = lax.ppermute(down_send, "xl", SWAP)
    pre = call(gate_up_kernel, [sds((32 * SLOTS, 2 * ff_half), bf16)], count=2)(received, w_in)
    pre_parts = lax.all_to_all(
        pre.reshape(8, 128, 2 * ff_half), "y", split_axis=0, concat_axis=0, tiled=True
    )
    pre_parts, down_got = lax.optimization_barrier((pre_parts, down_got))
    w_down = call(join_down_kernel, [sds((384, 3 * ff_half), bf16)], count=2)(down_keep, down_got)
    hidden = call(hidden_kernel, [sds((8, 128, ff_half), bf16)], count=1)(pre_parts)
    hidden_all = lax.all_to_all(hidden, "y", split_axis=0, concat_axis=0, tiled=True)
    expert_out = call(down_kernel, [travel], count=2)(
        hidden_all.reshape(32 * SLOTS, ff_half), w_down
    )
    returned = lax.all_to_all(expert_out, EXP, split_axis=0, concat_axis=0, tiled=True)
    mix_keep, mix_send = call(
        combine_kernel, [sds((128, width_out), f32), sds((128, width_out), bf16)], count=4
    )(weighting, returned, back_order.astype(bf16), split)
    mix_got = lax.ppermute(mix_send, "xl", SWAP)
    result = (mix_keep + mix_got.astype(f32)).astype(bf16)
    return result.reshape(8, 16, width_out)


def solution(mesh):
    grid = Mesh(mesh.devices.reshape(8, 2, 8, 2, 2), ("y", "xl", "z", "xh", "core"))
    return jax.shard_map(
        on_device,
        mesh=grid,
        in_specs=(
            P(CTX, EXP, None),
            P(CTX, None),
            P(CTX),
            P(EXP, None, None),
            P(EXP, None),
            P(CTX + EXP, None),
            P(),
            P(EXP, None, None),
            P(EXP, None, None),
            P(EXP, CTX, None),
            P(EXP, CTX, None),
            P(EXP, None, CTX),
        ),
        out_specs=P(EXP, None, CTX),
        check_vma=False,
    )
```
